256 devices in a mesh: gx: 16 (over y, x_hi, core), gy: 16 (over x_lo, z).
Axes of the slice: x: 4 (x_hi: 2, x_lo: 2; x = x_hi * 2 + x_lo), y: 4, z: 8, core: 2. Of those that a mesh axis runs over, the one named last changes fastest.
Arguments:
- noise: float32 [16, 2048, 2048], P(None, 'gx', 'gy'), may hold values from -6 to 6
- biofilm: int32 [16, 2048, 2048], P(None, 'gx', 'gy'), may hold values from 0 to 15
- source: float32 [16, 2048, 2048], P(None, 'gx', 'gy'), may hold values from -8 to 8
Outputs:
- pressure: float32 [16, 2048, 2048], P(None, 'gx', 'gy')
- residual: float32 [16, 2048, 2048], P(None, 'gx', 'gy')
The draws below stay inside these ranges and needn't reach their ends.
All inputs are finite; a program needn't handle non-finite values.
Results may differ from the reference program's by a relative error of at most 0.02.
Values sent between devices are 32-bit elements; how exact they have to be, the bound alone decides.
No kernel may reach another device: no remote copies, remote signals or barrier semaphores. Data moves between devices by JAX's collectives and lax.ppermute only.
A program may use at most 64 MiB of HBM per device.

```python
import jax
import jax.numpy as jnp
from jax import lax

NZ = 16
R = 64
ITERS = 3
NX = 2048
NY = 2048


def touch_ends(drawn, own_key, least, top_value):
    index_at = [jax.random.randint(jax.random.fold_in(own_key, axis), (), 0, length) for axis, length in enumerate(drawn.shape)]
    widest = drawn.shape.index(max(drawn.shape))
    beside = index_at[:widest] + [(index_at[widest] + 1) % drawn.shape[widest]] + index_at[widest + 1:]
    return drawn.at[tuple(index_at)].set(least).at[tuple(beside)].set(top_value)


def level_of(rng, shape, cuts, smallest, top_value):
    loudness = 1.0
    for position, blocks in cuts:
        draws = jax.random.uniform(jax.random.fold_in(jax.random.fold_in(rng, 6), position), (blocks,), jnp.float32, smallest / len(cuts), top_value / len(cuts))
        loudness = loudness * jnp.repeat(jnp.exp(draws), shape[position] // blocks).reshape((-1,) + (1,) * (len(shape) - 1 - position))
    return loudness


def bell_draw(own_key, extent, scale, most, cuts=(), held_as=jnp.bfloat16):
    gain = level_of(own_key, extent, cuts, -0.22, 0.18) if cuts else 1.0
    values = jax.random.normal(own_key, extent, jnp.float32) * scale * gain
    return jnp.minimum(jnp.maximum(values, -most), most).astype(held_as)


def setup_inputs(seed: int = 0) -> dict:
    arg_keys = jax.random.split(jax.random.key(seed), 4)
    return {
        "noise": bell_draw(arg_keys[0], (NZ, NX, NY), 1.0, 6.0, ((1, 16), (2, 16)), jnp.float32),
        "biofilm": touch_ends(jax.random.randint(arg_keys[1], (NZ, NX, NY), 0, 16), jax.random.fold_in(arg_keys[1], 1), 0, 15).astype(jnp.int32),
        "source": bell_draw(arg_keys[2], (NZ, NX, NY), 1.0, 8.0, ((1, 16), (2, 16)), jnp.float32),
    }


def smooth_axis(field, axis):
    width = 2 * R + 1

    def add_tap(tap, total):
        return total + jnp.roll(field, tap - R, axis=axis)

    total = lax.fori_loop(0, width, add_tap, jnp.zeros_like(field))
    return total * (1.0 / float(width) ** 0.5)


def kozeny(biofilm):
    fraction = 0.06 * biofilm.astype(jnp.float32)
    porosity = 0.35 * (1.0 - fraction)
    ratio = (1.0 - 0.35) / (1.0 - porosity)
    return (1.0 - fraction) ** 3 * ratio * ratio


def harmonic(left, right):
    return 2.0 * left * right / (left + right)


def operate(field, trans_x, trans_y, trans_z):
    flux_x = trans_x * (jnp.roll(field, -1, axis=1) - field)
    flux_y = trans_y * (jnp.roll(field, -1, axis=2) - field)
    flux_z = trans_z * (field[1:] - field[:-1])
    zeros = jnp.zeros_like(field[:1])
    result = 0.5 * field + jnp.roll(flux_x, 1, axis=1) - flux_x
    result = result + jnp.roll(flux_y, 1, axis=2) - flux_y
    result = result + jnp.concatenate([zeros, flux_z], 0) - jnp.concatenate([flux_z, zeros], 0)
    return result


def reference(noise, biofilm, source):
    logperm = smooth_axis(smooth_axis(noise, 1), 2)
    perm = jnp.exp(logperm) * kozeny(biofilm)
    trans_x = harmonic(perm, jnp.roll(perm, -1, axis=1))
    trans_y = harmonic(perm, jnp.roll(perm, -1, axis=2))
    trans_z = harmonic(perm[:-1], perm[1:])
    pressure = jnp.zeros_like(source)
    residual, direction = source, source
    norm_now = jnp.sum(residual * residual)
    for step in range(ITERS):
        image = operate(direction, trans_x, trans_y, trans_z)
        alpha = norm_now / jnp.sum(direction * image)
        pressure = pressure + alpha * direction
        residual = residual - alpha * image
        norm_next = jnp.sum(residual * residual)
        direction = residual + (norm_next / norm_now) * direction
        norm_now = norm_next
    return pressure, residual
```

```python
import jax
import jax.numpy as jnp
from jax import lax
from jax.experimental import pallas as pl
from jax.experimental.pallas import tpu as pltpu
from jax.sharding import PartitionSpec as P

R = 64
WIDTH = 2 * R + 1
NZ = 16
N = 128
F32 = jnp.float32
BF16 = jnp.bfloat16

MSG_Y = 8 * N + N + 16
MSG_X = 17 * 72 + 24
ROWS = 160
OWN = 16
HUGE = 1e30


def iota(shape, dim):
    return lax.broadcasted_iota(jnp.int32, shape, dim)


def roll(x, shift, axis):
    if isinstance(shift, int):
        shift = shift % x.shape[axis]
        if shift == 0:
            return x
    return pltpu.roll(x, shift, axis)


def split3(x):
    high = x.astype(BF16)
    rest = x - high.astype(F32)
    middle = rest.astype(BF16)
    low = (rest - middle.astype(F32)).astype(BF16)
    return high, middle, low


def dot(a, b):
    return lax.dot_general(a, b, (((1,), (0,)), ((), ())), preferred_element_type=F32)


def weights(mask):
    return jnp.where(mask, 1.0, 0.0).astype(BF16)


def pack_columns(noise, source, biofilm, to_right, to_left):
    lane = iota((16, N), 1)
    slot = lane % 8
    group = lane // 8
    low = lane < 64

    third_right = jnp.zeros((16, N), F32)
    third_left = jnp.zeros((16, N), F32)
    for g in range(8):
        rows = slice(16 * g, 16 * g + 16)
        zero = jnp.zeros((16, N), F32)
        nr, sr, nl, sl = zero, zero, zero, zero
        br = jnp.zeros((16, N), jnp.int32)
        bl = br
        for q in range(8):
            even = noise[2 * q, rows, :]
            odd = noise[2 * q + 1, rows, :]
            to_right[q * N + 16 * g : q * N + 16 * g + 16, :] = jnp.where(low, roll(even, 64, 1), odd)
            to_left[q * N + 16 * g : q * N + 16 * g + 16, :] = jnp.where(low, even, roll(odd, 64, 1))
            for z, n in ((2 * q, even), (2 * q + 1, odd)):
                here = group == z
                s = source[z, rows, :]
                b = biofilm[z, rows, :]
                nr = jnp.where(here, roll(n, 8 * z - 61, 1), nr)
                nl = jnp.where(here, roll(n, 8 * z + 5 - 64, 1), nl)
                sr = jnp.where(here, roll(s, 8 * z + 8, 1), sr)
                sl = jnp.where(here, roll(s, 8 * z, 1), sl)
                br = jnp.where(here, roll(b, 8 * z + 8, 1), br)
                bl = jnp.where(here, roll(b, 8 * z, 1), bl)
        br = br.astype(F32)
        bl = bl.astype(F32)
        to_right[8 * N + 16 * g : 8 * N + 16 * g + 16, :] = jnp.where(
            slot < 3, nr, jnp.where(slot < 5, roll(br, -3, 1), sr)
        )
        to_left[8 * N + 16 * g : 8 * N + 16 * g + 16, :] = jnp.where(
            slot < 3, sl, jnp.where(slot < 5, roll(bl, 3, 1), nl)
        )
        third_right = third_right + roll(jnp.where(slot == 5, br, 0.0), g, 1)
        third_left = third_left + roll(jnp.where(slot == 2, bl, 0.0), g, 1)
    to_right[9 * N :, :] = third_right
    to_left[9 * N :, :] = third_left


def column_weights():
    m = iota((N, 2 * N), 0)
    o = iota((N, 2 * N), 1)
    s = o - N
    own = ((o < N) & (m - o <= R) & (o - m <= R)) | ((o >= N) & (s <= 2) & (m >= s + 64)) | (
        (s >= 5) & (s <= 7) & (m <= s + 56)
    )
    lane = iota((N, 3 * N), 0)
    o = iota((N, 3 * N), 1)
    half = lane // 64
    m = lane % 64
    e = o - 2 * N
    same = (o < 2 * N) & (o // N == half)
    edge = (e >= 0) & (e < 16) & (e // 8 == half)
    left = (same & (m >= o % N)) | (edge & (o % 8 >= 5))
    right = (same & (m + 64 <= o % N)) | (edge & (o % 8 <= 2))
    a = iota((N, N), 0)
    b = iota((N, N), 1)
    together = a // 8 == b // 8
    t = a % 8
    s = b % 8
    left_extra = together & (t <= 2) & (s >= 5) & (t >= s - 5)
    right_extra = together & (t >= 5) & (s <= 2) & (t - 5 <= s)
    return [weights(w) for w in (own, left, right, left_extra, right_extra)]


def smooth_columns(
    noise, source, biofilm, from_left, from_right, middle, edge, edge_source, edge_biofilm, to_down, to_up
):
    own, left, right, left_extra, right_extra = column_weights()
    slot = iota((N, N), 1) % 8

    def times(x, w):
        high, mid, low = split3(x)
        return dot(high, w) + dot(mid, w) + dot(low, w)

    extra_left = from_left[8 * N : 9 * N, :]
    extra_right = from_right[8 * N : 9 * N, :]
    total = times(extra_left, left_extra) + times(extra_right, right_extra)
    for q in range(8):
        halo = times(from_left[q * N : q * N + N, :], left) + times(from_right[q * N : q * N + N, :], right)
        total = total + roll(halo[:, 2 * N :], 16 * q, 1)
        for z in (2 * q, 2 * q + 1):
            out = times(noise[z], own)
            total = total + roll(out[:, N:], 8 * z, 1)
            field = out[:, :N] + halo[:, (z % 2) * N : (z % 2) * N + N]
            middle[z] = field
            to_down[z * 72 : z * 72 + 72, :] = field[56:, :]
            to_up[z * 72 : z * 72 + 72, :] = field[:72, :]
    edge[...] = total
    to_down[16 * 72 : 17 * 72, :] = total[56:, :]
    to_up[16 * 72 : 17 * 72, :] = total[:72, :]

    edge_source[...] = jnp.where(slot >= 5, extra_left, jnp.where(slot <= 2, extra_right, 0.0))
    third_left = from_left[9 * N :, :]
    third_right = from_right[9 * N :, :]
    levels = jnp.where(slot >= 6, roll(extra_left, 3, 1), jnp.where(slot <= 1, roll(extra_right, -3, 1), 0.0))
    slot16 = iota((16, N), 1) % 8
    for g in range(8):
        rows = slice(16 * g, 16 * g + 16)
        edge_biofilm[rows, :] = jnp.where(
            slot16 == 5, roll(third_left, -g, 1), jnp.where(slot16 == 2, roll(third_right, -g, 1), levels[rows, :])
        )

    to_down[17 * 72 :, :] = jnp.zeros((24, N), F32)
    to_up[17 * 72 :, :] = jnp.zeros((24, N), F32)
    for z in range(17):
        s = source.at[z] if z < 16 else edge_source
        b = biofilm.at[z] if z < 16 else edge_biofilm
        to_down[z * 72 : z * 72 + 3, :] = s[125:128, :]
        to_down[z * 72 + 3 : z * 72 + 5, :] = b[126:128, :].astype(F32)
        to_down[17 * 72 + z : 17 * 72 + z + 1, :] = b[125:126, :].astype(F32)
        to_up[z * 72 + 67 : z * 72 + 70, :] = s[0:3, :]
        to_up[z * 72 + 70 : z * 72 + 72, :] = b[0:2, :].astype(F32)
        to_up[17 * 72 + z : 17 * 72 + z + 1, :] = b[2:3, :].astype(F32)


def row_weights():
    r = iota((144, N), 0) - 8
    m = iota((144, N), 1)
    inside = (r >= -3) & (r <= 130)
    own = inside & (m >= r - R) & (m <= r + R)
    r = iota((144, 72), 0) - 8
    m = iota((144, 72), 1)
    inside = (r >= -3) & (r <= 130)
    up = inside & (m >= 5) & (m >= r + 8)
    down = inside & (m <= 66) & (m <= r - R)
    return [weights(w) for w in (own, up, down)]


def resistance(logperm, biofilm, top):
    open_part = 1.0 - 0.06 * biofilm
    solid = (1.0 - 0.35 * open_part) * (1.0 / (1.0 - 0.35))
    value = jnp.exp(top - logperm) * (0.5 * solid * solid) / (open_part * open_part * open_part)
    return jnp.minimum(value, HUGE)


def chunks():
    return [(8, 48), (56, 48), (104, 48)]


def operate_powers(
    middle, edge, edge_source, edge_biofilm, source, biofilm, from_up, from_down,
    power1, power2, power3, table,
    resist, across_x, across_y, across_z, edge_right, field0, field1, field2, field3,
):
    lane = iota((8, N), 1)
    row8 = iota((8, N), 0)

    own, up, down = row_weights()
    edge_lane = (iota((144, N), 1) % 8 <= 2) | (iota((144, N), 1) % 8 >= 5)
    row144 = iota((144, N), 0)
    real_row = (row144 >= 5) & (row144 <= 138)

    def plane_logperm(data, z, real):
        total = jnp.zeros((144, N), F32)
        first = pl.multiple_of(z * 72, 8)
        for w, part in ((own, data), (up, from_up[pl.ds(first, 72), :]), (down, from_down[pl.ds(first, 72), :])):
            for piece in split3(part):
                total = total + dot(w, piece)
        total = total * (1.0 / WIDTH)
        resist[z, 8:152, :] = total
        return jnp.max(jnp.where(real, total, -HUGE).reshape(18, 8, N), axis=0)

    def smooth(z, largest):
        return jnp.maximum(largest, plane_logperm(middle[z], z, real_row))

    largest = plane_logperm(edge[...], 16, real_row & edge_lane)
    largest = lax.fori_loop(0, 16, smooth, largest)
    top = jnp.max(jnp.max(largest, axis=0, keepdims=True), axis=1, keepdims=True)
    top = jnp.maximum(top, -60.0)

    def halo_tiles(z):
        first = pl.multiple_of(z * 72, 8)
        above = from_up[pl.ds(first, 8), :]
        below = from_down[pl.ds(first + 64, 8), :]
        third_above = from_up[pl.ds(17 * 72 + z, 1), :]
        third_below = from_down[pl.ds(17 * 72 + z, 1), :]
        source_above = jnp.where(row8 >= 5, roll(above, 5, 0), 0.0)
        source_below = jnp.where(row8 <= 2, roll(below, 5, 0), 0.0)
        biofilm_above = jnp.where(row8 == 5, third_above, jnp.where(row8 >= 6, roll(above, 3, 0), 0.0))
        biofilm_below = jnp.where(row8 == 2, third_below, jnp.where(row8 <= 1, roll(below, 2, 0), 0.0))
        return source_above, source_below, biofilm_above, biofilm_below

    def prepare(z, own_source, own_biofilm, real8, real):
        source_above, source_below, biofilm_above, biofilm_below = halo_tiles(z)
        field0[z, 8:16, :] = source_above
        field0[z, 16:144, :] = own_source
        field0[z, 144:152, :] = source_below
        resist[z, 8:16, :] = jnp.where(
            real8 & (row8 >= 5), resistance(resist[z, 8:16, :], biofilm_above, top), HUGE
        )
        resist[z, 144:152, :] = jnp.where(
            real8 & (row8 <= 2), resistance(resist[z, 144:152, :], biofilm_below, top), HUGE
        )
        value = resistance(resist[z, 16:144, :], own_biofilm, top)
        resist[z, 16:144, :] = value if real is None else jnp.where(real, value, HUGE)
        empty = jnp.full((8, N), HUGE, F32)
        resist[z, 0:8, :] = empty
        resist[z, 152:160, :] = empty
        none = jnp.zeros((8, N), F32)
        for f in (field0, field1, field2):
            f[z, 0:8, :] = none
            f[z, 152:160, :] = none

    def prepare_layer(z, carry):
        prepare(z, source[z], biofilm[z].astype(F32), row8 >= 0, None)
        return carry

    slot128 = iota((N, N), 1) % 8
    slot8 = lane % 8
    prepare(
        16, edge_source[...], edge_biofilm[...],
        (slot8 <= 2) | (slot8 >= 5), (slot128 <= 2) | (slot128 >= 5),
    )
    lax.fori_loop(0, 16, prepare_layer, 0)

    lane48 = iota((48, N), 1)
    slot48 = lane48 % 8

    def block_ends(field, start, size):
        ends = jnp.zeros((size, N), F32)
        for z in range(16):
            ends = jnp.where(lane48 >= 8 * z, roll(field[z, start : start + size, :], 8 * z + 1, 1), ends)
        return ends

    def edge_neighbours(field, start, size):
        ends = block_ends(field, start, size)
        here = field[16, start : start + size, :]
        left = jnp.where(slot48 == 0, ends, roll(here, 1, 1))
        right = jnp.where(slot48 == 7, roll(ends, 6, 1), roll(here, -1, 1))
        return here, left, right

    for start, size in chunks():
        here, left, right = edge_neighbours(resist, start, size)
        before = resist[16, start - 1 : start - 1 + size, :]
        across_x[16, start : start + size, :] = 1.0 / (here + before)
        across_y[16, start : start + size, :] = 1.0 / (here + left)
        edge_right[start : start + size, :] = 1.0 / (here + right)
        across_z[16, start : start + size, :] = jnp.where(
            lane48 < 120, 1.0 / (here + roll(here, -8, 1)), 0.0
        )
    across_x[16, 152:160, :] = jnp.zeros((8, N), F32)

    def faces(z, carry):
        across_x[z, 152:160, :] = jnp.zeros((8, N), F32)
        for start, size in chunks():
            rows = slice(start, start + size)
            here = resist[z, rows, :]
            before = resist[z, start - 1 : start - 1 + size, :]
            outer = resist[16, rows, :]
            left = jnp.where(lane48 == 0, roll(outer, 121 - 8 * z, 1), roll(here, 1, 1))
            across_x[z, rows, :] = 1.0 / (here + before)
            across_y[z, rows, :] = 1.0 / (here + left)
            above = resist[jnp.maximum(z - 1, 0), rows, :]
            across_z[z, rows, :] = jnp.where(z > 0, 1.0 / (here + above), 0.0)
        return carry

    lax.fori_loop(0, 16, faces, 0)

    def apply(field, image, flux):
        for start, size in chunks():
            rows = slice(start, start + size)
            here, left, right = edge_neighbours(field, start, size)
            inward = across_y[16, rows, :] * (here - left)
            flux[rows, :] = inward
            value = inward - edge_right[rows, :] * (right - here)
            value = value + across_x[16, rows, :] * (here - field[16, start - 1 : start - 1 + size, :])
            value = value - across_x[16, start + 1 : start + 1 + size, :] * (
                field[16, start + 1 : start + 1 + size, :] - here
            )
            through = across_z[16, rows, :] * (roll(here, -8, 1) - here)
            image[16, rows, :] = value - through + roll(through, 8, 1)

        def layer(z, carry):
            for start, size in chunks():
                rows = slice(start, start + size)
                here = field[z, rows, :]
                left = jnp.where(lane48 == 0, roll(field[16, rows, :], 121 - 8 * z, 1), roll(here, 1, 1))
                inward = across_y[z, rows, :] * (here - left)
                outward = jnp.where(lane48 == 127, roll(flux[rows, :], 127 - 8 * z, 1), roll(inward, -1, 1))
                value = inward - outward
                value = value + across_x[z, rows, :] * (here - field[z, start - 1 : start - 1 + size, :])
                value = value - across_x[z, start + 1 : start + 1 + size, :] * (
                    field[z, start + 1 : start + 1 + size, :] - here
                )
                value = value + across_z[z, rows, :] * (here - field[jnp.maximum(z - 1, 0), rows, :])
                below = jnp.where(z < 15, across_z[jnp.minimum(z + 1, 15), rows, :], 0.0)
                value = value - below * (field[jnp.minimum(z + 1, 15), rows, :] - here)
                image[z, rows, :] = value
            return carry

        lax.fori_loop(0, 16, layer, 0)

    flux = edge_flux = field3.at[16]
    apply(field0, field1, edge_flux)
    apply(field1, field2, edge_flux)

    def last(z, carry):
        return carry

    apply(field2, field3, resist.at[16])

    def gather(z, sums):
        f0 = field0[z, 16:144, :]
        f1 = field1[z, 16:144, :]
        f2 = field2[z, 16:144, :]
        f3 = field3[z, 16:144, :]
        power1[z] = f1
        power2[z] = f2
        power3[z] = f3
        terms = (f0 * f0, f0 * f1, f1 * f1, f1 * f2, f2 * f2, f2 * f3)
        return tuple(s + jnp.sum(t.reshape(16, 8, N), axis=0) for s, t in zip(sums, terms))

    sums = lax.fori_loop(0, 16, gather, tuple(jnp.zeros((8, N), F32) for _ in range(6)))
    line = jnp.where((lane[:1] >= 8) & (lane[:1] < 16), top, 0.0)
    for k, s in enumerate(sums):
        amount = jnp.sum(jnp.sum(s, axis=0, keepdims=True), axis=1, keepdims=True)
        line = jnp.where(lane[:1] == k, amount, line)
    table[...] = jnp.broadcast_to(line, table.shape)


def combine(everyone, own, source, power1, power2, power3, pressure, residual):
    n = everyone.shape[0]
    rows = everyone[...]
    lane = iota((n, N), 1)
    tops = jnp.where(lane < 8, roll(rows, -8, 1), 0.0)
    top = jnp.max(tops, axis=0, keepdims=True)
    top = jnp.max(jnp.where(lane[:1] == 0, top, -HUGE), axis=1, keepdims=True)
    factor = jnp.exp((tops - top) * lane.astype(F32))
    moments = jnp.sum(jnp.where(lane < 6, rows * factor, 0.0), axis=0, keepdims=True)
    u0, u1, u2, u3, u4, u5 = [
        jnp.sum(jnp.where(lane[:1] == k, moments, 0.0), axis=1, keepdims=True) for k in range(6)
    ]
    own_top = jnp.sum(jnp.where(lane[:1] == 8, own[0:1, :], 0.0), axis=1, keepdims=True)
    ratio = jnp.exp(own_top - top)

    def over(a, b):
        return jnp.where(b > 0.0, a / jnp.where(b > 0.0, b, 1.0), 0.0)

    l10 = over(u1, u0)
    l20 = over(u2, u0)
    d1 = u2 - l10 * u1
    s12 = u3 - l10 * u2
    l21 = over(s12, d1)
    d2 = (u4 - l20 * u2) - l21 * s12
    y1 = u4 - l10 * u3
    y2 = u5 - l20 * u3 - l21 * y1
    e2 = -over(y2, d2)
    e1 = -over(y1, d1) - l21 * e2
    e0 = -over(u3, u0) - l10 * e1 - l20 * e2

    sigma = jnp.exp(top)
    tau = jnp.minimum(1.0, 2.0 * sigma)
    kappa = jnp.minimum(1.0, 0.5 / sigma)
    at_zero = ((e0 * tau - e1 * kappa) * tau + e2 * kappa * kappa) * tau - kappa * kappa * kappa
    r_scale = tau * tau * tau / at_zero
    p_scale = -jnp.minimum(1.0 / sigma, 2.0) / at_zero
    q1 = tau * e2 - kappa
    r0 = r_scale * e0
    r1 = r_scale * e1 * ratio
    r2 = r_scale * e2 * ratio * ratio
    r3 = r_scale * ratio * ratio * ratio
    p0 = p_scale * (tau * tau * e1 - kappa * q1)
    p1 = p_scale * (tau * q1) * ratio
    p2 = p_scale * (tau * tau) * ratio * ratio
    for z in range(source.shape[0]):
        f0 = source[z]
        f1 = power1[z]
        f2 = power2[z]
        pressure[z] = p0 * f0 + p1 * f1 + p2 * f2
        residual[z] = (r0 * f0 + r1 * f1) + (r2 * f2 + r3 * power3[z])


def vmem(count):
    return [pl.BlockSpec(memory_space=pltpu.VMEM)] * count


def shape(*dims):
    return jax.ShapeDtypeStruct(dims, F32)


def call(body, out, scratch=(), inputs=0, name=None):
    return pl.pallas_call(
        body,
        out_shape=out,
        in_specs=vmem(inputs),
        out_specs=vmem(len(out)),
        scratch_shapes=list(scratch),
        compiler_params=pltpu.CompilerParams(vmem_limit_bytes=40 * 1024 * 1024),
        name=name,
    )


def exchange(to_next, to_previous, axis):
    count = lax.axis_size(axis)
    forward = [(i, (i + 1) % count) for i in range(count)]
    backward = [(target, source) for source, target in forward]
    return lax.ppermute(to_next, axis, forward), lax.ppermute(to_previous, axis, backward)


def local(noise, biofilm, source):
    to_right, to_left = call(pack_columns, [shape(MSG_Y, N)] * 2, inputs=3, name="pack")(noise, source, biofilm)
    from_left, from_right = exchange(to_right, to_left, "gy")
    middle, edge, edge_source, edge_biofilm, to_down, to_up = call(
        smooth_columns,
        [shape(NZ, N, N), shape(N, N), shape(N, N), shape(N, N), shape(MSG_X, N), shape(MSG_X, N)],
        inputs=5,
        name="columns",
    )(noise, source, biofilm, from_left, from_right)
    from_up, from_down = exchange(to_down, to_up, "gx")
    devices = lax.axis_size("gx") * lax.axis_size("gy")
    planes = [pltpu.VMEM((17, ROWS, N), F32)]
    power1, power2, power3, table = call(
        operate_powers,
        [shape(NZ, N, N)] * 3 + [shape(devices, N)],
        scratch=planes * 4 + [pltpu.VMEM((ROWS, N), F32)] + planes * 4,
        inputs=8,
        name="powers",
    )(middle, edge, edge_source, edge_biofilm, source, biofilm, from_up, from_down)
    everyone = lax.all_to_all(table, ("gx", "gy"), 0, 0, tiled=True)

    layers = 4
    block = pl.BlockSpec((layers, N, N), lambda i: (i, 0, 0))
    whole = pl.BlockSpec((devices, N), lambda i: (0, 0))
    first = pl.BlockSpec((8, N), lambda i: (0, 0))
    return tuple(
        pl.pallas_call(
            combine,
            grid=(NZ // layers,),
            out_shape=[shape(NZ, N, N)] * 2,
            in_specs=[whole, first] + [block] * 4,
            out_specs=[block] * 2,
            name="combine",
        )(everyone, table, source, power1, power2, power3)
    )


def solution(mesh):
    in_specs = (P(None, "gx", "gy"), P(None, "gx", "gy"), P(None, "gx", "gy"))
    out_specs = (P(None, "gx", "gy"), P(None, "gx", "gy"))
    return jax.shard_map(local, mesh=mesh, in_specs=in_specs, out_specs=out_specs, check_vma=False)
```

```python
import jax
import jax.numpy as jnp
from jax import lax
from jax.experimental import pallas as pl
from jax.experimental.pallas import tpu as pltpu
from jax.sharding import PartitionSpec as P

R = 64
WIDTH = 2 * R + 1
NZ = 16
N = 128
F32 = jnp.float32
BF16 = jnp.bfloat16

MSG_Y = 8 * N + N + 16
MSG_X = 17 * 72 + 24
ROWS = 160
OWN = 16
HUGE = 1e30
U1, U2, U3, U4, U5, U6 = 16, 4, 2, 4, 4, 2


def iota(shape, dim):
    return lax.broadcasted_iota(jnp.int32, shape, dim)


def roll(x, shift, axis):
    if isinstance(shift, int):
        shift = shift % x.shape[axis]
        if shift == 0:
            return x
    return pltpu.roll(x, shift, axis)


def split3(x):
    high = x.astype(BF16)
    rest = x - high.astype(F32)
    middle = rest.astype(BF16)
    low = (rest - middle.astype(F32)).astype(BF16)
    return high, middle, low


def split2(x):
    high = x.astype(BF16)
    return high, (x - high.astype(F32)).astype(BF16)


def dot(a, b):
    return lax.dot_general(a, b, (((1,), (0,)), ((), ())), preferred_element_type=F32)


def weights(mask):
    return jnp.where(mask, 1.0, 0.0).astype(BF16)


def pack_columns(noise_in, source_in, biofilm_in, to_right, to_left, noise, source, biofilm, arrived):
    def arrivals(g):
        rows = slice(16 * g, 16 * g + 16)
        return [
            pltpu.make_async_copy(far.at[:, rows, :], near.at[:, rows, :], arrived.at[k, g])
            for k, (far, near) in enumerate(((noise_in, noise), (source_in, source), (biofilm_in, biofilm)))
        ]

    for g in range(8):
        for copy in arrivals(g):
            copy.start()

    lane = iota((16, N), 1)
    slot = lane % 8
    group = lane // 8
    low = lane < 64

    third_right = jnp.zeros((16, N), F32)
    third_left = jnp.zeros((16, N), F32)
    for g in range(8):
        for copy in arrivals(g):
            copy.wait()
        rows = slice(16 * g, 16 * g + 16)
        zero = jnp.zeros((16, N), F32)
        nr, sr, nl, sl = zero, zero, zero, zero
        br = jnp.zeros((16, N), jnp.int32)
        bl = br
        for q in range(8):
            even = noise[2 * q, rows, :]
            odd = noise[2 * q + 1, rows, :]
            to_right[q * N + 16 * g : q * N + 16 * g + 16, :] = jnp.where(low, roll(even, 64, 1), odd)
            to_left[q * N + 16 * g : q * N + 16 * g + 16, :] = jnp.where(low, even, roll(odd, 64, 1))
            for z, n in ((2 * q, even), (2 * q + 1, odd)):
                here = group == z
                s = source[z, rows, :]
                b = biofilm[z, rows, :]
                nr = jnp.where(here, roll(n, 8 * z - 61, 1), nr)
                nl = jnp.where(here, roll(n, 8 * z + 5 - 64, 1), nl)
                sr = jnp.where(here, roll(s, 8 * z + 8, 1), sr)
                sl = jnp.where(here, roll(s, 8 * z, 1), sl)
                br = jnp.where(here, roll(b, 8 * z + 8, 1), br)
                bl = jnp.where(here, roll(b, 8 * z, 1), bl)
        br = br.astype(F32)
        bl = bl.astype(F32)
        to_right[8 * N + 16 * g : 8 * N + 16 * g + 16, :] = jnp.where(
            slot < 3, nr, jnp.where(slot < 5, roll(br, -3, 1), sr)
        )
        to_left[8 * N + 16 * g : 8 * N + 16 * g + 16, :] = jnp.where(
            slot < 3, sl, jnp.where(slot < 5, roll(bl, 3, 1), nl)
        )
        third_right = third_right + roll(jnp.where(slot == 5, br, 0.0), g, 1)
        third_left = third_left + roll(jnp.where(slot == 2, bl, 0.0), g, 1)
    to_right[9 * N :, :] = third_right
    to_left[9 * N :, :] = third_left


def column_weights():
    m = iota((N, 2 * N), 0)
    o = iota((N, 2 * N), 1)
    s = o - N
    own = ((o < N) & (m - o <= R) & (o - m <= R)) | ((o >= N) & (s <= 2) & (m >= s + 64)) | (
        (s >= 5) & (s <= 7) & (m <= s + 56)
    )
    lane = iota((N, 3 * N), 0)
    o = iota((N, 3 * N), 1)
    half = lane // 64
    m = lane % 64
    e = o - 2 * N
    same = (o < 2 * N) & (o // N == half)
    edge = (e >= 0) & (e < 16) & (e // 8 == half)
    left = (same & (m >= o % N)) | (edge & (o % 8 >= 5))
    right = (same & (m + 64 <= o % N)) | (edge & (o % 8 <= 2))
    a = iota((N, N), 0)
    b = iota((N, N), 1)
    together = a // 8 == b // 8
    t = a % 8
    s = b % 8
    left_extra = together & (t <= 2) & (s >= 5) & (t >= s - 5)
    right_extra = together & (t >= 5) & (s <= 2) & (t - 5 <= s)
    return [weights(w) for w in (own, left, right, left_extra, right_extra)]


def column_sums_own(noise, biofilm, own_middle, own_edge, factor):
    own = column_weights()[0]
    twice = jnp.concatenate([own, own], axis=0)
    total = jnp.zeros((N, N), F32)
    for z in range(16):
        out = dot(jnp.concatenate(split2(noise[z]), axis=1), twice)
        own_middle[z] = out[:, :N]
        total = total + roll(out[:, N:], 8 * z, 1)
        factor[z] = resistance_factor(biofilm[z].astype(F32))
    own_edge[...] = total


def smooth_columns(
    own_middle, own_edge, source, biofilm, from_left, from_right,
    middle, edge, edge_source, edge_biofilm, to_down, to_up,
):
    _, left, right, left_extra, right_extra = column_weights()
    both = jnp.concatenate([left, right], axis=0)
    both_extra = jnp.concatenate([left_extra, right_extra], axis=0)
    slot = iota((N, N), 1) % 8

    def times(x, y, w):
        high, low = split2(jnp.concatenate([x, y], axis=1))
        return dot(high, w) + dot(low, w)

    extra_left = from_left[8 * N : 9 * N, :]
    extra_right = from_right[8 * N : 9 * N, :]
    total = own_edge[...] + times(extra_left, extra_right, both_extra)
    for q in range(8):
        halo = times(from_left[q * N : q * N + N, :], from_right[q * N : q * N + N, :], both)
        total = total + roll(halo[:, 2 * N :], 16 * q, 1)
        for z in (2 * q, 2 * q + 1):
            field = own_middle[z] + halo[:, (z % 2) * N : (z % 2) * N + N]
            middle[z] = field
            to_down[z * 72 : z * 72 + 72, :] = field[56:, :]
            to_up[z * 72 : z * 72 + 72, :] = field[:72, :]
    edge[...] = total
    to_down[16 * 72 : 17 * 72, :] = total[56:, :]
    to_up[16 * 72 : 17 * 72, :] = total[:72, :]

    edge_source[...] = jnp.where(slot >= 5, extra_left, jnp.where(slot <= 2, extra_right, 0.0))
    third_left = from_left[9 * N :, :]
    third_right = from_right[9 * N :, :]
    levels = jnp.where(slot >= 6, roll(extra_left, 3, 1), jnp.where(slot <= 1, roll(extra_right, -3, 1), 0.0))
    slot16 = iota((16, N), 1) % 8
    for g in range(8):
        rows = slice(16 * g, 16 * g + 16)
        edge_biofilm[rows, :] = jnp.where(
            slot16 == 5, roll(third_left, -g, 1), jnp.where(slot16 == 2, roll(third_right, -g, 1), levels[rows, :])
        )

    to_down[17 * 72 :, :] = jnp.zeros((24, N), F32)
    to_up[17 * 72 :, :] = jnp.zeros((24, N), F32)
    for z in range(17):
        s = source.at[z] if z < 16 else edge_source
        b = biofilm.at[z] if z < 16 else edge_biofilm
        to_down[z * 72 : z * 72 + 3, :] = s[125:128, :]
        to_down[z * 72 + 3 : z * 72 + 5, :] = b[126:128, :].astype(F32)
        to_down[17 * 72 + z : 17 * 72 + z + 1, :] = b[125:126, :].astype(F32)
        to_up[z * 72 + 67 : z * 72 + 70, :] = s[0:3, :]
        to_up[z * 72 + 70 : z * 72 + 72, :] = b[0:2, :].astype(F32)
        to_up[17 * 72 + z : 17 * 72 + z + 1, :] = b[2:3, :].astype(F32)


def row_weights():
    r = iota((144, N), 0) - 8
    m = iota((144, N), 1)
    inside = (r >= -3) & (r <= 130)
    own = inside & (m >= r - R) & (m <= r + R)
    halo = inside & (((m < 64) & (m >= r)) | ((m >= 64) & (m <= r)))
    return weights(own), weights(halo)


def row_sums(band, *planes):
    columns = [jnp.concatenate(split2(p), axis=0) for p in planes]
    out = dot(jnp.concatenate([band, band], axis=1), jnp.concatenate(columns, axis=1))
    return [out[:, k * N : k * N + N] for k in range(len(planes))]


def row_sums_own(middle, edge, edge_biofilm, partial, factor):
    own, _ = row_weights()
    for z in range(0, 16, 2):
        partial[z], partial[z + 1] = row_sums(own, middle[z], middle[z + 1])
    partial[16] = row_sums(own, edge[...])[0]
    factor[...] = resistance_factor(edge_biofilm[...])


def resistance_factor(biofilm):
    open_part = 1.0 - 0.06 * biofilm
    solid = (1.0 - 0.35 * open_part) * (1.0 / (1.0 - 0.35))
    return (0.5 * solid * solid) / (open_part * open_part * open_part)


def resistance(logperm, factor, top):
    return jnp.minimum(jnp.exp(top - logperm) * factor, HUGE)


def reciprocal(x):
    guess = pl.reciprocal(x, approx=True)
    return guess * (2.0 - x * guess)


WIDE = ((8, 48), (56, 48), (104, 48))
OWN_ROWS = ((16, 64), (80, 64))


def operate_powers(
    partial, factor, edge_factor, edge_source, source, from_up, from_down,
    power1, power2, power3, table,
    resist, across_x, across_y, across_z, flow, field0, field1, field2, field3, plane_resist, plane_field,
    side_resist, side_x, side_y, side_z, side0, side1, side2, side_flux, done,
):
    lane = iota((8, N), 1)
    row8 = iota((8, N), 0)

    _, halo = row_weights()
    edge_lane = (iota((144, N), 1) % 8 <= 2) | (iota((144, N), 1) % 8 >= 5)
    row144 = iota((144, N), 0)
    real_row = (row144 >= 5) & (row144 <= 138)

    def halo_rows(z):
        first = pl.multiple_of(z * 72, 8)
        return jnp.concatenate([from_up[pl.ds(first + 8, 64), :], from_down[pl.ds(first, 64), :]], axis=0)

    def finish(z, out, sums, real):
        first = pl.multiple_of(z * 72, 8)
        above = jnp.where(row8 >= 5, from_up[pl.ds(first, 8), :], 0.0)
        below = jnp.where(row8 <= 2, from_down[pl.ds(first + 64, 8), :], 0.0)
        above = jnp.where(row8 >= 5, above + roll(above, 7, 0) + roll(above, 6, 0), 0.0)
        below = jnp.where(row8 <= 2, below + roll(below, 1, 0) + roll(below, 2, 0), 0.0)
        total = sums + partial[z]
        total = jnp.concatenate([total[:8] + above, total[8:136], total[136:] + below], axis=0) * (1.0 / WIDTH)
        out[8:152, :] = total
        return jnp.max(jnp.where(real, total, -HUGE).reshape(18, 8, N), axis=0)

    def smooth(k, largest):
        first, second = row_sums(halo, halo_rows(2 * k), halo_rows(2 * k + 1))
        largest = jnp.maximum(largest, finish(2 * k, resist.at[2 * k], first, real_row))
        return jnp.maximum(largest, finish(2 * k + 1, resist.at[2 * k + 1], second, real_row))

    largest = finish(16, plane_resist, row_sums(halo, halo_rows(16))[0], real_row & edge_lane)
    largest = lax.fori_loop(0, 8, smooth, largest, unroll=U4)
    top = jnp.max(jnp.max(largest, axis=0, keepdims=True), axis=1, keepdims=True)
    top = jnp.maximum(top, -60.0)

    def halo_tiles(z):
        first = pl.multiple_of(z * 72, 8)
        above = from_up[pl.ds(first, 8), :]
        below = from_down[pl.ds(first + 64, 8), :]
        third_above = from_up[pl.ds(17 * 72 + z, 1), :]
        third_below = from_down[pl.ds(17 * 72 + z, 1), :]
        source_above = jnp.where(row8 >= 5, roll(above, 5, 0), 0.0)
        source_below = jnp.where(row8 <= 2, roll(below, 5, 0), 0.0)
        biofilm_above = jnp.where(row8 == 5, third_above, jnp.where(row8 >= 6, roll(above, 3, 0), 0.0))
        biofilm_below = jnp.where(row8 == 2, third_below, jnp.where(row8 <= 1, roll(below, 2, 0), 0.0))
        return source_above, source_below, biofilm_above, biofilm_below

    def prepare(z, out, field, own_source, own_factor):
        source_above, source_below, biofilm_above, biofilm_below = halo_tiles(z)
        field[8:16, :] = source_above
        field[16:144, :] = own_source
        field[144:152, :] = source_below
        out[8:16, :] = jnp.where(row8 >= 5, resistance(out[8:16, :], resistance_factor(biofilm_above), top), HUGE)
        out[144:152, :] = jnp.where(row8 <= 2, resistance(out[144:152, :], resistance_factor(biofilm_below), top), HUGE)
        out[16:144, :] = resistance(out[16:144, :], own_factor, top)
        empty = jnp.full((8, N), HUGE, F32)
        none = jnp.zeros((8, N), F32)
        out[0:8, :] = empty
        out[152:160, :] = empty
        field[0:8, :] = none
        field[152:160, :] = none

    def prepare_layer(z, carry):
        prepare(z, resist.at[z], field0.at[z], source[z], factor[z])
        none = jnp.zeros((8, N), F32)
        for ref in (field1, field2, across_x):
            ref[z, 0:8, :] = none
            ref[z, 152:160, :] = none
        return carry

    prepare(16, plane_resist, plane_field, edge_source[...], edge_factor[...])
    lax.fori_loop(0, 16, prepare_layer, 0, unroll=U6)

    a = iota((N, 2 * N), 0)
    o = iota((N, 2 * N), 1)
    t = o % 16
    spread = weights(
        (a // 8 == o // 16)
        & (((t >= 3) & (t <= 5) & (a % 8 == t - 3)) | ((t >= 10) & (t <= 12) & (a % 8 == t - 5)))
    )
    lane160 = iota((ROWS, N), 1)
    slot160 = lane160 % 16
    for plane, field, side, fill in ((plane_resist, resist, side_resist, HUGE), (plane_field, field0, side0, 0.0)):
        high, mid, low = split3(plane[...])
        outer = dot(high, spread) + dot(mid, spread) + dot(low, spread)
        for p in range(2):
            inner = jnp.zeros((ROWS, N), F32)
            for k in range(8):
                inner = jnp.where(lane160 // 16 == k, roll(field[8 * p + k], 16 * k + 3, 1), inner)
            value = jnp.where(slot160 <= 2, inner, jnp.where(slot160 >= 13, roll(inner, 10, 1), outer[:, p * N : p * N + N]))
            side[p] = jnp.where((slot160 <= 5) | (slot160 >= 10), value, fill)
    none = jnp.zeros((8, N), F32)
    for p in range(2):
        for ref in (side1, side2, side_x):
            ref[p, 0:8, :] = none
            ref[p, 152:160, :] = none

    def next_layer(first, second):
        lanes = iota(first.shape, 1)
        return jnp.where(lanes < 112, roll(first, -16, 1), roll(second, -16, 1)), roll(second, -16, 1)

    def last_layer(first, second):
        lanes = iota(first.shape, 1)
        return (
            jnp.where(lanes >= 16, roll(first, 16, 1), 0.0),
            jnp.where(lanes >= 16, roll(second, 16, 1), roll(first, 16, 1)),
        )

    for start, size in WIDE:
        rows = slice(start, start + size)
        here = [side_resist[p, rows, :] for p in range(2)]
        after = next_layer(*here)
        for p in range(2):
            side_x[p, rows, :] = reciprocal(here[p] + side_resist[p, start - 1 : start - 1 + size, :])
            side_y[p, rows, :] = reciprocal(here[p] + roll(here[p], 1, 1))
            value = reciprocal(here[p] + after[p])
            side_z[p, rows, :] = value if p == 0 else jnp.where(iota((size, N), 1) < 112, value, 0.0)

    def faces(z, carry):
        for start, size in WIDE:
            rows = slice(start, start + size)
            here = resist[z, rows, :]
            across_x[z, rows, :] = reciprocal(here + resist[z, start - 1 : start - 1 + size, :])
            across_y[z, rows, :] = jnp.where(iota((size, N), 1) == 0, 0.0, reciprocal(here + roll(here, 1, 1)))
            above = resist[jnp.maximum(z - 1, 0), rows, :]
            across_z[z, rows, :] = jnp.where(z > 0, reciprocal(here + above), 0.0)
        return carry

    lax.fori_loop(0, 16, faces, 0, unroll=U5)
    across_z[16] = jnp.zeros((ROWS, N), F32)

    def apply_sides(field, image):
        for start, size in WIDE:
            rows = slice(start, start + size)
            slot = iota((size, N), 1) % 16
            here = [field[p, rows, :] for p in range(2)]
            inward = [side_y[p, rows, :] * (here[p] - roll(here[p], 1, 1)) for p in range(2)]
            for p in range(2):
                side_flux[p, rows, :] = jnp.where(slot == 13, inward[p], -roll(inward[p], 9, 1))
            if image is None:
                continue
            after = next_layer(*here)
            through = [side_z[p, rows, :] * (after[p] - here[p]) for p in range(2)]
            back = last_layer(*through)
            for p in range(2):
                value = inward[p] - roll(inward[p], -1, 1) - through[p] + back[p]
                value = value + side_x[p, rows, :] * (here[p] - field[p, start - 1 : start - 1 + size, :])
                value = value - side_x[p, start + 1 : start + 1 + size, :] * (
                    field[p, start + 1 : start + 1 + size, :] - here[p]
                )
                image[p, rows, :] = value

    def flow_along_y(field):
        def layer(z, carry):
            for start, size in WIDE:
                rows = slice(start, start + size)
                here = field[z, rows, :]
                flow[z, rows, :] = across_y[z, rows, :] * (here - roll(here, 1, 1))
            return carry

        lax.fori_loop(0, 16, layer, 0, unroll=U1)

    def apply_rows(field, z, start, size):
        rows = slice(start, start + size)
        lanes = iota((size, N), 1)
        here = field[z, rows, :]
        inward = flow[z, rows, :]
        value = inward - roll(inward, -1, 1)
        beside = roll(side_flux[z // 8, rows, :], 115 - 16 * (z % 8), 1)
        value = value + jnp.where((lanes == 0) | (lanes == 127), beside, 0.0)
        value = value + across_x[z, rows, :] * (here - field[z, start - 1 : start - 1 + size, :])
        value = value - across_x[z, start + 1 : start + 1 + size, :] * (
            field[z, start + 1 : start + 1 + size, :] - here
        )
        value = value + across_z[z, rows, :] * (here - field[jnp.maximum(z - 1, 0), rows, :])
        return value - across_z[z + 1, rows, :] * (field[jnp.minimum(z + 1, 15), rows, :] - here)

    def apply(field, image):
        flow_along_y(field)

        def layer(z, carry):
            for start, size in WIDE:
                image[z, start : start + size, :] = apply_rows(field, z, start, size)
            return carry

        lax.fori_loop(0, 16, layer, 0, unroll=U2)

    def hand_out(field, power, k):
        return pltpu.make_async_copy(field.at[:, 16:144, :], power, done.at[k])

    apply_sides(side0, side1)
    apply(field0, field1)
    hand_out(field1, power1, 0).start()
    apply_sides(side1, side2)
    apply(field1, field2)
    hand_out(field2, power2, 1).start()
    apply_sides(side2, None)
    flow_along_y(field2)

    def last(z, sums):
        for start, size in OWN_ROWS:
            rows = slice(start, start + size)
            f3 = apply_rows(field2, z, start, size)
            field3[z, start - 16 : start - 16 + size, :] = f3
            f0 = field0[z, rows, :]
            f1 = field1[z, rows, :]
            f2 = field2[z, rows, :]
            terms = (f0 * f0, f0 * f1, f1 * f1, f1 * f2, f2 * f2, f2 * f3)
            sums = tuple(s + jnp.sum(t.reshape(size // 8, 8, N), axis=0) for s, t in zip(sums, terms))
        pltpu.make_async_copy(field3.at[z], power3.at[z], done.at[2]).start()
        return sums

    sums = lax.fori_loop(0, 16, last, tuple(jnp.zeros((8, N), F32) for _ in range(6)), unroll=U3)
    line = jnp.where((lane[:1] >= 8) & (lane[:1] < 16), top, 0.0)
    for k, s in enumerate(sums):
        amount = jnp.sum(jnp.sum(s, axis=0, keepdims=True), axis=1, keepdims=True)
        line = jnp.where(lane[:1] == k, amount, line)
    table[...] = jnp.broadcast_to(line, table.shape)
    hand_out(field1, power1, 0).wait()
    hand_out(field2, power2, 1).wait()
    pltpu.make_async_copy(field3, power3, done.at[2]).wait()


def coefficients(everyone, own):
    n = everyone.shape[0]
    rows = everyone[...]
    lane = iota((n, N), 1)
    tops = jnp.where(lane < 8, roll(rows, -8, 1), 0.0)
    top = jnp.max(tops, axis=0, keepdims=True)
    top = jnp.max(jnp.where(lane[:1] == 0, top, -HUGE), axis=1, keepdims=True)
    factor = jnp.exp((tops - top) * lane.astype(F32))
    moments = jnp.sum(jnp.where(lane < 6, rows * factor, 0.0), axis=0, keepdims=True)
    u0, u1, u2, u3, u4, u5 = [
        jnp.sum(jnp.where(lane[:1] == k, moments, 0.0), axis=1, keepdims=True) for k in range(6)
    ]
    own_top = jnp.sum(jnp.where(lane[:1] == 8, own[0:1, :], 0.0), axis=1, keepdims=True)
    ratio = jnp.exp(own_top - top)

    def over(a, b):
        return jnp.where(b > 0.0, a / jnp.where(b > 0.0, b, 1.0), 0.0)

    l10 = over(u1, u0)
    l20 = over(u2, u0)
    d1 = u2 - l10 * u1
    s12 = u3 - l10 * u2
    l21 = over(s12, d1)
    d2 = (u4 - l20 * u2) - l21 * s12
    y1 = u4 - l10 * u3
    y2 = u5 - l20 * u3 - l21 * y1
    e2 = -over(y2, d2)
    e1 = -over(y1, d1) - l21 * e2
    e0 = -over(u3, u0) - l10 * e1 - l20 * e2

    sigma = jnp.exp(top)
    tau = jnp.minimum(1.0, 2.0 * sigma)
    kappa = jnp.minimum(1.0, 0.5 / sigma)
    at_zero = ((e0 * tau - e1 * kappa) * tau + e2 * kappa * kappa) * tau - kappa * kappa * kappa
    r_scale = tau * tau * tau / at_zero
    p_scale = -jnp.minimum(1.0 / sigma, 2.0) / at_zero
    q1 = tau * e2 - kappa
    r0 = r_scale * e0
    r1 = r_scale * e1 * ratio
    r2 = r_scale * e2 * ratio * ratio
    r3 = r_scale * ratio * ratio * ratio
    p0 = p_scale * (tau * tau * e1 - kappa * q1)
    p1 = p_scale * (tau * q1) * ratio
    p2 = p_scale * (tau * tau) * ratio * ratio
    return p0, p1, p2, r0, r1, r2, r3


def combine(
    everyone, own, source_in, power1_in, power2_in, power3_in, pressure_out, residual_out,
    source, power1, power2, power3, pressure, residual, arrived, left,
):
    def arrivals(g):
        part = slice(4 * g, 4 * g + 4)
        pairs = ((source_in, source), (power1_in, power1), (power2_in, power2), (power3_in, power3))
        return [
            pltpu.make_async_copy(far.at[part], near.at[part], arrived.at[k, g]) for k, (far, near) in enumerate(pairs)
        ]

    def departures(g):
        part = slice(4 * g, 4 * g + 4)
        return [
            pltpu.make_async_copy(near.at[part], far.at[part], left.at[k, g])
            for k, (near, far) in enumerate(((pressure, pressure_out), (residual, residual_out)))
        ]

    for g in range(4):
        for copy in arrivals(g):
            copy.start()
    p0, p1, p2, r0, r1, r2, r3 = coefficients(everyone, own)
    for g in range(4):
        for copy in arrivals(g):
            copy.wait()
        for z in range(4 * g, 4 * g + 4):
            f0 = source[z]
            f1 = power1[z]
            f2 = power2[z]
            pressure[z] = p0 * f0 + p1 * f1 + p2 * f2
            residual[z] = (r0 * f0 + r1 * f1) + (r2 * f2 + r3 * power3[z])
        for copy in departures(g):
            copy.start()
    for g in range(4):
        for copy in departures(g):
            copy.wait()


def vmem(count):
    return [pl.BlockSpec(memory_space=pltpu.VMEM)] * count


def shape(*dims):
    return jax.ShapeDtypeStruct(dims, F32)


def hbm(count):
    return [pl.BlockSpec(memory_space=pltpu.HBM)] * count


def in_hbm(x):
    return pltpu.with_memory_space_constraint(x, pltpu.HBM)


def call(body, inputs, out, out_specs, scratch=(), name=None, cost=1e6):
    return pl.pallas_call(
        body,
        out_shape=out,
        in_specs=inputs,
        out_specs=out_specs,
        scratch_shapes=list(scratch),
        compiler_params=pltpu.CompilerParams(vmem_limit_bytes=40 * 1024 * 1024),
        cost_estimate=pl.CostEstimate(flops=int(cost), bytes_accessed=int(cost), transcendentals=0),
        name=name,
    )


def exchange(to_next, to_previous, axis):
    count = lax.axis_size(axis)
    forward = [(i, (i + 1) % count) for i in range(count)]
    backward = [(target, source) for source, target in forward]
    return lax.ppermute(to_next, axis, forward), lax.ppermute(to_previous, axis, backward)


def local(noise, biofilm, source):
    block = pltpu.VMEM((NZ, N, N), F32)
    to_right, to_left = call(
        pack_columns,
        hbm(3),
        [shape(MSG_Y, N)] * 2,
        vmem(2),
        [block, block, pltpu.VMEM((NZ, N, N), jnp.int32), pltpu.SemaphoreType.DMA((3, 8))],
        name="pack",
    )(in_hbm(noise), in_hbm(source), in_hbm(biofilm))
    from_left, from_right = exchange(to_right, to_left, "gy")
    own_middle, own_edge, factor = call(
        column_sums_own,
        vmem(2),
        [shape(NZ, N, N), shape(N, N), shape(NZ, N, N)],
        vmem(3),
        name="columns_own",
    )(noise, biofilm)
    middle, edge, edge_source, edge_biofilm, to_down, to_up = call(
        smooth_columns,
        vmem(6),
        [shape(NZ, N, N), shape(N, N), shape(N, N), shape(N, N), shape(MSG_X, N), shape(MSG_X, N)],
        vmem(6),
        name="columns",
    )(own_middle, own_edge, source, biofilm, from_left, from_right)
    from_up, from_down = exchange(to_down, to_up, "gx")
    partial, edge_factor = call(
        row_sums_own,
        vmem(3),
        [shape(NZ + 1, 144, N), shape(N, N)],
        vmem(2),
        name="rows_own",
    )(middle, edge, edge_biofilm)
    devices = lax.axis_size("gx") * lax.axis_size("gy")
    layers = pltpu.VMEM((NZ, ROWS, N), F32)
    plane = pltpu.VMEM((ROWS, N), F32)
    sides = pltpu.VMEM((2, ROWS, N), F32)
    power1, power2, power3, table = call(
        operate_powers,
        vmem(7),
        [pltpu.HBM((NZ, N, N), F32)] * 3 + [shape(devices, N)],
        hbm(3) + vmem(1),
        [layers] * 3
        + [pltpu.VMEM((NZ + 1, ROWS, N), F32)]
        + [layers] * 4
        + [block, plane, plane]
        + [sides] * 8
        + [pltpu.SemaphoreType.DMA((3,))],
        name="powers",
    )(partial, factor, edge_factor, edge_source, source, from_up, from_down)
    everyone = lax.all_to_all(table, ("gx", "gy"), 0, 0, tiled=True)
    return tuple(
        call(
            combine,
            vmem(2) + hbm(4),
            [pltpu.HBM((NZ, N, N), F32)] * 2,
            hbm(2),
            [block] * 6 + [pltpu.SemaphoreType.DMA((4, 4)), pltpu.SemaphoreType.DMA((2, 4))],
            name="combine",
        )(everyone, table, *[in_hbm(x) for x in (source, power1, power2, power3)])
    )


def solution(mesh):
    in_specs = (P(None, "gx", "gy"), P(None, "gx", "gy"), P(None, "gx", "gy"))
    out_specs = (P(None, "gx", "gy"), P(None, "gx", "gy"))
    return jax.shard_map(local, mesh=mesh, in_specs=in_specs, out_specs=out_specs, check_vma=False)
```

```python
import jax
import jax.numpy as jnp
from jax import lax
from jax.experimental import pallas as pl
from jax.experimental.pallas import tpu as pltpu
from jax.sharding import PartitionSpec as P

R = 64
WIDTH = 2 * R + 1
NZ = 16
N = 128
F32 = jnp.float32
BF16 = jnp.bfloat16

Y_ROWS = (4 * N, 4 * N + N + 16)
X_ROWS = (8 * 72 + 8, 9 * 72 + 16)
ROWS = 160
OWN = 16
HUGE = 1e30
U1, U2, U3, U5, U6 = 16, 4, 2, 4, 2


def iota(shape, dim):
    return lax.broadcasted_iota(jnp.int32, shape, dim)


def roll(x, shift, axis):
    if isinstance(shift, int):
        shift = shift % x.shape[axis]
        if shift == 0:
            return x
    return pltpu.roll(x, shift, axis)


def split3(x):
    high = x.astype(BF16)
    rest = x - high.astype(F32)
    middle = rest.astype(BF16)
    low = (rest - middle.astype(F32)).astype(BF16)
    return high, middle, low


def split2(x):
    high = x.astype(BF16)
    return high, (x - high.astype(F32)).astype(BF16)


def dot(a, b):
    return lax.dot_general(a, b, (((1,), (0,)), ((), ())), preferred_element_type=F32)


def weights(mask):
    return jnp.where(mask, 1.0, 0.0).astype(BF16)


def pack_first(noise_in, to_right, to_left, noise, arrived):
    low = iota((N, N), 1) < 64
    copies = [
        pltpu.make_async_copy(noise_in.at[2 * q : 2 * q + 2], noise.at[2 * q : 2 * q + 2], arrived.at[q])
        for q in range(4)
    ]
    for copy in copies:
        copy.start()
    for q in range(4):
        copies[q].wait()
        even = noise[2 * q]
        odd = noise[2 * q + 1]
        to_right[q * N : q * N + N, :] = jnp.where(low, roll(even, 64, 1), odd)
        to_left[q * N : q * N + N, :] = jnp.where(low, even, roll(odd, 64, 1))


def pack_second(noise_in, source_in, biofilm_in, to_right, to_left, noise, source, biofilm, arrived):
    def arrivals(g):
        rows = slice(16 * g, 16 * g + 16)
        return [
            pltpu.make_async_copy(far.at[:, rows, :], near.at[:, rows, :], arrived.at[k, g])
            for k, (far, near) in enumerate(((noise_in, noise), (source_in, source), (biofilm_in, biofilm)))
        ]

    for g in range(8):
        for copy in arrivals(g):
            copy.start()

    lane = iota((16, N), 1)
    slot = lane % 8
    group = lane // 8
    low = lane < 64

    third_right = jnp.zeros((16, N), F32)
    third_left = jnp.zeros((16, N), F32)
    for g in range(8):
        for copy in arrivals(g):
            copy.wait()
        rows = slice(16 * g, 16 * g + 16)
        zero = jnp.zeros((16, N), F32)
        nr, sr, nl, sl = zero, zero, zero, zero
        br = jnp.zeros((16, N), jnp.int32)
        bl = br
        for q in range(8):
            even = noise[2 * q, rows, :]
            odd = noise[2 * q + 1, rows, :]
            if q >= 4:
                first = (q - 4) * N + 16 * g
                to_right[first : first + 16, :] = jnp.where(low, roll(even, 64, 1), odd)
                to_left[first : first + 16, :] = jnp.where(low, even, roll(odd, 64, 1))
            for z, n in ((2 * q, even), (2 * q + 1, odd)):
                here = group == z
                s = source[z, rows, :]
                b = biofilm[z, rows, :]
                nr = jnp.where(here, roll(n, 8 * z - 61, 1), nr)
                nl = jnp.where(here, roll(n, 8 * z + 5 - 64, 1), nl)
                sr = jnp.where(here, roll(s, 8 * z + 8, 1), sr)
                sl = jnp.where(here, roll(s, 8 * z, 1), sl)
                br = jnp.where(here, roll(b, 8 * z + 8, 1), br)
                bl = jnp.where(here, roll(b, 8 * z, 1), bl)
        br = br.astype(F32)
        bl = bl.astype(F32)
        first = 4 * N + 16 * g
        to_right[first : first + 16, :] = jnp.where(slot < 3, nr, jnp.where(slot < 5, roll(br, -3, 1), sr))
        to_left[first : first + 16, :] = jnp.where(slot < 3, sl, jnp.where(slot < 5, roll(bl, 3, 1), nl))
        third_right = third_right + roll(jnp.where(slot == 5, br, 0.0), g, 1)
        third_left = third_left + roll(jnp.where(slot == 2, bl, 0.0), g, 1)
    to_right[5 * N :, :] = third_right
    to_left[5 * N :, :] = third_left


def column_weights():
    m = iota((N, 2 * N), 0)
    o = iota((N, 2 * N), 1)
    s = o - N
    own = ((o < N) & (m - o <= R) & (o - m <= R)) | ((o >= N) & (s <= 2) & (m >= s + 64)) | (
        (s >= 5) & (s <= 7) & (m <= s + 56)
    )
    lane = iota((N, 3 * N), 0)
    o = iota((N, 3 * N), 1)
    half = lane // 64
    m = lane % 64
    e = o - 2 * N
    same = (o < 2 * N) & (o // N == half)
    edge = (e >= 0) & (e < 16) & (e // 8 == half)
    left = (same & (m >= o % N)) | (edge & (o % 8 >= 5))
    right = (same & (m + 64 <= o % N)) | (edge & (o % 8 <= 2))
    a = iota((N, N), 0)
    b = iota((N, N), 1)
    together = a // 8 == b // 8
    t = a % 8
    s = b % 8
    left_extra = together & (t <= 2) & (s >= 5) & (t >= s - 5)
    right_extra = together & (t >= 5) & (s <= 2) & (t - 5 <= s)
    return [weights(w) for w in (own, left, right, left_extra, right_extra)]


def column_sums_own(noise, biofilm, own_middle, own_edge, factor):
    own = column_weights()[0]
    twice = jnp.concatenate([own, own], axis=0)
    total = jnp.zeros((N, N), F32)
    for z in range(16):
        out = dot(jnp.concatenate(split2(noise[z]), axis=1), twice)
        own_middle[z] = out[:, :N]
        total = total + roll(out[:, N:], 8 * z, 1)
        factor[z] = resistance_factor(biofilm[z].astype(F32))
    own_edge[...] = total


def sums_beside(x, y, w):
    high, low = split2(jnp.concatenate([x, y], axis=1))
    return dot(high, w) + dot(low, w)


def half_columns(first_layer, own_middle, from_left, from_right, middle, to_down, to_up):
    _, left, right, _, _ = column_weights()
    both = jnp.concatenate([left, right], axis=0)
    total = jnp.zeros((N, N), F32)
    for q in range(4):
        rows = slice(q * N, q * N + N)
        halo = sums_beside(from_left[rows, :], from_right[rows, :], both)
        total = total + roll(halo[:, 2 * N :], 8 * first_layer + 16 * q, 1)
        for k in (0, 1):
            z = 2 * q + k
            field = own_middle[first_layer + z] + halo[:, k * N : k * N + N]
            middle[z] = field
            to_down[z * 72 : z * 72 + 72, :] = field[56:, :]
            to_up[z * 72 : z * 72 + 72, :] = field[:72, :]
    return total


def outer_rows(to_down, to_up, z, tail, s, b):
    to_down[z * 72 : z * 72 + 3, :] = s[125:128, :]
    to_down[z * 72 + 3 : z * 72 + 5, :] = b[126:128, :].astype(F32)
    to_down[tail + z : tail + z + 1, :] = b[125:126, :].astype(F32)
    to_up[z * 72 + 67 : z * 72 + 70, :] = s[0:3, :]
    to_up[z * 72 + 70 : z * 72 + 72, :] = b[0:2, :].astype(F32)
    to_up[tail + z : tail + z + 1, :] = b[2:3, :].astype(F32)


def columns_first(own_middle, source, biofilm, from_left, from_right, middle, edge, to_down, to_up):
    edge[...] = half_columns(0, own_middle, from_left, from_right, middle, to_down, to_up)
    for z in range(8):
        outer_rows(to_down, to_up, z, 8 * 72, source.at[z], biofilm.at[z])


def columns_second(
    own_middle, own_edge, first_edge, source, biofilm, from_left, from_right,
    middle, edge, edge_source, edge_biofilm, to_down, to_up,
):
    _, _, _, left_extra, right_extra = column_weights()
    slot = iota((N, N), 1) % 8
    extra_left = from_left[4 * N : 5 * N, :]
    extra_right = from_right[4 * N : 5 * N, :]
    total = own_edge[...] + first_edge[...]
    total = total + sums_beside(extra_left, extra_right, jnp.concatenate([left_extra, right_extra], axis=0))
    total = total + half_columns(8, own_middle, from_left, from_right, middle, to_down, to_up)
    edge[...] = total
    to_down[8 * 72 : 9 * 72, :] = total[56:, :]
    to_up[8 * 72 : 9 * 72, :] = total[:72, :]

    edge_source[...] = jnp.where(slot >= 5, extra_left, jnp.where(slot <= 2, extra_right, 0.0))
    third_left = from_left[5 * N :, :]
    third_right = from_right[5 * N :, :]
    levels = jnp.where(slot >= 6, roll(extra_left, 3, 1), jnp.where(slot <= 1, roll(extra_right, -3, 1), 0.0))
    slot16 = iota((16, N), 1) % 8
    for g in range(8):
        rows = slice(16 * g, 16 * g + 16)
        edge_biofilm[rows, :] = jnp.where(
            slot16 == 5, roll(third_left, -g, 1), jnp.where(slot16 == 2, roll(third_right, -g, 1), levels[rows, :])
        )

    to_down[9 * 72 :, :] = jnp.zeros((16, N), F32)
    to_up[9 * 72 :, :] = jnp.zeros((16, N), F32)
    for z in range(8):
        outer_rows(to_down, to_up, z, 9 * 72, source.at[8 + z], biofilm.at[8 + z])
    outer_rows(to_down, to_up, 8, 9 * 72, edge_source, edge_biofilm)


def row_weights():
    r = iota((144, N), 0) - 8
    m = iota((144, N), 1)
    inside = (r >= -3) & (r <= 130)
    own = inside & (m >= r - R) & (m <= r + R)
    halo = inside & (((m < 64) & (m >= r)) | ((m >= 64) & (m <= r)))
    return weights(own), weights(halo)


def row_sums(band, *planes):
    columns = [jnp.concatenate(split2(p), axis=0) for p in planes]
    out = dot(jnp.concatenate([band, band], axis=1), jnp.concatenate(columns, axis=1))
    return [out[:, k * N : k * N + N] for k in range(len(planes))]


def halo_rows(from_up, from_down, z):
    first = pl.multiple_of(z * 72, 8)
    return jnp.concatenate([from_up[pl.ds(first + 8, 64), :], from_down[pl.ds(first, 64), :]], axis=0)


def finish_sums(from_up, from_down, z, sums, out, lanes=None):
    row8 = iota((8, N), 0)
    row144 = iota((144, N), 0)
    first = pl.multiple_of(z * 72, 8)
    above = jnp.where(row8 >= 5, from_up[pl.ds(first, 8), :], 0.0)
    below = jnp.where(row8 <= 2, from_down[pl.ds(first + 64, 8), :], 0.0)
    above = jnp.where(row8 >= 5, above + roll(above, 7, 0) + roll(above, 6, 0), 0.0)
    below = jnp.where(row8 <= 2, below + roll(below, 1, 0) + roll(below, 2, 0), 0.0)
    total = jnp.concatenate([sums[:8] + above, sums[8:136], sums[136:] + below], axis=0) * (1.0 / WIDTH)
    out[...] = total
    real = (row144 >= 5) & (row144 <= 138)
    if lanes is not None:
        real = real & lanes
    return jnp.max(jnp.where(real, total, -HUGE).reshape(18, 8, N), axis=0)


def rows_first(middle, from_up, from_down, logperm, largest):
    own, halo = row_weights()
    most = jnp.full((8, N), -HUGE, F32)
    for z in range(0, 8, 2):
        inner = row_sums(own, middle[z], middle[z + 1])
        outer = row_sums(halo, *[halo_rows(from_up, from_down, z + i) for i in (0, 1)])
        for i in (0, 1):
            most = jnp.maximum(
                most, finish_sums(from_up, from_down, z + i, inner[i] + outer[i], logperm.at[z + i])
            )
    largest[...] = most


def row_sums_own(middle, edge, edge_biofilm, partial, factor):
    own, _ = row_weights()
    for z in range(0, 8, 2):
        partial[z], partial[z + 1] = row_sums(own, middle[z], middle[z + 1])
    partial[8] = row_sums(own, edge[...])[0]
    factor[...] = resistance_factor(edge_biofilm[...])


def resistance_factor(biofilm):
    open_part = 1.0 - 0.06 * biofilm
    solid = (1.0 - 0.35 * open_part) * (1.0 / (1.0 - 0.35))
    return (0.5 * solid * solid) / (open_part * open_part * open_part)


def resistance(logperm, factor, top):
    return jnp.minimum(jnp.exp(top - logperm) * factor, HUGE)


def reciprocal(x):
    guess = pl.reciprocal(x, approx=True)
    return guess * (2.0 - x * guess)


WIDE = ((8, 48), (56, 48), (104, 48))
OWN_ROWS = ((16, 64), (80, 64))


def operate_powers(
    logperm1, largest1, partial, factor, edge_factor, edge_source, source, from_up1, from_down1, from_up2, from_down2,
    power1, power2, power3, table,
    resist, across_x, across_y, across_z, flow, field0, field1, field2, field3, logperm2, plane_resist, plane_field,
    side_resist, side_x, side_y, side_z, side0, side1, side2, side_flux, done,
):
    lane = iota((8, N), 1)
    row8 = iota((8, N), 0)

    _, halo = row_weights()
    edge_lane = (iota((144, N), 1) % 8 <= 2) | (iota((144, N), 1) % 8 >= 5)
    second = (from_up2, from_down2)
    largest = largest1[...]
    for z in (0, 2, 4, 6):
        pair = row_sums(halo, halo_rows(*second, z), halo_rows(*second, z + 1))
        for i in (0, 1):
            sums = partial[z + i] + pair[i]
            largest = jnp.maximum(largest, finish_sums(*second, z + i, sums, logperm2.at[z + i]))
    sums = partial[8] + row_sums(halo, halo_rows(*second, 8))[0]
    largest = jnp.maximum(largest, finish_sums(*second, 8, sums, logperm2.at[8], edge_lane))
    top = jnp.max(jnp.max(largest, axis=0, keepdims=True), axis=1, keepdims=True)
    top = jnp.maximum(top, -60.0)

    def halo_tiles(half, z):
        from_up, from_down, tail = half
        first = pl.multiple_of(z * 72, 8)
        above = from_up[pl.ds(first, 8), :]
        below = from_down[pl.ds(first + 64, 8), :]
        third_above = from_up[pl.ds(tail + z, 1), :]
        third_below = from_down[pl.ds(tail + z, 1), :]
        source_above = jnp.where(row8 >= 5, roll(above, 5, 0), 0.0)
        source_below = jnp.where(row8 <= 2, roll(below, 5, 0), 0.0)
        biofilm_above = jnp.where(row8 == 5, third_above, jnp.where(row8 >= 6, roll(above, 3, 0), 0.0))
        biofilm_below = jnp.where(row8 == 2, third_below, jnp.where(row8 <= 1, roll(below, 2, 0), 0.0))
        return source_above, source_below, biofilm_above, biofilm_below

    first_half = (from_up1, from_down1, 8 * 72)
    second_half = (from_up2, from_down2, 9 * 72)

    def prepare(half, z, logperm, out, field, own_source, own_factor):
        source_above, source_below, biofilm_above, biofilm_below = halo_tiles(half, z)
        field[8:16, :] = source_above
        field[16:144, :] = own_source
        field[144:152, :] = source_below
        out[8:16, :] = jnp.where(row8 >= 5, resistance(logperm[0:8, :], resistance_factor(biofilm_above), top), HUGE)
        out[144:152, :] = jnp.where(row8 <= 2, resistance(logperm[136:144, :], resistance_factor(biofilm_below), top), HUGE)
        out[16:144, :] = resistance(logperm[8:136, :], own_factor, top)
        empty = jnp.full((8, N), HUGE, F32)
        none = jnp.zeros((8, N), F32)
        out[0:8, :] = empty
        out[152:160, :] = empty
        field[0:8, :] = none
        field[152:160, :] = none

    prepare(second_half, 8, logperm2.at[8], plane_resist, plane_field, edge_source[...], edge_factor[...])
    for base, half, logperm in ((0, first_half, logperm1), (8, second_half, logperm2)):

        def prepare_layer(k, carry, base=base, half=half, logperm=logperm):
            z = base + k
            prepare(half, k, logperm.at[k], resist.at[z], field0.at[z], source[z], factor[z])
            none = jnp.zeros((8, N), F32)
            for ref in (field1, field2, across_x):
                ref[z, 0:8, :] = none
                ref[z, 152:160, :] = none
            return carry

        lax.fori_loop(0, 8, prepare_layer, 0, unroll=U6)

    a = iota((N, 2 * N), 0)
    o = iota((N, 2 * N), 1)
    t = o % 16
    spread = weights(
        (a // 8 == o // 16)
        & (((t >= 3) & (t <= 5) & (a % 8 == t - 3)) | ((t >= 10) & (t <= 12) & (a % 8 == t - 5)))
    )
    lane160 = iota((ROWS, N), 1)
    slot160 = lane160 % 16
    for plane, field, side, fill in ((plane_resist, resist, side_resist, HUGE), (plane_field, field0, side0, 0.0)):
        high, mid, low = split3(plane[...])
        outer = dot(high, spread) + dot(mid, spread) + dot(low, spread)
        for p in range(2):
            inner = jnp.zeros((ROWS, N), F32)
            for k in range(8):
                inner = jnp.where(lane160 // 16 == k, roll(field[8 * p + k], 16 * k + 3, 1), inner)
            value = jnp.where(slot160 <= 2, inner, jnp.where(slot160 >= 13, roll(inner, 10, 1), outer[:, p * N : p * N + N]))
            side[p] = jnp.where((slot160 <= 5) | (slot160 >= 10), value, fill)
    none = jnp.zeros((8, N), F32)
    for p in range(2):
        for ref in (side1, side2, side_x):
            ref[p, 0:8, :] = none
            ref[p, 152:160, :] = none

    def next_layer(first, second):
        lanes = iota(first.shape, 1)
        return jnp.where(lanes < 112, roll(first, -16, 1), roll(second, -16, 1)), roll(second, -16, 1)

    def last_layer(first, second):
        lanes = iota(first.shape, 1)
        return (
            jnp.where(lanes >= 16, roll(first, 16, 1), 0.0),
            jnp.where(lanes >= 16, roll(second, 16, 1), roll(first, 16, 1)),
        )

    for start, size in WIDE:
        rows = slice(start, start + size)
        here = [side_resist[p, rows, :] for p in range(2)]
        after = next_layer(*here)
        for p in range(2):
            side_x[p, rows, :] = reciprocal(here[p] + side_resist[p, start - 1 : start - 1 + size, :])
            side_y[p, rows, :] = reciprocal(here[p] + roll(here[p], 1, 1))
            value = reciprocal(here[p] + after[p])
            side_z[p, rows, :] = value if p == 0 else jnp.where(iota((size, N), 1) < 112, value, 0.0)

    def faces(z, carry):
        for start, size in WIDE:
            rows = slice(start, start + size)
            here = resist[z, rows, :]
            across_x[z, rows, :] = reciprocal(here + resist[z, start - 1 : start - 1 + size, :])
            across_y[z, rows, :] = jnp.where(iota((size, N), 1) == 0, 0.0, reciprocal(here + roll(here, 1, 1)))
            above = resist[jnp.maximum(z - 1, 0), rows, :]
            across_z[z, rows, :] = jnp.where(z > 0, reciprocal(here + above), 0.0)
        return carry

    lax.fori_loop(0, 16, faces, 0, unroll=U5)
    across_z[16] = jnp.zeros((ROWS, N), F32)

    def apply_sides(field, image):
        for start, size in WIDE:
            rows = slice(start, start + size)
            slot = iota((size, N), 1) % 16
            here = [field[p, rows, :] for p in range(2)]
            inward = [side_y[p, rows, :] * (here[p] - roll(here[p], 1, 1)) for p in range(2)]
            for p in range(2):
                side_flux[p, rows, :] = jnp.where(slot == 13, inward[p], -roll(inward[p], 9, 1))
            if image is None:
                continue
            after = next_layer(*here)
            through = [side_z[p, rows, :] * (after[p] - here[p]) for p in range(2)]
            back = last_layer(*through)
            for p in range(2):
                value = inward[p] - roll(inward[p], -1, 1) - through[p] + back[p]
                value = value + side_x[p, rows, :] * (here[p] - field[p, start - 1 : start - 1 + size, :])
                value = value - side_x[p, start + 1 : start + 1 + size, :] * (
                    field[p, start + 1 : start + 1 + size, :] - here[p]
                )
                image[p, rows, :] = value

    def flow_along_y(field):
        def layer(z, carry):
            for start, size in WIDE:
                rows = slice(start, start + size)
                here = field[z, rows, :]
                flow[z, rows, :] = across_y[z, rows, :] * (here - roll(here, 1, 1))
            return carry

        lax.fori_loop(0, 16, layer, 0, unroll=U1)

    def apply_rows(field, z, start, size):
        rows = slice(start, start + size)
        lanes = iota((size, N), 1)
        here = field[z, rows, :]
        inward = flow[z, rows, :]
        value = inward - roll(inward, -1, 1)
        beside = roll(side_flux[z // 8, rows, :], 115 - 16 * (z % 8), 1)
        value = value + jnp.where((lanes == 0) | (lanes == 127), beside, 0.0)
        value = value + across_x[z, rows, :] * (here - field[z, start - 1 : start - 1 + size, :])
        value = value - across_x[z, start + 1 : start + 1 + size, :] * (
            field[z, start + 1 : start + 1 + size, :] - here
        )
        value = value + across_z[z, rows, :] * (here - field[jnp.maximum(z - 1, 0), rows, :])
        return value - across_z[z + 1, rows, :] * (field[jnp.minimum(z + 1, 15), rows, :] - here)

    def apply(field, image):
        flow_along_y(field)

        def layer(z, carry):
            for start, size in WIDE:
                image[z, start : start + size, :] = apply_rows(field, z, start, size)
            return carry

        lax.fori_loop(0, 16, layer, 0, unroll=U2)

    def hand_out(field, power, k):
        return pltpu.make_async_copy(field.at[:, 16:144, :], power, done.at[k])

    apply_sides(side0, side1)
    apply(field0, field1)
    hand_out(field1, power1, 0).start()
    apply_sides(side1, side2)
    apply(field1, field2)
    hand_out(field2, power2, 1).start()
    apply_sides(side2, None)
    flow_along_y(field2)

    def last(z, sums):
        for start, size in OWN_ROWS:
            rows = slice(start, start + size)
            f3 = apply_rows(field2, z, start, size)
            field3[z, start - 16 : start - 16 + size, :] = f3
            f0 = field0[z, rows, :]
            f1 = field1[z, rows, :]
            f2 = field2[z, rows, :]
            terms = (f0 * f0, f0 * f1, f1 * f1, f1 * f2, f2 * f2, f2 * f3)
            sums = tuple(s + jnp.sum(t.reshape(size // 8, 8, N), axis=0) for s, t in zip(sums, terms))
        pltpu.make_async_copy(field3.at[z], power3.at[z], done.at[2]).start()
        return sums

    sums = lax.fori_loop(0, 16, last, tuple(jnp.zeros((8, N), F32) for _ in range(6)), unroll=U3)
    line = jnp.where((lane[:1] >= 8) & (lane[:1] < 16), top, 0.0)
    for k, s in enumerate(sums):
        amount = jnp.sum(jnp.sum(s, axis=0, keepdims=True), axis=1, keepdims=True)
        line = jnp.where(lane[:1] == k, amount, line)
    table[...] = jnp.broadcast_to(line, table.shape)
    hand_out(field1, power1, 0).wait()
    hand_out(field2, power2, 1).wait()
    pltpu.make_async_copy(field3, power3, done.at[2]).wait()


def coefficients(everyone, own):
    n = everyone.shape[0]
    rows = everyone[...]
    lane = iota((n, N), 1)
    tops = jnp.where(lane < 8, roll(rows, -8, 1), 0.0)
    top = jnp.max(tops, axis=0, keepdims=True)
    top = jnp.max(jnp.where(lane[:1] == 0, top, -HUGE), axis=1, keepdims=True)
    factor = jnp.exp((tops - top) * lane.astype(F32))
    moments = jnp.sum(jnp.where(lane < 6, rows * factor, 0.0), axis=0, keepdims=True)
    u0, u1, u2, u3, u4, u5 = [
        jnp.sum(jnp.where(lane[:1] == k, moments, 0.0), axis=1, keepdims=True) for k in range(6)
    ]
    own_top = jnp.sum(jnp.where(lane[:1] == 8, own[0:1, :], 0.0), axis=1, keepdims=True)
    ratio = jnp.exp(own_top - top)

    def over(a, b):
        return jnp.where(b > 0.0, a / jnp.where(b > 0.0, b, 1.0), 0.0)

    l10 = over(u1, u0)
    l20 = over(u2, u0)
    d1 = u2 - l10 * u1
    s12 = u3 - l10 * u2
    l21 = over(s12, d1)
    d2 = (u4 - l20 * u2) - l21 * s12
    y1 = u4 - l10 * u3
    y2 = u5 - l20 * u3 - l21 * y1
    e2 = -over(y2, d2)
    e1 = -over(y1, d1) - l21 * e2
    e0 = -over(u3, u0) - l10 * e1 - l20 * e2

    sigma = jnp.exp(top)
    tau = jnp.minimum(1.0, 2.0 * sigma)
    kappa = jnp.minimum(1.0, 0.5 / sigma)
    at_zero = ((e0 * tau - e1 * kappa) * tau + e2 * kappa * kappa) * tau - kappa * kappa * kappa
    r_scale = tau * tau * tau / at_zero
    p_scale = -jnp.minimum(1.0 / sigma, 2.0) / at_zero
    q1 = tau * e2 - kappa
    r0 = r_scale * e0
    r1 = r_scale * e1 * ratio
    r2 = r_scale * e2 * ratio * ratio
    r3 = r_scale * ratio * ratio * ratio
    p0 = p_scale * (tau * tau * e1 - kappa * q1)
    p1 = p_scale * (tau * q1) * ratio
    p2 = p_scale * (tau * tau) * ratio * ratio
    return p0, p1, p2, r0, r1, r2, r3


def combine(
    everyone, own, source_in, power1_in, power2_in, power3_in, pressure_out, residual_out,
    source, power1, power2, power3, pressure, residual, arrived, left,
):
    def arrivals(g):
        part = slice(4 * g, 4 * g + 4)
        pairs = ((source_in, source), (power1_in, power1), (power2_in, power2), (power3_in, power3))
        return [
            pltpu.make_async_copy(far.at[part], near.at[part], arrived.at[k, g]) for k, (far, near) in enumerate(pairs)
        ]

    def departures(g):
        part = slice(4 * g, 4 * g + 4)
        return [
            pltpu.make_async_copy(near.at[part], far.at[part], left.at[k, g])
            for k, (near, far) in enumerate(((pressure, pressure_out), (residual, residual_out)))
        ]

    for g in range(4):
        for copy in arrivals(g):
            copy.start()
    p0, p1, p2, r0, r1, r2, r3 = coefficients(everyone, own)
    for g in range(4):
        for copy in arrivals(g):
            copy.wait()
        for z in range(4 * g, 4 * g + 4):
            f0 = source[z]
            f1 = power1[z]
            f2 = power2[z]
            pressure[z] = p0 * f0 + p1 * f1 + p2 * f2
            residual[z] = (r0 * f0 + r1 * f1) + (r2 * f2 + r3 * power3[z])
        for copy in departures(g):
            copy.start()
    for g in range(4):
        for copy in departures(g):
            copy.wait()


def vmem(count):
    return [pl.BlockSpec(memory_space=pltpu.VMEM)] * count


def shape(*dims):
    return jax.ShapeDtypeStruct(dims, F32)


def hbm(count):
    return [pl.BlockSpec(memory_space=pltpu.HBM)] * count


def in_hbm(x):
    return pltpu.with_memory_space_constraint(x, pltpu.HBM)


def call(body, inputs, out, out_specs, scratch=(), name=None, cost=1e6):
    return pl.pallas_call(
        body,
        out_shape=out,
        in_specs=inputs,
        out_specs=out_specs,
        scratch_shapes=list(scratch),
        compiler_params=pltpu.CompilerParams(vmem_limit_bytes=40 * 1024 * 1024),
        cost_estimate=pl.CostEstimate(flops=int(cost), bytes_accessed=int(cost), transcendentals=0),
        name=name,
    )


def exchange(to_next, to_previous, axis):
    count = lax.axis_size(axis)
    forward = [(i, (i + 1) % count) for i in range(count)]
    backward = [(target, source) for source, target in forward]
    return lax.ppermute(to_next, axis, forward), lax.ppermute(to_previous, axis, backward)


def local(noise, biofilm, source):
    block = pltpu.VMEM((NZ, N, N), F32)
    to_right, to_left = call(
        pack_first,
        hbm(1),
        [shape(Y_ROWS[0], N)] * 2,
        vmem(2),
        [pltpu.VMEM((8, N, N), F32), pltpu.SemaphoreType.DMA((4,))],
        name="pack_first",
    )(in_hbm(noise))
    beside1 = exchange(to_right, to_left, "gy")
    to_right, to_left = call(
        pack_second,
        hbm(3),
        [shape(Y_ROWS[1], N)] * 2,
        vmem(2),
        [block, block, pltpu.VMEM((NZ, N, N), jnp.int32), pltpu.SemaphoreType.DMA((3, 8))],
        name="pack_second",
        cost=2e10,
    )(in_hbm(noise), in_hbm(source), in_hbm(biofilm))
    beside2 = exchange(to_right, to_left, "gy")
    own_middle, own_edge, factor = call(
        column_sums_own,
        vmem(2),
        [shape(NZ, N, N), shape(N, N), shape(NZ, N, N)],
        vmem(3),
        name="columns_own",
        cost=2e10,
    )(noise, biofilm)
    middle1, first_edge, to_down, to_up = call(
        columns_first,
        vmem(5),
        [shape(8, N, N), shape(N, N)] + [shape(X_ROWS[0], N)] * 2,
        vmem(4),
        name="columns_first",
    )(own_middle, source, biofilm, *beside1)
    above_below1 = exchange(to_down, to_up, "gx")
    middle2, edge, edge_source, edge_biofilm, to_down, to_up = call(
        columns_second,
        vmem(7),
        [shape(8, N, N), shape(N, N), shape(N, N), shape(N, N)] + [shape(X_ROWS[1], N)] * 2,
        vmem(6),
        name="columns_second",
        cost=2e10,
    )(own_middle, own_edge, first_edge, source, biofilm, *beside2)
    above_below2 = exchange(to_down, to_up, "gx")
    partial, edge_factor = call(
        row_sums_own,
        vmem(3),
        [shape(9, 144, N), shape(N, N)],
        vmem(2),
        name="rows_own",
        cost=1,
    )(middle2, edge, edge_biofilm)
    logperm1, largest1 = call(
        rows_first,
        vmem(3),
        [shape(8, 144, N), shape(8, N)],
        vmem(2),
        name="rows_first",
        cost=2e10,
    )(middle1, *above_below1)
    devices = lax.axis_size("gx") * lax.axis_size("gy")
    layers = pltpu.VMEM((NZ, ROWS, N), F32)
    plane = pltpu.VMEM((ROWS, N), F32)
    sides = pltpu.VMEM((2, ROWS, N), F32)
    power1, power2, power3, table = call(
        operate_powers,
        vmem(11),
        [pltpu.HBM((NZ, N, N), F32)] * 3 + [shape(devices, N)],
        hbm(3) + vmem(1),
        [layers] * 3
        + [pltpu.VMEM((NZ + 1, ROWS, N), F32)]
        + [layers] * 4
        + [block, pltpu.VMEM((9, 144, N), F32), plane, plane]
        + [sides] * 8
        + [pltpu.SemaphoreType.DMA((3,))],
        name="powers",
    )(logperm1, largest1, partial, factor, edge_factor, edge_source, source, *above_below1, *above_below2)
    everyone = lax.all_to_all(table, ("gx", "gy"), 0, 0, tiled=True)
    return tuple(
        call(
            combine,
            vmem(2) + hbm(4),
            [pltpu.HBM((NZ, N, N), F32)] * 2,
            hbm(2),
            [block] * 6 + [pltpu.SemaphoreType.DMA((4, 4)), pltpu.SemaphoreType.DMA((2, 4))],
            name="combine",
        )(everyone, table, *[in_hbm(x) for x in (source, power1, power2, power3)])
    )


def solution(mesh):
    in_specs = (P(None, "gx", "gy"), P(None, "gx", "gy"), P(None, "gx", "gy"))
    out_specs = (P(None, "gx", "gy"), P(None, "gx", "gy"))
    return jax.shard_map(local, mesh=mesh, in_specs=in_specs, out_specs=out_specs, check_vma=False)
```

```python
import jax
import jax.numpy as jnp
from jax import lax
from jax.experimental import pallas as pl
from jax.experimental.pallas import tpu as pltpu
from jax.sharding import PartitionSpec as P

R = 64
WIDTH = 2 * R + 1
NZ = 16
N = 128
F32 = jnp.float32
BF16 = jnp.bfloat16

Y_ROWS = (4 * N, 4 * N + N + 16)
X_ROWS = (8 * 72 + 8, 9 * 72 + 16)
ROWS = 160
OWN = 16
HUGE = 1e30
U1, U2, U3, U5, U6 = 16, 4, 4, 16, 8
V2, V3 = 4, 1
C2, C3 = 144, 64


def iota(shape, dim):
    return lax.broadcasted_iota(jnp.int32, shape, dim)


def roll(x, shift, axis):
    if isinstance(shift, int):
        shift = shift % x.shape[axis]
        if shift == 0:
            return x
    return pltpu.roll(x, shift, axis)


def split3(x):
    high = x.astype(BF16)
    rest = x - high.astype(F32)
    middle = rest.astype(BF16)
    low = (rest - middle.astype(F32)).astype(BF16)
    return high, middle, low


def split2(x):
    high = x.astype(BF16)
    return high, (x - high.astype(F32)).astype(BF16)


def dot(a, b):
    return lax.dot_general(a, b, (((1,), (0,)), ((), ())), preferred_element_type=F32)


def weights(mask):
    return jnp.where(mask, 1.0, 0.0).astype(BF16)


def pack_first(noise_in, to_right, to_left, noise, arrived):
    low = iota((N, N), 1) < 64
    copies = [
        pltpu.make_async_copy(noise_in.at[2 * q : 2 * q + 2], noise.at[2 * q : 2 * q + 2], arrived.at[q])
        for q in range(4)
    ]
    for copy in copies:
        copy.start()
    for q in range(4):
        copies[q].wait()
        even = noise[2 * q]
        odd = noise[2 * q + 1]
        to_right[q * N : q * N + N, :] = jnp.where(low, roll(even, 64, 1), odd)
        to_left[q * N : q * N + N, :] = jnp.where(low, even, roll(odd, 64, 1))


def pack_second(noise, source_in, biofilm_in, to_right, to_left, source, biofilm, arrived):
    def arrivals(g):
        rows = slice(16 * g, 16 * g + 16)
        return [
            pltpu.make_async_copy(far.at[:, rows, :], near.at[:, rows, :], arrived.at[k, g])
            for k, (far, near) in enumerate(((source_in, source), (biofilm_in, biofilm)))
        ]

    for g in range(8):
        for copy in arrivals(g):
            copy.start()

    lane = iota((16, N), 1)
    slot = lane % 8
    low = lane < 64
    outer = (lane < 32) | (lane >= 96)

    def six(k):
        return ((lane - (8 * k + 5)) & 127) < 6

    third_right = jnp.zeros((16, N), F32)
    third_left = jnp.zeros((16, N), F32)
    for g in range(8):
        for copy in arrivals(g):
            copy.wait()
        rows = slice(16 * g, 16 * g + 16)
        sources = jnp.zeros((16, N), F32)
        noises = jnp.zeros((16, N), F32)
        levels = jnp.zeros((16, N), jnp.int32)
        for z in range(16):
            n = noise[z, rows, :]
            both = roll(jnp.where(outer, source[z, rows, :], n), 8 * z + 8, 1)
            sources = jnp.where(six(z), both, sources)
            noises = jnp.where(six((z + 8) % 16), both, noises)
            levels = jnp.where(six(z), roll(biofilm[z, rows, :], 8 * z + 8, 1), levels)
            if z >= 8 and z % 2 == 1:
                even = noise[z - 1, rows, :]
                first = (z - 9) // 2 * N + 16 * g
                to_right[first : first + 16, :] = jnp.where(low, roll(even, 64, 1), n)
                to_left[first : first + 16, :] = jnp.where(low, even, roll(n, 64, 1))
        br = levels.astype(F32)
        bl = roll(br, -8, 1)
        first = 4 * N + 16 * g
        to_right[first : first + 16, :] = jnp.where(
            slot < 3, roll(noises, -69, 1), jnp.where(slot < 5, roll(br, -3, 1), sources)
        )
        to_left[first : first + 16, :] = jnp.where(
            slot < 3, roll(sources, -8, 1), jnp.where(slot < 5, roll(bl, 3, 1), roll(noises, -67, 1))
        )
        third_right = third_right + roll(jnp.where(slot == 5, br, 0.0), g, 1)
        third_left = third_left + roll(jnp.where(slot == 2, bl, 0.0), g, 1)
    to_right[5 * N :, :] = third_right
    to_left[5 * N :, :] = third_left


def column_weights():
    m = iota((N, 2 * N), 0)
    o = iota((N, 2 * N), 1)
    s = o - N
    own = ((o < N) & (m - o <= R) & (o - m <= R)) | ((o >= N) & (s <= 2) & (m >= s + 64)) | (
        (s >= 5) & (s <= 7) & (m <= s + 56)
    )
    lane = iota((N, 3 * N), 0)
    o = iota((N, 3 * N), 1)
    half = lane // 64
    m = lane % 64
    e = o - 2 * N
    same = (o < 2 * N) & (o // N == half)
    edge = (e >= 0) & (e < 16) & (e // 8 == half)
    left = (same & (m >= o % N)) | (edge & (o % 8 >= 5))
    right = (same & (m + 64 <= o % N)) | (edge & (o % 8 <= 2))
    a = iota((N, N), 0)
    b = iota((N, N), 1)
    together = a // 8 == b // 8
    t = a % 8
    s = b % 8
    left_extra = together & (t <= 2) & (s >= 5) & (t >= s - 5)
    right_extra = together & (t >= 5) & (s <= 2) & (t - 5 <= s)
    return [weights(w) for w in (own, left, right, left_extra, right_extra)]


def column_sums_own(noise, biofilm, own_middle, own_edge, factor):
    own = column_weights()[0]
    twice = jnp.concatenate([own, own], axis=0)
    total = jnp.zeros((N, N), F32)
    for z in range(16):
        out = dot(jnp.concatenate(split2(noise[z]), axis=1), twice)
        own_middle[z] = out[:, :N]
        total = total + roll(out[:, N:], 8 * z, 1)
        factor[z] = resistance_factor(biofilm[z].astype(F32))
    own_edge[...] = total


def sums_beside(x, y, w):
    high, low = split2(jnp.concatenate([x, y], axis=1))
    return dot(high, w) + dot(low, w)


def on_even():
    return lax.axis_index("gx") % 2 == 0


class Chosen:
    def __init__(self, first, a, b):
        self.first, self.a, self.b = first, a, b

    def __getitem__(self, index):
        return jnp.where(self.first, self.a[index], self.b[index])


def half_columns(first_layer, own_middle, from_left, from_right, middle):
    _, left, right, _, _ = column_weights()
    both = jnp.concatenate([left, right], axis=0)
    total = jnp.zeros((N, N), F32)
    for q in range(4):
        rows = slice(q * N, q * N + N)
        halo = sums_beside(from_left[rows, :], from_right[rows, :], both)
        total = total + roll(halo[:, 2 * N :], 8 * first_layer + 16 * q, 1)
        for k in (0, 1):
            z = 2 * q + k
            middle[z] = own_middle[first_layer + z] + halo[:, k * N : k * N + N]
    return total


def fill_messages(sums, sources, levels, tail, outer, inner):
    def fill(to_down, to_up):
        for z in range(len(sums)):
            to_down[z * 72 : z * 72 + 72, :] = sums[z][56:128, :]
            to_up[z * 72 : z * 72 + 72, :] = sums[z][0:72, :]
        for z, (s, b) in enumerate(zip(sources, levels)):
            to_down[z * 72 : z * 72 + 3, :] = s[125:128, :]
            to_down[z * 72 + 3 : z * 72 + 5, :] = b[126:128, :].astype(F32)
            to_down[tail + z : tail + z + 1, :] = b[125:126, :].astype(F32)
            to_up[z * 72 + 67 : z * 72 + 70, :] = s[0:3, :]
            to_up[z * 72 + 70 : z * 72 + 72, :] = b[0:2, :].astype(F32)
            to_up[tail + z : tail + z + 1, :] = b[2:3, :].astype(F32)

    even = on_even()

    @pl.when(even)
    def _():
        fill(inner, outer)

    @pl.when(jnp.logical_not(even))
    def _():
        fill(outer, inner)


def columns_first(own_middle, source, biofilm, from_left, from_right, middle, edge, outer, inner):
    edge[...] = half_columns(0, own_middle, from_left, from_right, middle)
    planes = [[ref.at[z] for z in range(8)] for ref in (middle, source, biofilm)]
    fill_messages(*planes, 8 * 72, outer, inner)


def columns_second(
    own_middle, own_edge, first_edge, source, biofilm, from_left, from_right,
    middle, edge, edge_source, edge_biofilm, outer, inner,
):
    _, _, _, left_extra, right_extra = column_weights()
    slot = iota((N, N), 1) % 8
    extra_left = from_left[4 * N : 5 * N, :]
    extra_right = from_right[4 * N : 5 * N, :]
    total = own_edge[...] + first_edge[...]
    total = total + sums_beside(extra_left, extra_right, jnp.concatenate([left_extra, right_extra], axis=0))
    edge[...] = total + half_columns(8, own_middle, from_left, from_right, middle)

    edge_source[...] = jnp.where(slot >= 5, extra_left, jnp.where(slot <= 2, extra_right, 0.0))
    third_left = from_left[5 * N :, :]
    third_right = from_right[5 * N :, :]
    levels = jnp.where(slot >= 6, roll(extra_left, 3, 1), jnp.where(slot <= 1, roll(extra_right, -3, 1), 0.0))
    slot16 = iota((16, N), 1) % 8
    for g in range(8):
        rows = slice(16 * g, 16 * g + 16)
        edge_biofilm[rows, :] = jnp.where(
            slot16 == 5, roll(third_left, -g, 1), jnp.where(slot16 == 2, roll(third_right, -g, 1), levels[rows, :])
        )

    outer[9 * 72 :, :] = jnp.zeros((16, N), F32)
    inner[9 * 72 :, :] = jnp.zeros((16, N), F32)
    planes = [[ref.at[8 + z] for z in range(8)] for ref in (source, biofilm)]
    fill_messages(
        [middle.at[z] for z in range(8)] + [edge],
        planes[0] + [edge_source],
        planes[1] + [edge_biofilm],
        9 * 72,
        outer,
        inner,
    )


def row_weights():
    r = iota((144, N), 0) - 8
    m = iota((144, N), 1)
    inside = (r >= -3) & (r <= 130)
    own = inside & (m >= r - R) & (m <= r + R)
    halo = inside & (((m < 64) & (m >= r)) | ((m >= 64) & (m <= r)))
    return weights(own), weights(halo)


def row_sums(band, *planes):
    columns = [jnp.concatenate(split2(p), axis=0) for p in planes]
    out = dot(jnp.concatenate([band, band], axis=1), jnp.concatenate(columns, axis=1))
    return [out[:, k * N : k * N + N] for k in range(len(planes))]


def halo_rows(from_up, from_down, z):
    first = pl.multiple_of(z * 72, 8)
    return jnp.concatenate([from_up[pl.ds(first + 8, 64), :], from_down[pl.ds(first, 64), :]], axis=0)


def finish_sums(from_up, from_down, z, sums, out, lanes=None):
    row8 = iota((8, N), 0)
    row144 = iota((144, N), 0)
    first = pl.multiple_of(z * 72, 8)
    above = jnp.where(row8 >= 5, from_up[pl.ds(first, 8), :], 0.0)
    below = jnp.where(row8 <= 2, from_down[pl.ds(first + 64, 8), :], 0.0)
    above = jnp.where(row8 >= 5, above + roll(above, 7, 0) + roll(above, 6, 0), 0.0)
    below = jnp.where(row8 <= 2, below + roll(below, 1, 0) + roll(below, 2, 0), 0.0)
    total = jnp.concatenate([sums[:8] + above, sums[8:136], sums[136:] + below], axis=0) * (1.0 / WIDTH)
    out[...] = total
    real = (row144 >= 5) & (row144 <= 138)
    if lanes is not None:
        real = real & lanes
    return jnp.max(jnp.where(real, total, -HUGE).reshape(18, 8, N), axis=0)


def rows_first(middle, outer, inner, logperm, largest):
    even = on_even()
    from_up, from_down = Chosen(even, outer, inner), Chosen(even, inner, outer)
    own, halo = row_weights()
    most = jnp.full((8, N), -HUGE, F32)
    for z in range(0, 8, 2):
        near = row_sums(own, middle[z], middle[z + 1])
        far = row_sums(halo, *[halo_rows(from_up, from_down, z + i) for i in (0, 1)])
        for i in (0, 1):
            most = jnp.maximum(most, finish_sums(from_up, from_down, z + i, near[i] + far[i], logperm.at[z + i]))
    largest[...] = most


def row_sums_own(middle, edge, edge_biofilm, partial, factor):
    own, _ = row_weights()
    for z in range(0, 8, 2):
        partial[z], partial[z + 1] = row_sums(own, middle[z], middle[z + 1])
    partial[8] = row_sums(own, edge[...])[0]
    factor[...] = resistance_factor(edge_biofilm[...])


def resistance_factor(biofilm):
    open_part = 1.0 - 0.06 * biofilm
    solid = (1.0 - 0.35 * open_part) * (1.0 / (1.0 - 0.35))
    return (0.5 * solid * solid) / (open_part * open_part * open_part)


def resistance(logperm, factor, top):
    return jnp.minimum(jnp.exp(top - logperm) * factor, HUGE)


def reciprocal(x):
    guess = pl.reciprocal(x, approx=True)
    return guess * (2.0 - x * guess)


WIDE = tuple((start, C2) for start in range(8, 152, C2))
OWN_ROWS = tuple((start, C3) for start in range(16, 144, C3))


def operate_powers(
    logperm1, largest1, partial, factor, edge_factor, edge_source, source, outer1, inner1, outer2, inner2,
    power1, power2, power3, table,
    resist, across_x, across_y, across_z, flow, field0, field1, field2, field3, logperm2, plane_resist, plane_field,
    side_resist, side_x, side_y, side_z, side0, side1, side2, side_flux, done,
):
    lane = iota((8, N), 1)
    row8 = iota((8, N), 0)

    even = on_even()
    from_up1, from_down1 = Chosen(even, outer1, inner1), Chosen(even, inner1, outer1)
    from_up2, from_down2 = Chosen(even, outer2, inner2), Chosen(even, inner2, outer2)

    _, halo = row_weights()
    edge_lane = (iota((144, N), 1) % 8 <= 2) | (iota((144, N), 1) % 8 >= 5)
    second = (from_up2, from_down2)
    largest = largest1[...]
    for z in (0, 2, 4, 6):
        pair = row_sums(halo, halo_rows(*second, z), halo_rows(*second, z + 1))
        for i in (0, 1):
            sums = partial[z + i] + pair[i]
            largest = jnp.maximum(largest, finish_sums(*second, z + i, sums, logperm2.at[z + i]))
    sums = partial[8] + row_sums(halo, halo_rows(*second, 8))[0]
    largest = jnp.maximum(largest, finish_sums(*second, 8, sums, logperm2.at[8], edge_lane))
    top = jnp.max(jnp.max(largest, axis=0, keepdims=True), axis=1, keepdims=True)
    top = jnp.maximum(top, -60.0)

    def halo_tiles(half, z):
        from_up, from_down, tail = half
        first = pl.multiple_of(z * 72, 8)
        above = from_up[pl.ds(first, 8), :]
        below = from_down[pl.ds(first + 64, 8), :]
        third_above = from_up[pl.ds(tail + z, 1), :]
        third_below = from_down[pl.ds(tail + z, 1), :]
        source_above = jnp.where(row8 >= 5, roll(above, 5, 0), 0.0)
        source_below = jnp.where(row8 <= 2, roll(below, 5, 0), 0.0)
        biofilm_above = jnp.where(row8 == 5, third_above, jnp.where(row8 >= 6, roll(above, 3, 0), 0.0))
        biofilm_below = jnp.where(row8 == 2, third_below, jnp.where(row8 <= 1, roll(below, 2, 0), 0.0))
        return source_above, source_below, biofilm_above, biofilm_below

    first_half = (from_up1, from_down1, 8 * 72)
    second_half = (from_up2, from_down2, 9 * 72)

    def prepare(half, z, logperm, out, field, own_source, own_factor):
        source_above, source_below, biofilm_above, biofilm_below = halo_tiles(half, z)
        field[8:16, :] = source_above
        field[16:144, :] = own_source
        field[144:152, :] = source_below
        out[8:16, :] = jnp.where(row8 >= 5, resistance(logperm[0:8, :], resistance_factor(biofilm_above), top), HUGE)
        out[144:152, :] = jnp.where(row8 <= 2, resistance(logperm[136:144, :], resistance_factor(biofilm_below), top), HUGE)
        out[16:144, :] = resistance(logperm[8:136, :], own_factor, top)
        empty = jnp.full((8, N), HUGE, F32)
        none = jnp.zeros((8, N), F32)
        out[0:8, :] = empty
        out[152:160, :] = empty
        field[0:8, :] = none
        field[152:160, :] = none

    prepare(second_half, 8, logperm2.at[8], plane_resist, plane_field, edge_source[...], edge_factor[...])
    for base, half, logperm in ((0, first_half, logperm1), (8, second_half, logperm2)):

        def prepare_layer(k, carry, base=base, half=half, logperm=logperm):
            z = base + k
            prepare(half, k, logperm.at[k], resist.at[z], field0.at[z], source[z], factor[z])
            none = jnp.zeros((8, N), F32)
            for ref in (field1, field2, across_x):
                ref[z, 0:8, :] = none
                ref[z, 152:160, :] = none
            return carry

        lax.fori_loop(0, 8, prepare_layer, 0, unroll=U6)

    a = iota((N, 2 * N), 0)
    o = iota((N, 2 * N), 1)
    t = o % 16
    spread = weights(
        (a // 8 == o // 16)
        & (((t >= 3) & (t <= 5) & (a % 8 == t - 3)) | ((t >= 10) & (t <= 12) & (a % 8 == t - 5)))
    )
    lane160 = iota((ROWS, N), 1)
    slot160 = lane160 % 16
    for plane, field, side, fill in ((plane_resist, resist, side_resist, HUGE), (plane_field, field0, side0, 0.0)):
        high, mid, low = split3(plane[...])
        outer = dot(high, spread) + dot(mid, spread) + dot(low, spread)
        for p in range(2):
            inner = jnp.zeros((ROWS, N), F32)
            for k in range(8):
                inner = jnp.where(lane160 // 16 == k, roll(field[8 * p + k], 16 * k + 3, 1), inner)
            value = jnp.where(slot160 <= 2, inner, jnp.where(slot160 >= 13, roll(inner, 10, 1), outer[:, p * N : p * N + N]))
            side[p] = jnp.where((slot160 <= 5) | (slot160 >= 10), value, fill)
    none = jnp.zeros((8, N), F32)
    for p in range(2):
        for ref in (side1, side2, side_x):
            ref[p, 0:8, :] = none
            ref[p, 152:160, :] = none

    def next_layer(first, second):
        lanes = iota(first.shape, 1)
        return jnp.where(lanes < 112, roll(first, -16, 1), roll(second, -16, 1)), roll(second, -16, 1)

    def last_layer(first, second):
        lanes = iota(first.shape, 1)
        return (
            jnp.where(lanes >= 16, roll(first, 16, 1), 0.0),
            jnp.where(lanes >= 16, roll(second, 16, 1), roll(first, 16, 1)),
        )

    for start, size in WIDE:
        rows = slice(start, start + size)
        here = [side_resist[p, rows, :] for p in range(2)]
        after = next_layer(*here)
        for p in range(2):
            side_x[p, rows, :] = reciprocal(here[p] + side_resist[p, start - 1 : start - 1 + size, :])
            side_y[p, rows, :] = reciprocal(here[p] + roll(here[p], 1, 1))
            value = reciprocal(here[p] + after[p])
            side_z[p, rows, :] = value if p == 0 else jnp.where(iota((size, N), 1) < 112, value, 0.0)

    def faces(z, carry):
        for start, size in WIDE:
            rows = slice(start, start + size)
            here = resist[z, rows, :]
            across_x[z, rows, :] = reciprocal(here + resist[z, start - 1 : start - 1 + size, :])
            across_y[z, rows, :] = jnp.where(iota((size, N), 1) == 0, 0.0, reciprocal(here + roll(here, 1, 1)))
            above = resist[jnp.maximum(z - 1, 0), rows, :]
            across_z[z, rows, :] = jnp.where(z > 0, reciprocal(here + above), 0.0)
        return carry

    lax.fori_loop(0, 16, faces, 0, unroll=U5)
    across_z[16] = jnp.zeros((ROWS, N), F32)

    def apply_sides(field, image):
        for start, size in WIDE:
            rows = slice(start, start + size)
            slot = iota((size, N), 1) % 16
            here = [field[p, rows, :] for p in range(2)]
            inward = [side_y[p, rows, :] * (here[p] - roll(here[p], 1, 1)) for p in range(2)]
            for p in range(2):
                side_flux[p, rows, :] = jnp.where(slot == 13, inward[p], -roll(inward[p], 9, 1))
            if image is None:
                continue
            after = next_layer(*here)
            through = [side_z[p, rows, :] * (after[p] - here[p]) for p in range(2)]
            back = last_layer(*through)
            for p in range(2):
                value = inward[p] - roll(inward[p], -1, 1) - through[p] + back[p]
                value = value + side_x[p, rows, :] * (here[p] - field[p, start - 1 : start - 1 + size, :])
                value = value - side_x[p, start + 1 : start + 1 + size, :] * (
                    field[p, start + 1 : start + 1 + size, :] - here[p]
                )
                image[p, rows, :] = value

    def flow_along_y(field):
        def layer(z, carry):
            for start, size in WIDE:
                rows = slice(start, start + size)
                here = field[z, rows, :]
                flow[z, rows, :] = across_y[z, rows, :] * (here - roll(here, 1, 1))
            return carry

        lax.fori_loop(0, 16, layer, 0, unroll=U1)

    def apply_layers(field, first, count, start, size):
        rows = slice(start, start + size)
        lanes = iota((size, N), 1)
        ends = (lanes == 0) | (lanes == 127)
        here = field[first, rows, :]
        from_last = across_z[first, rows, :] * (here - field[jnp.maximum(first - 1, 0), rows, :])
        for k in range(count):
            z = first + k
            after = field[jnp.minimum(z + 1, 15) if k == count - 1 else z + 1, rows, :]
            to_next = across_z[z + 1, rows, :] * (after - here)
            inward = flow[z, rows, :]
            beside = roll(side_flux[z // 8, rows, :], 115 - 16 * (z % 8), 1)
            value = inward - roll(inward, -1, 1) + jnp.where(ends, beside, 0.0)
            value = value + across_x[z, rows, :] * (here - field[z, start - 1 : start - 1 + size, :])
            value = value - across_x[z, start + 1 : start + 1 + size, :] * (
                field[z, start + 1 : start + 1 + size, :] - here
            )
            yield z, here, value + from_last - to_next
            here, from_last = after, to_next

    def apply(field, image):
        flow_along_y(field)

        def layers(k, carry):
            for start, size in WIDE:
                for z, _, value in apply_layers(field, k * U2, U2, start, size):
                    image[z, start : start + size, :] = value
            return carry

        lax.fori_loop(0, 16 // U2, layers, 0, unroll=V2)

    def hand_out(field, power, k):
        return pltpu.make_async_copy(field.at[:, 16:144, :], power, done.at[k])

    apply_sides(side0, side1)
    apply(field0, field1)
    hand_out(field1, power1, 0).start()
    apply_sides(side1, side2)
    apply(field1, field2)
    hand_out(field2, power2, 1).start()
    apply_sides(side2, None)
    flow_along_y(field2)

    def last(k, sums):
        for start, size in OWN_ROWS:
            rows = slice(start, start + size)
            for z, f2, f3 in apply_layers(field2, k * U3, U3, start, size):
                field3[z, start - 16 : start - 16 + size, :] = f3
                f0 = field0[z, rows, :]
                f1 = field1[z, rows, :]
                terms = (f0 * f0, f0 * f1, f1 * f1, f1 * f2, f2 * f2, f2 * f3)
                sums = tuple(s + jnp.sum(t.reshape(size // 8, 8, N), axis=0) for s, t in zip(sums, terms))
        part = pl.ds(k * U3, U3)
        pltpu.make_async_copy(field3.at[part], power3.at[part], done.at[2]).start()
        return sums

    sums = lax.fori_loop(0, 16 // U3, last, tuple(jnp.zeros((8, N), F32) for _ in range(6)), unroll=V3)
    line = jnp.where((lane[:1] >= 8) & (lane[:1] < 16), top, 0.0)
    for k, s in enumerate(sums):
        amount = jnp.sum(jnp.sum(s, axis=0, keepdims=True), axis=1, keepdims=True)
        line = jnp.where(lane[:1] == k, amount, line)
    table[...] = jnp.broadcast_to(line, table.shape)
    hand_out(field1, power1, 0).wait()
    hand_out(field2, power2, 1).wait()
    pltpu.make_async_copy(field3, power3, done.at[2]).wait()


def coefficients(everyone, own):
    n = everyone.shape[0]
    rows = everyone[...]
    lane = iota((n, N), 1)
    tops = jnp.where(lane < 8, roll(rows, -8, 1), 0.0)
    top = jnp.max(tops, axis=0, keepdims=True)
    top = jnp.max(jnp.where(lane[:1] == 0, top, -HUGE), axis=1, keepdims=True)
    factor = jnp.exp((tops - top) * lane.astype(F32))
    moments = jnp.sum(jnp.where(lane < 6, rows * factor, 0.0), axis=0, keepdims=True)
    u0, u1, u2, u3, u4, u5 = [
        jnp.sum(jnp.where(lane[:1] == k, moments, 0.0), axis=1, keepdims=True) for k in range(6)
    ]
    own_top = jnp.sum(jnp.where(lane[:1] == 8, own[0:1, :], 0.0), axis=1, keepdims=True)
    ratio = jnp.exp(own_top - top)

    def over(a, b):
        return jnp.where(b > 0.0, a / jnp.where(b > 0.0, b, 1.0), 0.0)

    l10 = over(u1, u0)
    l20 = over(u2, u0)
    d1 = u2 - l10 * u1
    s12 = u3 - l10 * u2
    l21 = over(s12, d1)
    d2 = (u4 - l20 * u2) - l21 * s12
    y1 = u4 - l10 * u3
    y2 = u5 - l20 * u3 - l21 * y1
    e2 = -over(y2, d2)
    e1 = -over(y1, d1) - l21 * e2
    e0 = -over(u3, u0) - l10 * e1 - l20 * e2

    sigma = jnp.exp(top)
    tau = jnp.minimum(1.0, 2.0 * sigma)
    kappa = jnp.minimum(1.0, 0.5 / sigma)
    at_zero = ((e0 * tau - e1 * kappa) * tau + e2 * kappa * kappa) * tau - kappa * kappa * kappa
    r_scale = tau * tau * tau / at_zero
    p_scale = -jnp.minimum(1.0 / sigma, 2.0) / at_zero
    q1 = tau * e2 - kappa
    r0 = r_scale * e0
    r1 = r_scale * e1 * ratio
    r2 = r_scale * e2 * ratio * ratio
    r3 = r_scale * ratio * ratio * ratio
    p0 = p_scale * (tau * tau * e1 - kappa * q1)
    p1 = p_scale * (tau * q1) * ratio
    p2 = p_scale * (tau * tau) * ratio * ratio
    return p0, p1, p2, r0, r1, r2, r3


def combine(
    everyone, own, source_in, power1_in, power2_in, power3_in, pressure_out, residual_out,
    source, power1, power2, power3, pressure, residual, arrived, left,
):
    def arrivals(g):
        part = slice(4 * g, 4 * g + 4)
        pairs = ((source_in, source), (power1_in, power1), (power2_in, power2), (power3_in, power3))
        return [
            pltpu.make_async_copy(far.at[part], near.at[part], arrived.at[k, g]) for k, (far, near) in enumerate(pairs)
        ]

    def departures(g):
        part = slice(4 * g, 4 * g + 4)
        return [
            pltpu.make_async_copy(near.at[part], far.at[part], left.at[k, g])
            for k, (near, far) in enumerate(((pressure, pressure_out), (residual, residual_out)))
        ]

    for g in range(4):
        for copy in arrivals(g):
            copy.start()
    p0, p1, p2, r0, r1, r2, r3 = coefficients(everyone, own)
    for g in range(4):
        for copy in arrivals(g):
            copy.wait()
        for z in range(4 * g, 4 * g + 4):
            f0 = source[z]
            f1 = power1[z]
            f2 = power2[z]
            pressure[z] = p0 * f0 + p1 * f1 + p2 * f2
            residual[z] = (r0 * f0 + r1 * f1) + (r2 * f2 + r3 * power3[z])
        for copy in departures(g):
            copy.start()
    for g in range(4):
        for copy in departures(g):
            copy.wait()


def vmem(count):
    return [pl.BlockSpec(memory_space=pltpu.VMEM)] * count


def shape(*dims):
    return jax.ShapeDtypeStruct(dims, F32)


def hbm(count):
    return [pl.BlockSpec(memory_space=pltpu.HBM)] * count


def in_hbm(x):
    return pltpu.with_memory_space_constraint(x, pltpu.HBM)


def call(body, inputs, out, out_specs, scratch=(), name=None, cost=1e6):
    return pl.pallas_call(
        body,
        out_shape=out,
        in_specs=inputs,
        out_specs=out_specs,
        scratch_shapes=list(scratch),
        compiler_params=pltpu.CompilerParams(vmem_limit_bytes=40 * 1024 * 1024),
        cost_estimate=pl.CostEstimate(flops=int(cost), bytes_accessed=int(cost), transcendentals=0),
        name=name,
    )


def exchange(to_next, to_previous, axis):
    count = lax.axis_size(axis)
    forward = [(i, (i + 1) % count) for i in range(count)]
    backward = [(target, source) for source, target in forward]
    return lax.ppermute(to_next, axis, forward), lax.ppermute(to_previous, axis, backward)


def exchange_pairs(outer, inner, axis):
    count = lax.axis_size(axis)
    across = [(i, (i + 1 if i % 2 else i - 1) % count) for i in range(count)]
    return lax.ppermute(outer, axis, across), lax.ppermute(inner, axis, [(i, i ^ 1) for i in range(count)])


def local(noise, biofilm, source):
    block = pltpu.VMEM((NZ, N, N), F32)
    to_right, to_left = call(
        pack_first,
        hbm(1),
        [shape(Y_ROWS[0], N)] * 2,
        vmem(2),
        [pltpu.VMEM((8, N, N), F32), pltpu.SemaphoreType.DMA((4,))],
        name="pack_first",
    )(in_hbm(noise))
    beside1 = exchange(to_right, to_left, "gy")
    to_right, to_left = call(
        pack_second,
        vmem(1) + hbm(2),
        [shape(Y_ROWS[1], N)] * 2,
        vmem(2),
        [block, pltpu.VMEM((NZ, N, N), jnp.int32), pltpu.SemaphoreType.DMA((2, 8))],
        name="pack_second",
        cost=2e10,
    )(noise, in_hbm(source), in_hbm(biofilm))
    beside2 = exchange(to_right, to_left, "gy")
    own_middle, own_edge, factor = call(
        column_sums_own,
        vmem(2),
        [shape(NZ, N, N), shape(N, N), shape(NZ, N, N)],
        vmem(3),
        name="columns_own",
        cost=2e10,
    )(noise, biofilm)
    middle1, first_edge, outer, inner = call(
        columns_first,
        vmem(5),
        [shape(8, N, N), shape(N, N)] + [shape(X_ROWS[0], N)] * 2,
        vmem(4),
        name="columns_first",
    )(own_middle, source, biofilm, *beside1)
    above_below1 = exchange_pairs(outer, inner, "gx")
    middle2, edge, edge_source, edge_biofilm, outer, inner = call(
        columns_second,
        vmem(7),
        [shape(8, N, N), shape(N, N), shape(N, N), shape(N, N)] + [shape(X_ROWS[1], N)] * 2,
        vmem(6),
        name="columns_second",
        cost=2e10,
    )(own_middle, own_edge, first_edge, source, biofilm, *beside2)
    above_below2 = exchange_pairs(outer, inner, "gx")
    partial, edge_factor = call(
        row_sums_own,
        vmem(3),
        [shape(9, 144, N), shape(N, N)],
        vmem(2),
        name="rows_own",
        cost=1,
    )(middle2, edge, edge_biofilm)
    logperm1, largest1 = call(
        rows_first,
        vmem(3),
        [shape(8, 144, N), shape(8, N)],
        vmem(2),
        name="rows_first",
        cost=2e10,
    )(middle1, *above_below1)
    devices = lax.axis_size("gx") * lax.axis_size("gy")
    layers = pltpu.VMEM((NZ, ROWS, N), F32)
    plane = pltpu.VMEM((ROWS, N), F32)
    sides = pltpu.VMEM((2, ROWS, N), F32)
    power1, power2, power3, table = call(
        operate_powers,
        vmem(11),
        [pltpu.HBM((NZ, N, N), F32)] * 3 + [shape(devices, N)],
        hbm(3) + vmem(1),
        [layers] * 3
        + [pltpu.VMEM((NZ + 1, ROWS, N), F32)]
        + [layers] * 4
        + [block, pltpu.VMEM((9, 144, N), F32), plane, plane]
        + [sides] * 8
        + [pltpu.SemaphoreType.DMA((3,))],
        name="powers",
    )(logperm1, largest1, partial, factor, edge_factor, edge_source, source, *above_below1, *above_below2)
    everyone = lax.all_to_all(table, ("gx", "gy"), 0, 0, tiled=True)
    return tuple(
        call(
            combine,
            vmem(2) + hbm(4),
            [pltpu.HBM((NZ, N, N), F32)] * 2,
            hbm(2),
            [block] * 6 + [pltpu.SemaphoreType.DMA((4, 4)), pltpu.SemaphoreType.DMA((2, 4))],
            name="combine",
        )(everyone, table, *[in_hbm(x) for x in (source, power1, power2, power3)])
    )


def solution(mesh):
    in_specs = (P(None, "gx", "gy"), P(None, "gx", "gy"), P(None, "gx", "gy"))
    out_specs = (P(None, "gx", "gy"), P(None, "gx", "gy"))
    return jax.shard_map(local, mesh=mesh, in_specs=in_specs, out_specs=out_specs, check_vma=False)
```

```python
import jax
import jax.numpy as jnp
from jax import lax
from jax.experimental import pallas as pl
from jax.experimental.pallas import tpu as pltpu
from jax.sharding import PartitionSpec as P

R = 64
WIDTH = 2 * R + 1
NZ = 16
N = 128
F32 = jnp.float32
BF16 = jnp.bfloat16

H = 10
G = NZ - H
Y_ROWS = (H // 2 * N, G // 2 * N + N + 16)
X_TAIL = (H * 72, (G + 1) * 72)
X_ROWS = (X_TAIL[0] + (H + 7) // 8 * 8, X_TAIL[1] + (G + 8) // 8 * 8)
ROWS = 160
OWN = 16
HUGE = 1e30
U1, U2, U3, U5 = 16, 4, 4, 16
V2, V3 = 4, 1
C2, C3 = 144, 64


def iota(shape, dim):
    return lax.broadcasted_iota(jnp.int32, shape, dim)


def roll(x, shift, axis):
    if isinstance(shift, int):
        shift = shift % x.shape[axis]
        if shift == 0:
            return x
    return pltpu.roll(x, shift, axis)


def split3(x):
    high = x.astype(BF16)
    rest = x - high.astype(F32)
    middle = rest.astype(BF16)
    low = (rest - middle.astype(F32)).astype(BF16)
    return high, middle, low


def split2(x):
    high = x.astype(BF16)
    return high, (x - high.astype(F32)).astype(BF16)


def dot(a, b):
    return lax.dot_general(a, b, (((1,), (0,)), ((), ())), preferred_element_type=F32)


def weights(mask):
    return jnp.where(mask, 1.0, 0.0).astype(BF16)


def pack_first(noise_in, to_right, to_left, noise, arrived):
    low = iota((N, N), 1) < 64
    copies = [
        pltpu.make_async_copy(noise_in.at[2 * q : 2 * q + 2], noise.at[2 * q : 2 * q + 2], arrived.at[q])
        for q in range(H // 2)
    ]
    for copy in copies:
        copy.start()
    for q in range(H // 2):
        copies[q].wait()
        even = noise[2 * q]
        odd = noise[2 * q + 1]
        to_right[q * N : q * N + N, :] = jnp.where(low, roll(even, 64, 1), odd)
        to_left[q * N : q * N + N, :] = jnp.where(low, even, roll(odd, 64, 1))


def pack_second(after, noise, source_in, biofilm_in, to_right, to_left, source, biofilm, arrived):
    def arrivals(g):
        rows = slice(16 * g, 16 * g + 16)
        return [
            pltpu.make_async_copy(far.at[:, rows, :], near.at[:, rows, :], arrived.at[k, g])
            for k, (far, near) in enumerate(((source_in, source), (biofilm_in, biofilm)))
        ]

    del after
    for g in range(8):
        for copy in arrivals(g):
            copy.start()

    lane = iota((16, N), 1)
    slot = lane % 8
    low = lane < 64
    outer = (lane < 32) | (lane >= 96)

    def six(k):
        return ((lane - (8 * k + 5)) & 127) < 6

    third_right = jnp.zeros((16, N), F32)
    third_left = jnp.zeros((16, N), F32)
    for g in range(8):
        for copy in arrivals(g):
            copy.wait()
        rows = slice(16 * g, 16 * g + 16)
        sources = jnp.zeros((16, N), F32)
        noises = jnp.zeros((16, N), F32)
        levels = jnp.zeros((16, N), jnp.int32)
        for z in range(16):
            n = noise[z, rows, :]
            both = roll(jnp.where(outer, source[z, rows, :], n), 8 * z + 8, 1)
            sources = jnp.where(six(z), both, sources)
            noises = jnp.where(six((z + 8) % 16), both, noises)
            levels = jnp.where(six(z), roll(biofilm[z, rows, :], 8 * z + 8, 1), levels)
            if z >= H and z % 2 == 1:
                even = noise[z - 1, rows, :]
                first = (z - 1 - H) // 2 * N + 16 * g
                to_right[first : first + 16, :] = jnp.where(low, roll(even, 64, 1), n)
                to_left[first : first + 16, :] = jnp.where(low, even, roll(n, 64, 1))
        br = levels.astype(F32)
        bl = roll(br, -8, 1)
        first = G // 2 * N + 16 * g
        to_right[first : first + 16, :] = jnp.where(
            slot < 3, roll(noises, -69, 1), jnp.where(slot < 5, roll(br, -3, 1), sources)
        )
        to_left[first : first + 16, :] = jnp.where(
            slot < 3, roll(sources, -8, 1), jnp.where(slot < 5, roll(bl, 3, 1), roll(noises, -67, 1))
        )
        third_right = third_right + roll(jnp.where(slot == 5, br, 0.0), g, 1)
        third_left = third_left + roll(jnp.where(slot == 2, bl, 0.0), g, 1)
    to_right[G // 2 * N + N :, :] = third_right
    to_left[G // 2 * N + N :, :] = third_left


def column_weights():
    m = iota((N, 2 * N), 0)
    o = iota((N, 2 * N), 1)
    s = o - N
    own = ((o < N) & (m - o <= R) & (o - m <= R)) | ((o >= N) & (s <= 2) & (m >= s + 64)) | (
        (s >= 5) & (s <= 7) & (m <= s + 56)
    )
    lane = iota((N, 3 * N), 0)
    o = iota((N, 3 * N), 1)
    half = lane // 64
    m = lane % 64
    e = o - 2 * N
    same = (o < 2 * N) & (o // N == half)
    edge = (e >= 0) & (e < 16) & (e // 8 == half)
    left = (same & (m >= o % N)) | (edge & (o % 8 >= 5))
    right = (same & (m + 64 <= o % N)) | (edge & (o % 8 <= 2))
    a = iota((N, N), 0)
    b = iota((N, N), 1)
    together = a // 8 == b // 8
    t = a % 8
    s = b % 8
    left_extra = together & (t <= 2) & (s >= 5) & (t >= s - 5)
    right_extra = together & (t >= 5) & (s <= 2) & (t - 5 <= s)
    return [weights(w) for w in (own, left, right, left_extra, right_extra)]


def column_sums_own(noise, biofilm, own_middle, own_edge, factor):
    own = column_weights()[0]
    twice = jnp.concatenate([own, own], axis=0)
    total = jnp.zeros((N, N), F32)
    for z in range(16):
        out = dot(jnp.concatenate(split2(noise[z]), axis=1), twice)
        own_middle[z] = out[:, :N]
        total = total + roll(out[:, N:], 8 * z, 1)
        factor[z] = resistance_factor(biofilm[z].astype(F32))
    own_edge[...] = total


def sums_beside(x, y, w):
    high, low = split2(jnp.concatenate([x, y], axis=1))
    return dot(high, w) + dot(low, w)


def on_even():
    return lax.axis_index("gx") % 2 == 0


class Chosen:
    def __init__(self, first, a, b):
        self.first, self.a, self.b = first, a, b

    def __getitem__(self, index):
        return jnp.where(self.first, self.a[index], self.b[index])


def part_columns(first_layer, count, own_middle, from_left, from_right, middle):
    _, left, right, _, _ = column_weights()
    both = jnp.concatenate([left, right], axis=0)
    total = jnp.zeros((N, N), F32)
    for q in range(count // 2):
        rows = slice(q * N, q * N + N)
        halo = sums_beside(from_left[rows, :], from_right[rows, :], both)
        total = total + roll(halo[:, 2 * N :], 8 * first_layer + 16 * q, 1)
        for k in (0, 1):
            z = 2 * q + k
            middle[z] = own_middle[first_layer + z] + halo[:, k * N : k * N + N]
    return total


def fill_messages(sums, sources, levels, tail, outer, inner):
    def fill(to_down, to_up):
        for ref in (to_down, to_up):
            ref[tail:, :] = jnp.zeros((ref.shape[0] - tail, N), F32)
        for z in range(len(sums)):
            to_down[z * 72 : z * 72 + 72, :] = sums[z][56:128, :]
            to_up[z * 72 : z * 72 + 72, :] = sums[z][0:72, :]
        for z, (s, b) in enumerate(zip(sources, levels)):
            to_down[z * 72 : z * 72 + 3, :] = s[125:128, :]
            to_down[z * 72 + 3 : z * 72 + 5, :] = b[126:128, :].astype(F32)
            to_down[tail + z : tail + z + 1, :] = b[125:126, :].astype(F32)
            to_up[z * 72 + 67 : z * 72 + 70, :] = s[0:3, :]
            to_up[z * 72 + 70 : z * 72 + 72, :] = b[0:2, :].astype(F32)
            to_up[tail + z : tail + z + 1, :] = b[2:3, :].astype(F32)

    even = on_even()

    @pl.when(even)
    def _():
        fill(inner, outer)

    @pl.when(jnp.logical_not(even))
    def _():
        fill(outer, inner)


def columns_first(own_middle, source, biofilm, from_left, from_right, middle, edge, outer, inner):
    edge[...] = part_columns(0, H, own_middle, from_left, from_right, middle)
    planes = [[ref.at[z] for z in range(H)] for ref in (middle, source, biofilm)]
    fill_messages(*planes, X_TAIL[0], outer, inner)


def columns_second(
    own_middle, own_edge, first_edge, source, biofilm, from_left, from_right,
    middle, edge, edge_source, edge_biofilm, outer, inner,
):
    _, _, _, left_extra, right_extra = column_weights()
    slot = iota((N, N), 1) % 8
    first = G // 2 * N
    extra_left = from_left[first : first + N, :]
    extra_right = from_right[first : first + N, :]
    total = own_edge[...] + first_edge[...]
    total = total + sums_beside(extra_left, extra_right, jnp.concatenate([left_extra, right_extra], axis=0))
    edge[...] = total + part_columns(H, G, own_middle, from_left, from_right, middle)

    edge_source[...] = jnp.where(slot >= 5, extra_left, jnp.where(slot <= 2, extra_right, 0.0))
    third_left = from_left[first + N :, :]
    third_right = from_right[first + N :, :]
    levels = jnp.where(slot >= 6, roll(extra_left, 3, 1), jnp.where(slot <= 1, roll(extra_right, -3, 1), 0.0))
    slot16 = iota((16, N), 1) % 8
    for g in range(8):
        rows = slice(16 * g, 16 * g + 16)
        edge_biofilm[rows, :] = jnp.where(
            slot16 == 5, roll(third_left, -g, 1), jnp.where(slot16 == 2, roll(third_right, -g, 1), levels[rows, :])
        )

    planes = [[ref.at[H + z] for z in range(G)] for ref in (source, biofilm)]
    fill_messages(
        [middle.at[z] for z in range(G)] + [edge],
        planes[0] + [edge_source],
        planes[1] + [edge_biofilm],
        X_TAIL[1],
        outer,
        inner,
    )


def row_weights():
    r = iota((144, N), 0) - 8
    m = iota((144, N), 1)
    inside = (r >= -3) & (r <= 130)
    own = inside & (m >= r - R) & (m <= r + R)
    halo = inside & (((m < 64) & (m >= r)) | ((m >= 64) & (m <= r)))
    return weights(own), weights(halo)


def row_sums(band, *planes):
    columns = [jnp.concatenate(split2(p), axis=0) for p in planes]
    out = dot(jnp.concatenate([band, band], axis=1), jnp.concatenate(columns, axis=1))
    return [out[:, k * N : k * N + N] for k in range(len(planes))]


def halo_rows(from_up, from_down, z):
    first = pl.multiple_of(z * 72, 8)
    return jnp.concatenate([from_up[pl.ds(first + 8, 64), :], from_down[pl.ds(first, 64), :]], axis=0)


def finish_sums(from_up, from_down, z, sums, out, lanes=None):
    row8 = iota((8, N), 0)
    row144 = iota((144, N), 0)
    first = pl.multiple_of(z * 72, 8)
    above = jnp.where(row8 >= 5, from_up[pl.ds(first, 8), :], 0.0)
    below = jnp.where(row8 <= 2, from_down[pl.ds(first + 64, 8), :], 0.0)
    above = jnp.where(row8 >= 5, above + roll(above, 7, 0) + roll(above, 6, 0), 0.0)
    below = jnp.where(row8 <= 2, below + roll(below, 1, 0) + roll(below, 2, 0), 0.0)
    total = jnp.concatenate([sums[:8] + above, sums[8:136], sums[136:] + below], axis=0) * (1.0 / WIDTH)
    out[...] = total
    real = (row144 >= 5) & (row144 <= 138)
    if lanes is not None:
        real = real & lanes
    return jnp.max(jnp.where(real, total, -HUGE).reshape(18, 8, N), axis=0)


def rows_first(middle, outer, inner, logperm, largest):
    even = on_even()
    from_up, from_down = Chosen(even, outer, inner), Chosen(even, inner, outer)
    own, halo = row_weights()
    most = jnp.full((8, N), -HUGE, F32)
    for z in range(0, H, 2):
        near = row_sums(own, middle[z], middle[z + 1])
        far = row_sums(halo, *[halo_rows(from_up, from_down, z + i) for i in (0, 1)])
        for i in (0, 1):
            most = jnp.maximum(most, finish_sums(from_up, from_down, z + i, near[i] + far[i], logperm.at[z + i]))
    largest[...] = most


def row_sums_own(middle, edge, edge_biofilm, partial, factor):
    own, _ = row_weights()
    for z in range(0, G, 2):
        partial[z], partial[z + 1] = row_sums(own, middle[z], middle[z + 1])
    partial[G] = row_sums(own, edge[...])[0]
    factor[...] = resistance_factor(edge_biofilm[...])


def resistance_factor(biofilm):
    open_part = 1.0 - 0.06 * biofilm
    solid = (1.0 - 0.35 * open_part) * (1.0 / (1.0 - 0.35))
    return (0.5 * solid * solid) / (open_part * open_part * open_part)


def resistance(logperm, factor, top):
    return jnp.minimum(jnp.exp(top - logperm) * factor, HUGE)


def reciprocal(x):
    guess = pl.reciprocal(x, approx=True)
    return guess * (2.0 - x * guess)


WIDE = tuple((start, C2) for start in range(8, 152, C2))
OWN_ROWS = tuple((start, C3) for start in range(16, 144, C3))


def operate_powers(
    logperm1, largest1, partial, factor, edge_factor, edge_source, source, outer1, inner1, outer2, inner2,
    power1, power2, power3, table,
    resist, across_x, across_y, across_z, flow, field0, field1, field2, field3, logperm2, plane_resist, plane_field,
    side_resist, side_x, side_y, side_z, side0, side1, side2, side_flux, done,
):
    lane = iota((8, N), 1)
    row8 = iota((8, N), 0)

    even = on_even()
    from_up1, from_down1 = Chosen(even, outer1, inner1), Chosen(even, inner1, outer1)
    from_up2, from_down2 = Chosen(even, outer2, inner2), Chosen(even, inner2, outer2)

    _, halo = row_weights()
    edge_lane = (iota((144, N), 1) % 8 <= 2) | (iota((144, N), 1) % 8 >= 5)
    second = (from_up2, from_down2)
    largest = largest1[...]
    for z in range(0, G, 2):
        pair = row_sums(halo, halo_rows(*second, z), halo_rows(*second, z + 1))
        for i in (0, 1):
            sums = partial[z + i] + pair[i]
            largest = jnp.maximum(largest, finish_sums(*second, z + i, sums, logperm2.at[z + i]))
    sums = partial[G] + row_sums(halo, halo_rows(*second, G))[0]
    largest = jnp.maximum(largest, finish_sums(*second, G, sums, logperm2.at[G], edge_lane))
    top = jnp.max(jnp.max(largest, axis=0, keepdims=True), axis=1, keepdims=True)
    top = jnp.maximum(top, -60.0)

    def halo_tiles(part, z):
        from_up, from_down, tail = part
        first = pl.multiple_of(z * 72, 8)
        above = from_up[pl.ds(first, 8), :]
        below = from_down[pl.ds(first + 64, 8), :]
        third_above = from_up[pl.ds(tail + z, 1), :]
        third_below = from_down[pl.ds(tail + z, 1), :]
        source_above = jnp.where(row8 >= 5, roll(above, 5, 0), 0.0)
        source_below = jnp.where(row8 <= 2, roll(below, 5, 0), 0.0)
        biofilm_above = jnp.where(row8 == 5, third_above, jnp.where(row8 >= 6, roll(above, 3, 0), 0.0))
        biofilm_below = jnp.where(row8 == 2, third_below, jnp.where(row8 <= 1, roll(below, 2, 0), 0.0))
        return source_above, source_below, biofilm_above, biofilm_below

    first_part = (from_up1, from_down1, X_TAIL[0])
    second_part = (from_up2, from_down2, X_TAIL[1])

    def prepare(part, z, logperm, out, field, own_source, own_factor):
        source_above, source_below, biofilm_above, biofilm_below = halo_tiles(part, z)
        field[8:16, :] = source_above
        field[16:144, :] = own_source
        field[144:152, :] = source_below
        out[8:16, :] = jnp.where(row8 >= 5, resistance(logperm[0:8, :], resistance_factor(biofilm_above), top), HUGE)
        out[144:152, :] = jnp.where(row8 <= 2, resistance(logperm[136:144, :], resistance_factor(biofilm_below), top), HUGE)
        out[16:144, :] = resistance(logperm[8:136, :], own_factor, top)
        empty = jnp.full((8, N), HUGE, F32)
        none = jnp.zeros((8, N), F32)
        out[0:8, :] = empty
        out[152:160, :] = empty
        field[0:8, :] = none
        field[152:160, :] = none

    prepare(second_part, G, logperm2.at[G], plane_resist, plane_field, edge_source[...], edge_factor[...])
    for base, count, part, logperm in ((0, H, first_part, logperm1), (H, G, second_part, logperm2)):

        def prepare_layer(k, carry, base=base, part=part, logperm=logperm):
            z = base + k
            prepare(part, k, logperm.at[k], resist.at[z], field0.at[z], source[z], factor[z])
            none = jnp.zeros((8, N), F32)
            for ref in (field1, field2, across_x):
                ref[z, 0:8, :] = none
                ref[z, 152:160, :] = none
            return carry

        lax.fori_loop(0, count, prepare_layer, 0, unroll=count)

    a = iota((N, 2 * N), 0)
    o = iota((N, 2 * N), 1)
    t = o % 16
    spread = weights(
        (a // 8 == o // 16)
        & (((t >= 3) & (t <= 5) & (a % 8 == t - 3)) | ((t >= 10) & (t <= 12) & (a % 8 == t - 5)))
    )
    lane160 = iota((ROWS, N), 1)
    slot160 = lane160 % 16
    for plane, field, side, fill in ((plane_resist, resist, side_resist, HUGE), (plane_field, field0, side0, 0.0)):
        high, mid, low = split3(plane[...])
        outer = dot(high, spread) + dot(mid, spread) + dot(low, spread)
        for p in range(2):
            inner = jnp.zeros((ROWS, N), F32)
            for k in range(8):
                inner = jnp.where(lane160 // 16 == k, roll(field[8 * p + k], 16 * k + 3, 1), inner)
            value = jnp.where(slot160 <= 2, inner, jnp.where(slot160 >= 13, roll(inner, 10, 1), outer[:, p * N : p * N + N]))
            side[p] = jnp.where((slot160 <= 5) | (slot160 >= 10), value, fill)
    none = jnp.zeros((8, N), F32)
    for p in range(2):
        for ref in (side1, side2, side_x):
            ref[p, 0:8, :] = none
            ref[p, 152:160, :] = none

    def next_layer(first, second):
        lanes = iota(first.shape, 1)
        return jnp.where(lanes < 112, roll(first, -16, 1), roll(second, -16, 1)), roll(second, -16, 1)

    def last_layer(first, second):
        lanes = iota(first.shape, 1)
        return (
            jnp.where(lanes >= 16, roll(first, 16, 1), 0.0),
            jnp.where(lanes >= 16, roll(second, 16, 1), roll(first, 16, 1)),
        )

    for start, size in WIDE:
        rows = slice(start, start + size)
        here = [side_resist[p, rows, :] for p in range(2)]
        after = next_layer(*here)
        for p in range(2):
            side_x[p, rows, :] = reciprocal(here[p] + side_resist[p, start - 1 : start - 1 + size, :])
            side_y[p, rows, :] = reciprocal(here[p] + roll(here[p], 1, 1))
            value = reciprocal(here[p] + after[p])
            side_z[p, rows, :] = value if p == 0 else jnp.where(iota((size, N), 1) < 112, value, 0.0)

    def faces(z, carry):
        for start, size in WIDE:
            rows = slice(start, start + size)
            here = resist[z, rows, :]
            across_x[z, rows, :] = reciprocal(here + resist[z, start - 1 : start - 1 + size, :])
            across_y[z, rows, :] = jnp.where(iota((size, N), 1) == 0, 0.0, reciprocal(here + roll(here, 1, 1)))
            above = resist[jnp.maximum(z - 1, 0), rows, :]
            across_z[z, rows, :] = jnp.where(z > 0, reciprocal(here + above), 0.0)
        return carry

    lax.fori_loop(0, 16, faces, 0, unroll=U5)
    across_z[16] = jnp.zeros((ROWS, N), F32)

    def apply_sides(field, image):
        for start, size in WIDE:
            rows = slice(start, start + size)
            slot = iota((size, N), 1) % 16
            here = [field[p, rows, :] for p in range(2)]
            inward = [side_y[p, rows, :] * (here[p] - roll(here[p], 1, 1)) for p in range(2)]
            for p in range(2):
                side_flux[p, rows, :] = jnp.where(slot == 13, inward[p], -roll(inward[p], 9, 1))
            if image is None:
                continue
            after = next_layer(*here)
            through = [side_z[p, rows, :] * (after[p] - here[p]) for p in range(2)]
            back = last_layer(*through)
            for p in range(2):
                value = inward[p] - roll(inward[p], -1, 1) - through[p] + back[p]
                value = value + side_x[p, rows, :] * (here[p] - field[p, start - 1 : start - 1 + size, :])
                value = value - side_x[p, start + 1 : start + 1 + size, :] * (
                    field[p, start + 1 : start + 1 + size, :] - here[p]
                )
                image[p, rows, :] = value

    def flow_along_y(field):
        def layer(z, carry):
            for start, size in WIDE:
                rows = slice(start, start + size)
                here = field[z, rows, :]
                flow[z, rows, :] = across_y[z, rows, :] * (here - roll(here, 1, 1))
            return carry

        lax.fori_loop(0, 16, layer, 0, unroll=U1)

    def apply_layers(field, first, count, start, size):
        rows = slice(start, start + size)
        lanes = iota((size, N), 1)
        ends = (lanes == 0) | (lanes == 127)
        here = field[first, rows, :]
        from_last = across_z[first, rows, :] * (here - field[jnp.maximum(first - 1, 0), rows, :])
        for k in range(count):
            z = first + k
            after = field[jnp.minimum(z + 1, 15) if k == count - 1 else z + 1, rows, :]
            to_next = across_z[z + 1, rows, :] * (after - here)
            inward = flow[z, rows, :]
            beside = roll(side_flux[z // 8, rows, :], 115 - 16 * (z % 8), 1)
            value = inward - roll(inward, -1, 1) + jnp.where(ends, beside, 0.0)
            value = value + across_x[z, rows, :] * (here - field[z, start - 1 : start - 1 + size, :])
            value = value - across_x[z, start + 1 : start + 1 + size, :] * (
                field[z, start + 1 : start + 1 + size, :] - here
            )
            yield z, here, value + from_last - to_next
            here, from_last = after, to_next

    def apply(field, image):
        flow_along_y(field)

        def layers(k, carry):
            for start, size in WIDE:
                for z, _, value in apply_layers(field, k * U2, U2, start, size):
                    image[z, start : start + size, :] = value
            return carry

        lax.fori_loop(0, 16 // U2, layers, 0, unroll=V2)

    def hand_out(field, power, k):
        return pltpu.make_async_copy(field.at[:, 16:144, :], power, done.at[k])

    apply_sides(side0, side1)
    apply(field0, field1)
    hand_out(field1, power1, 0).start()
    apply_sides(side1, side2)
    apply(field1, field2)
    hand_out(field2, power2, 1).start()
    apply_sides(side2, None)
    flow_along_y(field2)

    def last(k, sums):
        for start, size in OWN_ROWS:
            rows = slice(start, start + size)
            for z, f2, f3 in apply_layers(field2, k * U3, U3, start, size):
                field3[z, start - 16 : start - 16 + size, :] = f3
                f0 = field0[z, rows, :]
                f1 = field1[z, rows, :]
                terms = (f0 * f0, f0 * f1, f1 * f1, f1 * f2, f2 * f2, f2 * f3)
                sums = tuple(s + jnp.sum(t.reshape(size // 8, 8, N), axis=0) for s, t in zip(sums, terms))
        part = pl.ds(k * U3, U3)
        pltpu.make_async_copy(field3.at[part], power3.at[part], done.at[2]).start()
        return sums

    sums = lax.fori_loop(0, 16 // U3, last, tuple(jnp.zeros((8, N), F32) for _ in range(6)), unroll=V3)
    line = jnp.where((lane[:1] >= 8) & (lane[:1] < 16), top, 0.0)
    for k, s in enumerate(sums):
        amount = jnp.sum(jnp.sum(s, axis=0, keepdims=True), axis=1, keepdims=True)
        line = jnp.where(lane[:1] == k, amount, line)
    table[...] = jnp.broadcast_to(line, table.shape)
    hand_out(field1, power1, 0).wait()
    hand_out(field2, power2, 1).wait()
    pltpu.make_async_copy(field3, power3, done.at[2]).wait()


def coefficients(everyone, own):
    n = everyone.shape[0]
    rows = everyone[...]
    lane = iota((n, N), 1)
    tops = jnp.where(lane < 8, roll(rows, -8, 1), 0.0)
    top = jnp.max(tops, axis=0, keepdims=True)
    top = jnp.max(jnp.where(lane[:1] == 0, top, -HUGE), axis=1, keepdims=True)
    factor = jnp.exp((tops - top) * lane.astype(F32))
    moments = jnp.sum(jnp.where(lane < 6, rows * factor, 0.0), axis=0, keepdims=True)
    u0, u1, u2, u3, u4, u5 = [
        jnp.sum(jnp.where(lane[:1] == k, moments, 0.0), axis=1, keepdims=True) for k in range(6)
    ]
    own_top = jnp.sum(jnp.where(lane[:1] == 8, own[0:1, :], 0.0), axis=1, keepdims=True)
    ratio = jnp.exp(own_top - top)

    def over(a, b):
        return jnp.where(b > 0.0, a / jnp.where(b > 0.0, b, 1.0), 0.0)

    l10 = over(u1, u0)
    l20 = over(u2, u0)
    d1 = u2 - l10 * u1
    s12 = u3 - l10 * u2
    l21 = over(s12, d1)
    d2 = (u4 - l20 * u2) - l21 * s12
    y1 = u4 - l10 * u3
    y2 = u5 - l20 * u3 - l21 * y1
    e2 = -over(y2, d2)
    e1 = -over(y1, d1) - l21 * e2
    e0 = -over(u3, u0) - l10 * e1 - l20 * e2

    sigma = jnp.exp(top)
    tau = jnp.minimum(1.0, 2.0 * sigma)
    kappa = jnp.minimum(1.0, 0.5 / sigma)
    at_zero = ((e0 * tau - e1 * kappa) * tau + e2 * kappa * kappa) * tau - kappa * kappa * kappa
    r_scale = tau * tau * tau / at_zero
    p_scale = -jnp.minimum(1.0 / sigma, 2.0) / at_zero
    q1 = tau * e2 - kappa
    r0 = r_scale * e0
    r1 = r_scale * e1 * ratio
    r2 = r_scale * e2 * ratio * ratio
    r3 = r_scale * ratio * ratio * ratio
    p0 = p_scale * (tau * tau * e1 - kappa * q1)
    p1 = p_scale * (tau * q1) * ratio
    p2 = p_scale * (tau * tau) * ratio * ratio
    return p0, p1, p2, r0, r1, r2, r3


def combine(
    everyone, own, source_in, power1_in, power2_in, power3_in, pressure_out, residual_out,
    source, power1, power2, power3, pressure, residual, arrived, left,
):
    def arrivals(g):
        part = slice(4 * g, 4 * g + 4)
        pairs = ((source_in, source), (power1_in, power1), (power2_in, power2), (power3_in, power3))
        return [
            pltpu.make_async_copy(far.at[part], near.at[part], arrived.at[k, g]) for k, (far, near) in enumerate(pairs)
        ]

    def departures(g):
        part = slice(4 * g, 4 * g + 4)
        return [
            pltpu.make_async_copy(near.at[part], far.at[part], left.at[k, g])
            for k, (near, far) in enumerate(((pressure, pressure_out), (residual, residual_out)))
        ]

    for g in range(4):
        for copy in arrivals(g):
            copy.start()
    p0, p1, p2, r0, r1, r2, r3 = coefficients(everyone, own)
    for g in range(4):
        for copy in arrivals(g):
            copy.wait()
        for z in range(4 * g, 4 * g + 4):
            f0 = source[z]
            f1 = power1[z]
            f2 = power2[z]
            pressure[z] = p0 * f0 + p1 * f1 + p2 * f2
            residual[z] = (r0 * f0 + r1 * f1) + (r2 * f2 + r3 * power3[z])
        for copy in departures(g):
            copy.start()
    for g in range(4):
        for copy in departures(g):
            copy.wait()


def vmem(count):
    return [pl.BlockSpec(memory_space=pltpu.VMEM)] * count


def shape(*dims):
    return jax.ShapeDtypeStruct(dims, F32)


def hbm(count):
    return [pl.BlockSpec(memory_space=pltpu.HBM)] * count


def in_hbm(x):
    return pltpu.with_memory_space_constraint(x, pltpu.HBM)


def call(body, inputs, out, out_specs, scratch=(), name=None, cost=1e6):
    return pl.pallas_call(
        body,
        out_shape=out,
        in_specs=inputs,
        out_specs=out_specs,
        scratch_shapes=list(scratch),
        compiler_params=pltpu.CompilerParams(vmem_limit_bytes=40 * 1024 * 1024),
        cost_estimate=pl.CostEstimate(flops=int(cost), bytes_accessed=int(cost), transcendentals=0),
        name=name,
    )


def exchange(to_next, to_previous, axis):
    count = lax.axis_size(axis)
    forward = [(i, (i + 1) % count) for i in range(count)]
    backward = [(target, source) for source, target in forward]
    return lax.ppermute(to_next, axis, forward), lax.ppermute(to_previous, axis, backward)


def exchange_pairs(outer, inner, axis):
    count = lax.axis_size(axis)
    across = [(i, (i + 1 if i % 2 else i - 1) % count) for i in range(count)]
    return lax.ppermute(outer, axis, across), lax.ppermute(inner, axis, [(i, i ^ 1) for i in range(count)])


def local(noise, biofilm, source):
    block = pltpu.VMEM((NZ, N, N), F32)
    to_right, to_left = call(
        pack_first,
        hbm(1),
        [shape(Y_ROWS[0], N)] * 2,
        vmem(2),
        [pltpu.VMEM((H, N, N), F32), pltpu.SemaphoreType.DMA((H // 2,))],
        name="pack_first",
    )(in_hbm(noise))
    beside1 = exchange(to_right, to_left, "gy")
    to_right, to_left = call(
        pack_second,
        vmem(2) + hbm(2),
        [shape(Y_ROWS[1], N)] * 2,
        vmem(2),
        [block, pltpu.VMEM((NZ, N, N), jnp.int32), pltpu.SemaphoreType.DMA((2, 8))],
        name="pack_second",
        cost=2e10,
    )(to_left, noise, in_hbm(source), in_hbm(biofilm))
    beside2 = exchange(to_right, to_left, "gy")
    own_middle, own_edge, factor = call(
        column_sums_own,
        vmem(2),
        [shape(NZ, N, N), shape(N, N), shape(NZ, N, N)],
        vmem(3),
        name="columns_own",
        cost=2e10,
    )(noise, biofilm)
    middle1, first_edge, outer, inner = call(
        columns_first,
        vmem(5),
        [shape(H, N, N), shape(N, N)] + [shape(X_ROWS[0], N)] * 2,
        vmem(4),
        name="columns_first",
    )(own_middle, source, biofilm, *beside1)
    above_below1 = exchange_pairs(outer, inner, "gx")
    middle2, edge, edge_source, edge_biofilm, outer, inner = call(
        columns_second,
        vmem(7),
        [shape(G, N, N), shape(N, N), shape(N, N), shape(N, N)] + [shape(X_ROWS[1], N)] * 2,
        vmem(6),
        name="columns_second",
        cost=2e10,
    )(own_middle, own_edge, first_edge, source, biofilm, *beside2)
    above_below2 = exchange_pairs(outer, inner, "gx")
    partial, edge_factor = call(
        row_sums_own,
        vmem(3),
        [shape(G + 1, 144, N), shape(N, N)],
        vmem(2),
        name="rows_own",
        cost=1,
    )(middle2, edge, edge_biofilm)
    logperm1, largest1 = call(
        rows_first,
        vmem(3),
        [shape(H, 144, N), shape(8, N)],
        vmem(2),
        name="rows_first",
        cost=2e10,
    )(middle1, *above_below1)
    devices = lax.axis_size("gx") * lax.axis_size("gy")
    layers = pltpu.VMEM((NZ, ROWS, N), F32)
    plane = pltpu.VMEM((ROWS, N), F32)
    sides = pltpu.VMEM((2, ROWS, N), F32)
    power1, power2, power3, table = call(
        operate_powers,
        vmem(11),
        [pltpu.HBM((NZ, N, N), F32)] * 3 + [shape(devices, N)],
        hbm(3) + vmem(1),
        [layers] * 3
        + [pltpu.VMEM((NZ + 1, ROWS, N), F32)]
        + [layers] * 4
        + [block, pltpu.VMEM((G + 1, 144, N), F32), plane, plane]
        + [sides] * 8
        + [pltpu.SemaphoreType.DMA((3,))],
        name="powers",
    )(logperm1, largest1, partial, factor, edge_factor, edge_source, source, *above_below1, *above_below2)
    everyone = lax.all_to_all(table, ("gx", "gy"), 0, 0, tiled=True)
    return tuple(
        call(
            combine,
            vmem(2) + hbm(4),
            [pltpu.HBM((NZ, N, N), F32)] * 2,
            hbm(2),
            [block] * 6 + [pltpu.SemaphoreType.DMA((4, 4)), pltpu.SemaphoreType.DMA((2, 4))],
            name="combine",
        )(everyone, table, *[in_hbm(x) for x in (source, power1, power2, power3)])
    )


def solution(mesh):
    in_specs = (P(None, "gx", "gy"), P(None, "gx", "gy"), P(None, "gx", "gy"))
    out_specs = (P(None, "gx", "gy"), P(None, "gx", "gy"))
    return jax.shard_map(local, mesh=mesh, in_specs=in_specs, out_specs=out_specs, check_vma=False)
```

```python
import jax
import jax.numpy as jnp
from jax import lax
from jax.experimental import pallas as pl
from jax.experimental.pallas import tpu as pltpu
from jax.sharding import PartitionSpec as P

R = 64
WIDTH = 2 * R + 1
NZ = 16
N = 128
F32 = jnp.float32
BF16 = jnp.bfloat16

H = 10
G = NZ - H
Y_ROWS = (H // 2 * N, G // 2 * N + N + 16)
X_TAIL = (H * 72, (G + 1) * 72)
X_ROWS = (X_TAIL[0] + (H + 7) // 8 * 8, X_TAIL[1] + (G + 8) // 8 * 8)
ROWS = 160
OWN = 16
HUGE = 1e30
C3 = 64


def iota(shape, dim):
    return lax.broadcasted_iota(jnp.int32, shape, dim)


def roll(x, shift, axis):
    if isinstance(shift, int):
        shift = shift % x.shape[axis]
        if shift == 0:
            return x
    return pltpu.roll(x, shift, axis)


def split3(x):
    high = x.astype(BF16)
    rest = x - high.astype(F32)
    middle = rest.astype(BF16)
    low = (rest - middle.astype(F32)).astype(BF16)
    return high, middle, low


def split2(x):
    high = x.astype(BF16)
    return high, (x - high.astype(F32)).astype(BF16)


def dot(a, b):
    return lax.dot_general(a, b, (((1,), (0,)), ((), ())), preferred_element_type=F32)


def weights(mask):
    return jnp.where(mask, 1.0, 0.0).astype(BF16)


def pack_first(noise_in, to_right, to_left, noise, arrived):
    low = iota((N, N), 1) < 64
    copies = [
        pltpu.make_async_copy(noise_in.at[2 * q : 2 * q + 2], noise.at[2 * q : 2 * q + 2], arrived.at[q])
        for q in range(H // 2)
    ]
    for copy in copies:
        copy.start()
    for q in range(H // 2):
        copies[q].wait()
        even = noise[2 * q]
        odd = noise[2 * q + 1]
        to_right[q * N : q * N + N, :] = jnp.where(low, roll(even, 64, 1), odd)
        to_left[q * N : q * N + N, :] = jnp.where(low, even, roll(odd, 64, 1))


def pack_second(after, noise, source_in, biofilm_in, to_right, to_left, source, biofilm, arrived):
    def arrivals(g):
        rows = slice(16 * g, 16 * g + 16)
        return [
            pltpu.make_async_copy(far.at[:, rows, :], near.at[:, rows, :], arrived.at[k, g])
            for k, (far, near) in enumerate(((source_in, source), (biofilm_in, biofilm)))
        ]

    del after
    for g in range(8):
        for copy in arrivals(g):
            copy.start()

    lane = iota((16, N), 1)
    slot = lane % 8
    low = lane < 64
    outer = (lane < 32) | (lane >= 96)

    def six(k):
        return ((lane - (8 * k + 5)) & 127) < 6

    third_right = jnp.zeros((16, N), F32)
    third_left = jnp.zeros((16, N), F32)
    for g in range(8):
        for copy in arrivals(g):
            copy.wait()
        rows = slice(16 * g, 16 * g + 16)
        sources = jnp.zeros((16, N), F32)
        noises = jnp.zeros((16, N), F32)
        levels = jnp.zeros((16, N), jnp.int32)
        for z in range(16):
            n = noise[z, rows, :]
            both = roll(jnp.where(outer, source[z, rows, :], n), 8 * z + 8, 1)
            sources = jnp.where(six(z), both, sources)
            noises = jnp.where(six((z + 8) % 16), both, noises)
            levels = jnp.where(six(z), roll(biofilm[z, rows, :], 8 * z + 8, 1), levels)
            if z >= H and z % 2 == 1:
                even = noise[z - 1, rows, :]
                first = (z - 1 - H) // 2 * N + 16 * g
                to_right[first : first + 16, :] = jnp.where(low, roll(even, 64, 1), n)
                to_left[first : first + 16, :] = jnp.where(low, even, roll(n, 64, 1))
        br = levels.astype(F32)
        bl = roll(br, -8, 1)
        first = G // 2 * N + 16 * g
        to_right[first : first + 16, :] = jnp.where(
            slot < 3, roll(noises, -69, 1), jnp.where(slot < 5, roll(br, -3, 1), sources)
        )
        to_left[first : first + 16, :] = jnp.where(
            slot < 3, roll(sources, -8, 1), jnp.where(slot < 5, roll(bl, 3, 1), roll(noises, -67, 1))
        )
        third_right = third_right + roll(jnp.where(slot == 5, br, 0.0), g, 1)
        third_left = third_left + roll(jnp.where(slot == 2, bl, 0.0), g, 1)
    to_right[G // 2 * N + N :, :] = third_right
    to_left[G // 2 * N + N :, :] = third_left


def column_weights():
    m = iota((N, 2 * N), 0)
    o = iota((N, 2 * N), 1)
    s = o - N
    own = ((o < N) & (m - o <= R) & (o - m <= R)) | ((o >= N) & (s <= 2) & (m >= s + 64)) | (
        (s >= 5) & (s <= 7) & (m <= s + 56)
    )
    lane = iota((N, 3 * N), 0)
    o = iota((N, 3 * N), 1)
    half = lane // 64
    m = lane % 64
    e = o - 2 * N
    same = (o < 2 * N) & (o // N == half)
    edge = (e >= 0) & (e < 16) & (e // 8 == half)
    left = (same & (m >= o % N)) | (edge & (o % 8 >= 5))
    right = (same & (m + 64 <= o % N)) | (edge & (o % 8 <= 2))
    a = iota((N, N), 0)
    b = iota((N, N), 1)
    together = a // 8 == b // 8
    t = a % 8
    s = b % 8
    left_extra = together & (t <= 2) & (s >= 5) & (t >= s - 5)
    right_extra = together & (t >= 5) & (s <= 2) & (t - 5 <= s)
    return [weights(w) for w in (own, left, right, left_extra, right_extra)]


def column_sums_own(noise, biofilm, own_middle, own_edge, factor):
    own = column_weights()[0]
    twice = jnp.concatenate([own, own], axis=0)
    total = jnp.zeros((N, N), F32)
    for z in range(16):
        out = dot(jnp.concatenate(split2(noise[z]), axis=1), twice)
        own_middle[z] = out[:, :N]
        total = total + roll(out[:, N:], 8 * z, 1)
        factor[z] = resistance_factor(biofilm[z].astype(F32))
    own_edge[...] = total


def sums_beside(x, y, w):
    high, low = split2(jnp.concatenate([x, y], axis=1))
    return dot(high, w) + dot(low, w)


def on_even():
    return lax.axis_index("gx") % 2 == 0


class Chosen:
    def __init__(self, first, a, b):
        self.first, self.a, self.b = first, a, b

    def __getitem__(self, index):
        return jnp.where(self.first, self.a[index], self.b[index])


def part_columns(first_layer, count, own_middle, from_left, from_right, middle):
    _, left, right, _, _ = column_weights()
    both = jnp.concatenate([left, right], axis=0)
    total = jnp.zeros((N, N), F32)
    for q in range(count // 2):
        rows = slice(q * N, q * N + N)
        halo = sums_beside(from_left[rows, :], from_right[rows, :], both)
        total = total + roll(halo[:, 2 * N :], 8 * first_layer + 16 * q, 1)
        for k in (0, 1):
            z = 2 * q + k
            middle[z] = own_middle[first_layer + z] + halo[:, k * N : k * N + N]
    return total


def fill_messages(sums, sources, levels, tail, outer, inner):
    def fill(to_down, to_up):
        for ref in (to_down, to_up):
            ref[tail:, :] = jnp.zeros((ref.shape[0] - tail, N), F32)
        for z in range(len(sums)):
            to_down[z * 72 : z * 72 + 72, :] = sums[z][56:128, :]
            to_up[z * 72 : z * 72 + 72, :] = sums[z][0:72, :]
        for z, (s, b) in enumerate(zip(sources, levels)):
            to_down[z * 72 : z * 72 + 3, :] = s[125:128, :]
            to_down[z * 72 + 3 : z * 72 + 5, :] = b[126:128, :].astype(F32)
            to_down[tail + z : tail + z + 1, :] = b[125:126, :].astype(F32)
            to_up[z * 72 + 67 : z * 72 + 70, :] = s[0:3, :]
            to_up[z * 72 + 70 : z * 72 + 72, :] = b[0:2, :].astype(F32)
            to_up[tail + z : tail + z + 1, :] = b[2:3, :].astype(F32)

    even = on_even()

    @pl.when(even)
    def _():
        fill(inner, outer)

    @pl.when(jnp.logical_not(even))
    def _():
        fill(outer, inner)


def columns_first(own_middle, source, biofilm, from_left, from_right, middle, edge, outer, inner):
    edge[...] = part_columns(0, H, own_middle, from_left, from_right, middle)
    planes = [[ref.at[z] for z in range(H)] for ref in (middle, source, biofilm)]
    fill_messages(*planes, X_TAIL[0], outer, inner)


def columns_second(
    own_middle, own_edge, first_edge, source, biofilm, from_left, from_right,
    middle, edge, edge_source, edge_biofilm, outer, inner,
):
    _, _, _, left_extra, right_extra = column_weights()
    slot = iota((N, N), 1) % 8
    first = G // 2 * N
    extra_left = from_left[first : first + N, :]
    extra_right = from_right[first : first + N, :]
    total = own_edge[...] + first_edge[...]
    total = total + sums_beside(extra_left, extra_right, jnp.concatenate([left_extra, right_extra], axis=0))
    edge[...] = total + part_columns(H, G, own_middle, from_left, from_right, middle)

    edge_source[...] = jnp.where(slot >= 5, extra_left, jnp.where(slot <= 2, extra_right, 0.0))
    third_left = from_left[first + N :, :]
    third_right = from_right[first + N :, :]
    levels = jnp.where(slot >= 6, roll(extra_left, 3, 1), jnp.where(slot <= 1, roll(extra_right, -3, 1), 0.0))
    slot16 = iota((16, N), 1) % 8
    for g in range(8):
        rows = slice(16 * g, 16 * g + 16)
        edge_biofilm[rows, :] = jnp.where(
            slot16 == 5, roll(third_left, -g, 1), jnp.where(slot16 == 2, roll(third_right, -g, 1), levels[rows, :])
        )

    planes = [[ref.at[H + z] for z in range(G)] for ref in (source, biofilm)]
    fill_messages(
        [middle.at[z] for z in range(G)] + [edge],
        planes[0] + [edge_source],
        planes[1] + [edge_biofilm],
        X_TAIL[1],
        outer,
        inner,
    )


def row_weights():
    r = iota((144, N), 0) - 8
    m = iota((144, N), 1)
    inside = (r >= -3) & (r <= 130)
    own = inside & (m >= r - R) & (m <= r + R)
    halo = inside & (((m < 64) & (m >= r)) | ((m >= 64) & (m <= r)))
    return weights(own), weights(halo)


def row_sums(band, *planes):
    columns = [jnp.concatenate(split2(p), axis=0) for p in planes]
    out = dot(jnp.concatenate([band, band], axis=1), jnp.concatenate(columns, axis=1))
    return [out[:, k * N : k * N + N] for k in range(len(planes))]


def halo_rows(from_up, from_down, z):
    first = pl.multiple_of(z * 72, 8)
    return jnp.concatenate([from_up[pl.ds(first + 8, 64), :], from_down[pl.ds(first, 64), :]], axis=0)


def finish_sums(from_up, from_down, z, sums, out, lanes=None):
    row8 = iota((8, N), 0)
    row144 = iota((144, N), 0)
    first = pl.multiple_of(z * 72, 8)
    above = jnp.where(row8 >= 5, from_up[pl.ds(first, 8), :], 0.0)
    below = jnp.where(row8 <= 2, from_down[pl.ds(first + 64, 8), :], 0.0)
    above = jnp.where(row8 >= 5, above + roll(above, 7, 0) + roll(above, 6, 0), 0.0)
    below = jnp.where(row8 <= 2, below + roll(below, 1, 0) + roll(below, 2, 0), 0.0)
    total = jnp.concatenate([sums[:8] + above, sums[8:136], sums[136:] + below], axis=0) * (1.0 / WIDTH)
    out[...] = total
    real = (row144 >= 5) & (row144 <= 138)
    if lanes is not None:
        real = real & lanes
    return jnp.max(jnp.where(real, total, -HUGE).reshape(18, 8, N), axis=0)


def row_sums_own(middle, edge, edge_biofilm, partial, factor):
    own, _ = row_weights()
    for z in range(0, G, 2):
        partial[z], partial[z + 1] = row_sums(own, middle[z], middle[z + 1])
    partial[G] = row_sums(own, edge[...])[0]
    factor[...] = resistance_factor(edge_biofilm[...])


def resistance_factor(biofilm):
    open_part = 1.0 - 0.06 * biofilm
    solid = (1.0 - 0.35 * open_part) * (1.0 / (1.0 - 0.35))
    return (0.5 * solid * solid) / (open_part * open_part * open_part)


def resistance(logperm, factor, top):
    return jnp.minimum(jnp.exp(top - logperm) * factor, HUGE)


def reciprocal(x):
    guess = pl.reciprocal(x, approx=True)
    return guess * (2.0 - x * guess)


MAIN = slice(8, 152)
BEFORE = slice(7, 151)
AFTER = slice(9, 153)
OWN_ROWS = tuple((start, C3) for start in range(16, 144, C3))


def largest_of(tile):
    return jnp.maximum(jnp.max(jnp.max(tile, axis=0, keepdims=True), axis=1, keepdims=True), -60.0)


def halo_tiles(part, z):
    from_up, from_down, tail = part
    row8 = iota((8, N), 0)
    first = pl.multiple_of(z * 72, 8)
    above = from_up[pl.ds(first, 8), :]
    below = from_down[pl.ds(first + 64, 8), :]
    third_above = from_up[pl.ds(tail + z, 1), :]
    third_below = from_down[pl.ds(tail + z, 1), :]
    source_above = jnp.where(row8 >= 5, roll(above, 5, 0), 0.0)
    source_below = jnp.where(row8 <= 2, roll(below, 5, 0), 0.0)
    biofilm_above = jnp.where(row8 == 5, third_above, jnp.where(row8 >= 6, roll(above, 3, 0), 0.0))
    biofilm_below = jnp.where(row8 == 2, third_below, jnp.where(row8 <= 1, roll(below, 2, 0), 0.0))
    return source_above, source_below, biofilm_above, biofilm_below


def prepare(part, z, top, logperm, out, field, own_source, own_factor):
    row8 = iota((8, N), 0)
    source_above, source_below, biofilm_above, biofilm_below = halo_tiles(part, z)
    field[8:16, :] = source_above
    field[16:144, :] = own_source
    field[144:152, :] = source_below
    out[8:16, :] = jnp.where(row8 >= 5, resistance(logperm[0:8, :], resistance_factor(biofilm_above), top), HUGE)
    out[144:152, :] = jnp.where(row8 <= 2, resistance(logperm[136:144, :], resistance_factor(biofilm_below), top), HUGE)
    out[16:144, :] = resistance(logperm[8:136, :], own_factor, top)
    empty = jnp.full((8, N), HUGE, F32)
    none = jnp.zeros((8, N), F32)
    out[0:8, :] = empty
    out[152:160, :] = empty
    field[0:8, :] = none
    field[152:160, :] = none


def block_faces(here_ref, last_ref, across_x, across_y, across_z):
    here = here_ref[MAIN, :]
    across_x[MAIN, :] = reciprocal(here + here_ref[BEFORE, :])
    across_x[152:160, :] = jnp.zeros((8, N), F32)
    across_y[MAIN, :] = jnp.where(iota((144, N), 1) == 0, 0.0, reciprocal(here + roll(here, 1, 1)))
    if last_ref is None:
        across_z[MAIN, :] = jnp.zeros((144, N), F32)
    else:
        across_z[MAIN, :] = reciprocal(here + last_ref[MAIN, :])


def pack_inner(p, layers):
    group = iota((ROWS, N), 1) // 16
    packed = jnp.zeros((ROWS, N), F32)
    for z, ref in layers:
        if z // 8 == p:
            packed = jnp.where(group == z % 8, roll(ref[...], 16 * (z % 8) + 3, 1), packed)
    return packed


def rows_first(
    middle, factor, source, outer, inner,
    largest, field0, across_x, across_y, across_z, image, last_resist, packed_resist, packed_field,
    logperm, resist, flow,
):
    even = on_even()
    from_up, from_down = Chosen(even, outer, inner), Chosen(even, inner, outer)
    part = (from_up, from_down, X_TAIL[0])
    own, halo = row_weights()
    most = jnp.full((8, N), -HUGE, F32)
    for z in range(0, H, 2):
        near = row_sums(own, middle[z], middle[z + 1])
        far = row_sums(halo, *[halo_rows(from_up, from_down, z + i) for i in (0, 1)])
        for i in (0, 1):
            most = jnp.maximum(most, finish_sums(from_up, from_down, z + i, near[i] + far[i], logperm.at[z + i]))
    top = largest_of(most)
    largest[...] = jnp.broadcast_to(top, (8, N))
    for z in range(H):
        prepare(part, z, top, logperm.at[z], resist.at[z], field0.at[z], source[z], factor[z])
    for z in range(H):
        block_faces(
            resist.at[z], resist.at[z - 1] if z else None, across_x.at[z], across_y.at[z], across_z.at[z]
        )
    last_resist[...] = resist[H - 1]
    for packed, ref in ((packed_resist, resist), (packed_field, field0)):
        for p in range(2):
            packed[p] = pack_inner(p, [(z, ref.at[z]) for z in range(H)])
    for z in range(H):
        here = field0[z, MAIN, :]
        flow[z, MAIN, :] = across_y[z, MAIN, :] * (here - roll(here, 1, 1))
    from_last = jnp.zeros((144, N), F32)
    for z in range(H):
        here = field0[z, MAIN, :]
        inward = flow[z, MAIN, :]
        value = inward - roll(inward, -1, 1) + from_last
        value = value + across_x[z, MAIN, :] * (here - field0[z, BEFORE, :])
        value = value - across_x[z, AFTER, :] * (field0[z, AFTER, :] - here)
        if z < H - 1:
            from_last = across_z[z + 1, MAIN, :] * (field0[z + 1, MAIN, :] - here)
            value = value - from_last
        image[z] = value


def operate_powers(
    largest1, field0_1, across_x1, across_y1, across_z1, image1, last_resist, packed_resist, packed_field,
    partial, factor, edge_factor, edge_source, source, outer2, inner2,
    power1, power2, power3, table,
    resist, across_x2, across_y2, across_z2, flow, field0_2, field1, field2, field3,
    logperm2, plane_resist, plane_field,
    side_resist, side_x, side_y, side_z, side0, side1, side2, side_flux, done,
):
    lane = iota((8, N), 1)
    even = on_even()
    from_up2, from_down2 = Chosen(even, outer2, inner2), Chosen(even, inner2, outer2)
    part = (from_up2, from_down2, X_TAIL[1])

    _, halo = row_weights()
    edge_lane = (iota((144, N), 1) % 8 <= 2) | (iota((144, N), 1) % 8 >= 5)
    largest = largest1[...]
    top1 = largest[:1, :1]
    for z in range(0, G, 2):
        pair = row_sums(halo, halo_rows(from_up2, from_down2, z), halo_rows(from_up2, from_down2, z + 1))
        for i in (0, 1):
            sums = partial[z + i] + pair[i]
            largest = jnp.maximum(largest, finish_sums(from_up2, from_down2, z + i, sums, logperm2.at[z + i]))
    sums = partial[G] + row_sums(halo, halo_rows(from_up2, from_down2, G))[0]
    largest = jnp.maximum(largest, finish_sums(from_up2, from_down2, G, sums, logperm2.at[G], edge_lane))
    top = largest_of(largest)
    shrink = jnp.exp(top1 - top)
    grow = jnp.exp(top - top1)

    prepare(part, G, top, logperm2.at[G], plane_resist, plane_field, edge_source[...], edge_factor[...])
    for k in range(G):
        prepare(part, k, top, logperm2.at[k], resist.at[1 + k], field0_2.at[k], source[H + k], factor[H + k])
    resist[0] = jnp.minimum(last_resist[...] * grow, HUGE)
    none = jnp.zeros((8, N), F32)
    for ref in (field1, field2):
        for z in range(NZ):
            ref[z, 0:8, :] = none
            ref[z, 152:160, :] = none
    for ref in (side1, side2, side_x):
        for p in range(2):
            ref[p, 0:8, :] = none
            ref[p, 152:160, :] = none

    a = iota((N, 2 * N), 0)
    o = iota((N, 2 * N), 1)
    t = o % 16
    spread = weights(
        (a // 8 == o // 16)
        & (((t >= 3) & (t <= 5) & (a % 8 == t - 3)) | ((t >= 10) & (t <= 12) & (a % 8 == t - 5)))
    )
    slot160 = iota((ROWS, N), 1) % 16
    second_resist = [(H + k, resist.at[1 + k]) for k in range(G)]
    second_field = [(H + k, field0_2.at[k]) for k in range(G)]
    first_group = iota((ROWS, N), 1) // 16
    for plane, packed, second, side, fill in (
        (plane_resist, packed_resist, second_resist, side_resist, HUGE),
        (plane_field, packed_field, second_field, side0, 0.0),
    ):
        high, mid, low = split3(plane[...])
        beyond = dot(high, spread) + dot(mid, spread) + dot(low, spread)
        for p in range(2):
            inside = packed[p]
            if fill:
                inside = jnp.minimum(inside * grow, HUGE)
            inside = jnp.where(first_group + 8 * p < H, inside, pack_inner(p, second))
            value = jnp.where(
                slot160 <= 2, inside, jnp.where(slot160 >= 13, roll(inside, 10, 1), beyond[:, p * N : p * N + N])
            )
            side[p] = jnp.where((slot160 <= 5) | (slot160 >= 10), value, fill)

    def next_layer(first, second):
        lanes = iota(first.shape, 1)
        return jnp.where(lanes < 112, roll(first, -16, 1), roll(second, -16, 1)), roll(second, -16, 1)

    def last_layer(first, second):
        lanes = iota(first.shape, 1)
        return (
            jnp.where(lanes >= 16, roll(first, 16, 1), 0.0),
            jnp.where(lanes >= 16, roll(second, 16, 1), roll(first, 16, 1)),
        )

    here = [side_resist[p, MAIN, :] for p in range(2)]
    after = next_layer(*here)
    for p in range(2):
        side_x[p, MAIN, :] = reciprocal(here[p] + side_resist[p, BEFORE, :])
        side_y[p, MAIN, :] = reciprocal(here[p] + roll(here[p], 1, 1))
        value = reciprocal(here[p] + after[p])
        side_z[p, MAIN, :] = value if p == 0 else jnp.where(iota((144, N), 1) < 112, value, 0.0)
    for k in range(G):
        block_faces(resist.at[1 + k], resist.at[k], across_x2.at[k], across_y2.at[k], across_z2.at[k])

    def layer_of(first, second, z):
        return first.at[z] if z < H else second.at[z - H]

    field0 = [layer_of(field0_1, field0_2, z) for z in range(NZ)]
    across_x = [layer_of(across_x1, across_x2, z) for z in range(NZ)]
    across_y = [layer_of(across_y1, across_y2, z) for z in range(NZ)]
    across_z = [layer_of(across_z1, across_z2, z) for z in range(NZ)]

    def apply_sides(field, image):
        slot = iota((144, N), 1) % 16
        here = [field[p, MAIN, :] for p in range(2)]
        inward = [side_y[p, MAIN, :] * (here[p] - roll(here[p], 1, 1)) for p in range(2)]
        for p in range(2):
            side_flux[p, MAIN, :] = jnp.where(slot == 13, inward[p], -roll(inward[p], 9, 1))
        if image is None:
            return
        after = next_layer(*here)
        through = [side_z[p, MAIN, :] * (after[p] - here[p]) for p in range(2)]
        back = last_layer(*through)
        for p in range(2):
            value = inward[p] - roll(inward[p], -1, 1) - through[p] + back[p]
            value = value + side_x[p, MAIN, :] * (here[p] - field[p, BEFORE, :])
            value = value - side_x[p, AFTER, :] * (field[p, AFTER, :] - here[p])
            image[p, MAIN, :] = value

    def flow_along_y(field, layers):
        for z in layers:
            here = field[z][MAIN, :]
            flow[z, MAIN, :] = across_y[z][MAIN, :] * (here - roll(here, 1, 1))

    def from_beside(z, rows, size):
        lanes = iota((size, N), 1)
        beside = roll(side_flux[z // 8, rows, :], 115 - 16 * (z % 8), 1)
        return jnp.where((lanes == 0) | (lanes == 127), beside, 0.0)

    def apply_layers(field, layers, start, size):
        rows = slice(start, start + size)
        before = slice(start - 1, start - 1 + size)
        after = slice(start + 1, start + 1 + size)
        first = layers[0]
        here = field[first][rows, :]
        from_last = 0.0 if first == 0 else across_z[first][rows, :] * (here - field[first - 1][rows, :])
        for z in layers:
            inward = flow[z, rows, :]
            value = inward - roll(inward, -1, 1)
            value = value + across_x[z][rows, :] * (here - field[z][before, :])
            value = value - across_x[z][after, :] * (field[z][after, :] - here)
            nearby = from_beside(z, rows, size)
            if z < NZ - 1:
                following = field[z + 1][rows, :]
                to_next = across_z[z + 1][rows, :] * (following - here)
            else:
                following, to_next = here, 0.0
            if z < H - 1:
                value = shrink * (value + from_last - to_next) + nearby
            elif z == H - 1:
                value = shrink * (value + from_last) + nearby - to_next
            else:
                value = value + nearby + from_last - to_next
            yield z, here, value
            here, from_last = following, to_next

    def hand_out(field, power, k):
        return pltpu.make_async_copy(field.at[:, 16:144, :], power, done.at[k])

    def layers_of(ref):
        return [ref.at[z] for z in range(NZ)]

    apply_sides(side0, side1)
    flow_along_y(field0, range(H, NZ))
    for z in range(H):
        value = shrink * image1[z] + from_beside(z, MAIN, 144)
        if z == H - 1:
            value = value - across_z[H][MAIN, :] * (field0[H][MAIN, :] - field0[z][MAIN, :])
        field1[z, MAIN, :] = value
    for z, _, value in apply_layers(field0, range(H, NZ), 8, 144):
        field1[z, MAIN, :] = value
    hand_out(field1, power1, 0).start()
    apply_sides(side1, side2)
    flow_along_y(layers_of(field1), range(NZ))
    for z, _, value in apply_layers(layers_of(field1), range(NZ), 8, 144):
        field2[z, MAIN, :] = value
    hand_out(field2, power2, 1).start()
    apply_sides(side2, None)
    flow_along_y(layers_of(field2), range(NZ))

    sums = tuple(jnp.zeros((8, N), F32) for _ in range(6))
    for group in range(0, NZ, 4):
        for start, size in OWN_ROWS:
            rows = slice(start, start + size)
            for z, f2, f3 in apply_layers(layers_of(field2), range(group, group + 4), start, size):
                field3[z, start - 16 : start - 16 + size, :] = f3
                f0 = field0[z][rows, :]
                f1 = field1[z, rows, :]
                terms = (f0 * f0, f0 * f1, f1 * f1, f1 * f2, f2 * f2, f2 * f3)
                sums = tuple(s + jnp.sum(t.reshape(size // 8, 8, N), axis=0) for s, t in zip(sums, terms))
        part = pl.ds(group, 4)
        pltpu.make_async_copy(field3.at[part], power3.at[part], done.at[2]).start()

    line = jnp.where((lane[:1] >= 8) & (lane[:1] < 16), top, 0.0)
    for k, s in enumerate(sums):
        amount = jnp.sum(jnp.sum(s, axis=0, keepdims=True), axis=1, keepdims=True)
        line = jnp.where(lane[:1] == k, amount, line)
    table[...] = jnp.broadcast_to(line, table.shape)
    hand_out(field1, power1, 0).wait()
    hand_out(field2, power2, 1).wait()
    pltpu.make_async_copy(field3, power3, done.at[2]).wait()


def coefficients(everyone, own):
    n = everyone.shape[0]
    rows = everyone[...]
    lane = iota((n, N), 1)
    tops = jnp.where(lane < 8, roll(rows, -8, 1), 0.0)
    top = jnp.max(tops, axis=0, keepdims=True)
    top = jnp.max(jnp.where(lane[:1] == 0, top, -HUGE), axis=1, keepdims=True)
    factor = jnp.exp((tops - top) * lane.astype(F32))
    moments = jnp.sum(jnp.where(lane < 6, rows * factor, 0.0), axis=0, keepdims=True)
    u0, u1, u2, u3, u4, u5 = [
        jnp.sum(jnp.where(lane[:1] == k, moments, 0.0), axis=1, keepdims=True) for k in range(6)
    ]
    own_top = jnp.sum(jnp.where(lane[:1] == 8, own[0:1, :], 0.0), axis=1, keepdims=True)
    ratio = jnp.exp(own_top - top)

    def over(a, b):
        return jnp.where(b > 0.0, a / jnp.where(b > 0.0, b, 1.0), 0.0)

    l10 = over(u1, u0)
    l20 = over(u2, u0)
    d1 = u2 - l10 * u1
    s12 = u3 - l10 * u2
    l21 = over(s12, d1)
    d2 = (u4 - l20 * u2) - l21 * s12
    y1 = u4 - l10 * u3
    y2 = u5 - l20 * u3 - l21 * y1
    e2 = -over(y2, d2)
    e1 = -over(y1, d1) - l21 * e2
    e0 = -over(u3, u0) - l10 * e1 - l20 * e2

    sigma = jnp.exp(top)
    tau = jnp.minimum(1.0, 2.0 * sigma)
    kappa = jnp.minimum(1.0, 0.5 / sigma)
    at_zero = ((e0 * tau - e1 * kappa) * tau + e2 * kappa * kappa) * tau - kappa * kappa * kappa
    r_scale = tau * tau * tau / at_zero
    p_scale = -jnp.minimum(1.0 / sigma, 2.0) / at_zero
    q1 = tau * e2 - kappa
    r0 = r_scale * e0
    r1 = r_scale * e1 * ratio
    r2 = r_scale * e2 * ratio * ratio
    r3 = r_scale * ratio * ratio * ratio
    p0 = p_scale * (tau * tau * e1 - kappa * q1)
    p1 = p_scale * (tau * q1) * ratio
    p2 = p_scale * (tau * tau) * ratio * ratio
    return p0, p1, p2, r0, r1, r2, r3


def combine(
    everyone, own, source_in, power1_in, power2_in, power3_in, pressure_out, residual_out,
    source, power1, power2, power3, pressure, residual, arrived, left,
):
    def arrivals(g):
        part = slice(4 * g, 4 * g + 4)
        pairs = ((source_in, source), (power1_in, power1), (power2_in, power2), (power3_in, power3))
        return [
            pltpu.make_async_copy(far.at[part], near.at[part], arrived.at[k, g]) for k, (far, near) in enumerate(pairs)
        ]

    def departures(g):
        part = slice(4 * g, 4 * g + 4)
        return [
            pltpu.make_async_copy(near.at[part], far.at[part], left.at[k, g])
            for k, (near, far) in enumerate(((pressure, pressure_out), (residual, residual_out)))
        ]

    for g in range(4):
        for copy in arrivals(g):
            copy.start()
    p0, p1, p2, r0, r1, r2, r3 = coefficients(everyone, own)
    for g in range(4):
        for copy in arrivals(g):
            copy.wait()
        for z in range(4 * g, 4 * g + 4):
            f0 = source[z]
            f1 = power1[z]
            f2 = power2[z]
            pressure[z] = p0 * f0 + p1 * f1 + p2 * f2
            residual[z] = (r0 * f0 + r1 * f1) + (r2 * f2 + r3 * power3[z])
        for copy in departures(g):
            copy.start()
    for g in range(4):
        for copy in departures(g):
            copy.wait()


def vmem(count):
    return [pl.BlockSpec(memory_space=pltpu.VMEM)] * count


def shape(*dims):
    return jax.ShapeDtypeStruct(dims, F32)


def hbm(count):
    return [pl.BlockSpec(memory_space=pltpu.HBM)] * count


def in_hbm(x):
    return pltpu.with_memory_space_constraint(x, pltpu.HBM)


def call(body, inputs, out, out_specs, scratch=(), name=None, cost=1e6):
    return pl.pallas_call(
        body,
        out_shape=out,
        in_specs=inputs,
        out_specs=out_specs,
        scratch_shapes=list(scratch),
        compiler_params=pltpu.CompilerParams(vmem_limit_bytes=40 * 1024 * 1024),
        cost_estimate=pl.CostEstimate(flops=int(cost), bytes_accessed=int(cost), transcendentals=0),
        name=name,
    )


def exchange(to_next, to_previous, axis):
    count = lax.axis_size(axis)
    forward = [(i, (i + 1) % count) for i in range(count)]
    backward = [(target, source) for source, target in forward]
    return lax.ppermute(to_next, axis, forward), lax.ppermute(to_previous, axis, backward)


def exchange_pairs(outer, inner, axis):
    count = lax.axis_size(axis)
    across = [(i, (i + 1 if i % 2 else i - 1) % count) for i in range(count)]
    from_partner = lax.ppermute(inner, axis, [(i, i ^ 1) for i in range(count)])
    return lax.ppermute(outer, axis, across), from_partner


def local(noise, biofilm, source):
    block = pltpu.VMEM((NZ, N, N), F32)
    to_right, to_left = call(
        pack_first,
        hbm(1),
        [shape(Y_ROWS[0], N)] * 2,
        vmem(2),
        [pltpu.VMEM((H, N, N), F32), pltpu.SemaphoreType.DMA((H // 2,))],
        name="pack_first",
    )(in_hbm(noise))
    beside1 = exchange(to_right, to_left, "gy")
    to_right, to_left = call(
        pack_second,
        vmem(2) + hbm(2),
        [shape(Y_ROWS[1], N)] * 2,
        vmem(2),
        [block, pltpu.VMEM((NZ, N, N), jnp.int32), pltpu.SemaphoreType.DMA((2, 8))],
        name="pack_second",
        cost=2e10,
    )(to_left, noise, in_hbm(source), in_hbm(biofilm))
    beside2 = exchange(to_right, to_left, "gy")
    own_middle, own_edge, factor = call(
        column_sums_own,
        vmem(2),
        [shape(NZ, N, N), shape(N, N), shape(NZ, N, N)],
        vmem(3),
        name="columns_own",
        cost=2e10,
    )(noise, biofilm)
    middle1, first_edge, outer, inner = call(
        columns_first,
        vmem(5),
        [shape(H, N, N), shape(N, N)] + [shape(X_ROWS[0], N)] * 2,
        vmem(4),
        name="columns_first",
    )(own_middle, source, biofilm, *beside1)
    above_below1 = exchange_pairs(outer, inner, "gx")
    middle2, edge, edge_source, edge_biofilm, outer, inner = call(
        columns_second,
        vmem(7),
        [shape(G, N, N), shape(N, N), shape(N, N), shape(N, N)] + [shape(X_ROWS[1], N)] * 2,
        vmem(6),
        name="columns_second",
        cost=2e10,
    )(own_middle, own_edge, first_edge, source, biofilm, *beside2)
    above_below2 = exchange_pairs(outer, inner, "gx")
    partial, edge_factor = call(
        row_sums_own,
        vmem(3),
        [shape(G + 1, 144, N), shape(N, N)],
        vmem(2),
        name="rows_own",
        cost=1,
    )(middle2, edge, edge_biofilm)
    first_layers = shape(H, ROWS, N)
    sides = pltpu.VMEM((2, ROWS, N), F32)
    layers = pltpu.VMEM((NZ, ROWS, N), F32)
    second_layers = pltpu.VMEM((G, ROWS, N), F32)
    plane = pltpu.VMEM((ROWS, N), F32)
    first_results = call(
        rows_first,
        vmem(5),
        [shape(8, N)]
        + [first_layers] * 4
        + [shape(H, 144, N), shape(ROWS, N), shape(2, ROWS, N), shape(2, ROWS, N)],
        vmem(9),
        [pltpu.VMEM((H, 144, N), F32), pltpu.VMEM((H, ROWS, N), F32), pltpu.VMEM((H, ROWS, N), F32)],
        name="rows_first",
        cost=2e10,
    )(middle1, factor, source, *above_below1)
    devices = lax.axis_size("gx") * lax.axis_size("gy")
    power1, power2, power3, table = call(
        operate_powers,
        vmem(16),
        [pltpu.HBM((NZ, N, N), F32)] * 3 + [shape(devices, N)],
        hbm(3) + vmem(1),
        [pltpu.VMEM((G + 1, ROWS, N), F32)]
        + [second_layers] * 3
        + [layers, second_layers, layers, layers, block]
        + [pltpu.VMEM((G + 1, 144, N), F32), plane, plane]
        + [sides] * 8
        + [pltpu.SemaphoreType.DMA((3,))],
        name="powers",
    )(*first_results, partial, factor, edge_factor, edge_source, source, *above_below2)
    everyone = lax.all_to_all(table, ("gx", "gy"), 0, 0, tiled=True)
    return tuple(
        call(
            combine,
            vmem(2) + hbm(4),
            [pltpu.HBM((NZ, N, N), F32)] * 2,
            hbm(2),
            [block] * 6 + [pltpu.SemaphoreType.DMA((4, 4)), pltpu.SemaphoreType.DMA((2, 4))],
            name="combine",
        )(everyone, table, *[in_hbm(x) for x in (source, power1, power2, power3)])
    )


def solution(mesh):
    in_specs = (P(None, "gx", "gy"), P(None, "gx", "gy"), P(None, "gx", "gy"))
    out_specs = (P(None, "gx", "gy"), P(None, "gx", "gy"))
    return jax.shard_map(local, mesh=mesh, in_specs=in_specs, out_specs=out_specs, check_vma=False)
```

```python
import jax
import jax.numpy as jnp
from jax import lax
from jax.experimental import pallas as pl
from jax.experimental.pallas import tpu as pltpu
from jax.sharding import PartitionSpec as P

R = 64
WIDTH = 2 * R + 1
NZ = 16
N = 128
F32 = jnp.float32
BF16 = jnp.bfloat16

H = 10
G = NZ - H
Y_ROWS = (H // 2 * N, G // 2 * N + N + 16)
X_TAIL = (H * 72, (G + 1) * 72)
X_ROWS = (X_TAIL[0] + (H + 7) // 8 * 8, X_TAIL[1] + (G + 8) // 8 * 8)
ROWS = 160
OWN = 16
HUGE = 1e30
C3 = 64


def iota(shape, dim):
    return lax.broadcasted_iota(jnp.int32, shape, dim)


def roll(x, shift, axis):
    if isinstance(shift, int):
        shift = shift % x.shape[axis]
        if shift == 0:
            return x
    return pltpu.roll(x, shift, axis)


def split3(x):
    high = x.astype(BF16)
    rest = x - high.astype(F32)
    middle = rest.astype(BF16)
    low = (rest - middle.astype(F32)).astype(BF16)
    return high, middle, low


def split2(x):
    high = x.astype(BF16)
    return high, (x - high.astype(F32)).astype(BF16)


def dot(a, b):
    return lax.dot_general(a, b, (((1,), (0,)), ((), ())), preferred_element_type=F32)


def weights(mask):
    return jnp.where(mask, 1.0, 0.0).astype(BF16)


def pack_first(noise_in, to_right, to_left, noise, arrived):
    low = iota((N, N), 1) < 64
    copies = [
        pltpu.make_async_copy(noise_in.at[2 * q : 2 * q + 2], noise.at[2 * q : 2 * q + 2], arrived.at[q])
        for q in range(H // 2)
    ]
    for copy in copies:
        copy.start()
    for q in range(H // 2):
        copies[q].wait()
        even = noise[2 * q]
        odd = noise[2 * q + 1]
        to_right[q * N : q * N + N, :] = jnp.where(low, roll(even, 64, 1), odd)
        to_left[q * N : q * N + N, :] = jnp.where(low, even, roll(odd, 64, 1))


def pack_second(after, noise, source_in, biofilm_in, to_right, to_left, source, biofilm, arrived):
    def arrivals(g):
        rows = slice(16 * g, 16 * g + 16)
        return [
            pltpu.make_async_copy(far.at[:, rows, :], near.at[:, rows, :], arrived.at[k, g])
            for k, (far, near) in enumerate(((source_in, source), (biofilm_in, biofilm)))
        ]

    del after
    for g in range(8):
        for copy in arrivals(g):
            copy.start()

    lane = iota((16, N), 1)
    slot = lane % 8
    low = lane < 64
    outer = (lane < 32) | (lane >= 96)

    def six(k):
        return ((lane - (8 * k + 5)) & 127) < 6

    third_right = jnp.zeros((16, N), F32)
    third_left = jnp.zeros((16, N), F32)
    for g in range(8):
        for copy in arrivals(g):
            copy.wait()
        rows = slice(16 * g, 16 * g + 16)
        sources = jnp.zeros((16, N), F32)
        noises = jnp.zeros((16, N), F32)
        levels = jnp.zeros((16, N), jnp.int32)
        for z in range(16):
            n = noise[z, rows, :]
            both = roll(jnp.where(outer, source[z, rows, :], n), 8 * z + 8, 1)
            sources = jnp.where(six(z), both, sources)
            noises = jnp.where(six((z + 8) % 16), both, noises)
            levels = jnp.where(six(z), roll(biofilm[z, rows, :], 8 * z + 8, 1), levels)
            if z >= H and z % 2 == 1:
                even = noise[z - 1, rows, :]
                first = (z - 1 - H) // 2 * N + 16 * g
                to_right[first : first + 16, :] = jnp.where(low, roll(even, 64, 1), n)
                to_left[first : first + 16, :] = jnp.where(low, even, roll(n, 64, 1))
        br = levels.astype(F32)
        bl = roll(br, -8, 1)
        first = G // 2 * N + 16 * g
        to_right[first : first + 16, :] = jnp.where(
            slot < 3, roll(noises, -69, 1), jnp.where(slot < 5, roll(br, -3, 1), sources)
        )
        to_left[first : first + 16, :] = jnp.where(
            slot < 3, roll(sources, -8, 1), jnp.where(slot < 5, roll(bl, 3, 1), roll(noises, -67, 1))
        )
        third_right = third_right + roll(jnp.where(slot == 5, br, 0.0), g, 1)
        third_left = third_left + roll(jnp.where(slot == 2, bl, 0.0), g, 1)
    to_right[G // 2 * N + N :, :] = third_right
    to_left[G // 2 * N + N :, :] = third_left


def column_weights():
    m = iota((N, 2 * N), 0)
    o = iota((N, 2 * N), 1)
    s = o - N
    own = ((o < N) & (m - o <= R) & (o - m <= R)) | ((o >= N) & (s <= 2) & (m >= s + 64)) | (
        (s >= 5) & (s <= 7) & (m <= s + 56)
    )
    lane = iota((N, 3 * N), 0)
    o = iota((N, 3 * N), 1)
    half = lane // 64
    m = lane % 64
    e = o - 2 * N
    same = (o < 2 * N) & (o // N == half)
    edge = (e >= 0) & (e < 16) & (e // 8 == half)
    left = (same & (m >= o % N)) | (edge & (o % 8 >= 5))
    right = (same & (m + 64 <= o % N)) | (edge & (o % 8 <= 2))
    a = iota((N, N), 0)
    b = iota((N, N), 1)
    together = a // 8 == b // 8
    t = a % 8
    s = b % 8
    left_extra = together & (t <= 2) & (s >= 5) & (t >= s - 5)
    right_extra = together & (t >= 5) & (s <= 2) & (t - 5 <= s)
    return [weights(w) for w in (own, left, right, left_extra, right_extra)]


def column_sums_own(noise, own_middle, own_edge):
    own = column_weights()[0]
    twice = jnp.concatenate([own, own], axis=0)
    total = jnp.zeros((N, N), F32)
    for z in range(16):
        out = dot(jnp.concatenate(split2(noise[z]), axis=1), twice)
        own_middle[z] = out[:, :N]
        total = total + roll(out[:, N:], 8 * z, 1)
    own_edge[...] = total


def sums_beside(x, y, w):
    high, low = split2(jnp.concatenate([x, y], axis=1))
    return dot(high, w) + dot(low, w)


def on_even():
    return lax.axis_index("gx") % 2 == 0


class Chosen:
    def __init__(self, first, a, b):
        self.first, self.a, self.b = first, a, b

    def __getitem__(self, index):
        return jnp.where(self.first, self.a[index], self.b[index])


def part_columns(first_layer, count, own_middle, from_left, from_right, middle):
    _, left, right, _, _ = column_weights()
    both = jnp.concatenate([left, right], axis=0)
    total = jnp.zeros((N, N), F32)
    for q in range(count // 2):
        rows = slice(q * N, q * N + N)
        halo = sums_beside(from_left[rows, :], from_right[rows, :], both)
        total = total + roll(halo[:, 2 * N :], 8 * first_layer + 16 * q, 1)
        for k in (0, 1):
            z = 2 * q + k
            middle[z] = own_middle[first_layer + z] + halo[:, k * N : k * N + N]
    return total


def fill_messages(sums, sources, levels, tail, outer, inner):
    def fill(to_down, to_up):
        for ref in (to_down, to_up):
            ref[tail:, :] = jnp.zeros((ref.shape[0] - tail, N), F32)
        for z in range(len(sums)):
            to_down[z * 72 : z * 72 + 72, :] = sums[z][56:128, :]
            to_up[z * 72 : z * 72 + 72, :] = sums[z][0:72, :]
        for z, (s, b) in enumerate(zip(sources, levels)):
            to_down[z * 72 : z * 72 + 3, :] = s[125:128, :]
            to_down[z * 72 + 3 : z * 72 + 5, :] = b[126:128, :].astype(F32)
            to_down[tail + z : tail + z + 1, :] = b[125:126, :].astype(F32)
            to_up[z * 72 + 67 : z * 72 + 70, :] = s[0:3, :]
            to_up[z * 72 + 70 : z * 72 + 72, :] = b[0:2, :].astype(F32)
            to_up[tail + z : tail + z + 1, :] = b[2:3, :].astype(F32)

    even = on_even()

    @pl.when(even)
    def _():
        fill(inner, outer)

    @pl.when(jnp.logical_not(even))
    def _():
        fill(outer, inner)


def columns_first(own_middle, source, biofilm, from_left, from_right, middle, edge, outer, inner):
    edge[...] = part_columns(0, H, own_middle, from_left, from_right, middle)
    planes = [[ref.at[z] for z in range(H)] for ref in (middle, source, biofilm)]
    fill_messages(*planes, X_TAIL[0], outer, inner)


def columns_second(
    own_middle, own_edge, first_edge, source, biofilm, from_left, from_right,
    middle, edge, edge_source, edge_biofilm, outer, inner,
):
    _, _, _, left_extra, right_extra = column_weights()
    slot = iota((N, N), 1) % 8
    first = G // 2 * N
    extra_left = from_left[first : first + N, :]
    extra_right = from_right[first : first + N, :]
    total = own_edge[...] + first_edge[...]
    total = total + sums_beside(extra_left, extra_right, jnp.concatenate([left_extra, right_extra], axis=0))
    edge[...] = total + part_columns(H, G, own_middle, from_left, from_right, middle)

    edge_source[...] = jnp.where(slot >= 5, extra_left, jnp.where(slot <= 2, extra_right, 0.0))
    third_left = from_left[first + N :, :]
    third_right = from_right[first + N :, :]
    levels = jnp.where(slot >= 6, roll(extra_left, 3, 1), jnp.where(slot <= 1, roll(extra_right, -3, 1), 0.0))
    slot16 = iota((16, N), 1) % 8
    for g in range(8):
        rows = slice(16 * g, 16 * g + 16)
        edge_biofilm[rows, :] = jnp.where(
            slot16 == 5, roll(third_left, -g, 1), jnp.where(slot16 == 2, roll(third_right, -g, 1), levels[rows, :])
        )

    planes = [[ref.at[H + z] for z in range(G)] for ref in (source, biofilm)]
    fill_messages(
        [middle.at[z] for z in range(G)] + [edge],
        planes[0] + [edge_source],
        planes[1] + [edge_biofilm],
        X_TAIL[1],
        outer,
        inner,
    )


def row_weights():
    r = iota((144, N), 0) - 8
    m = iota((144, N), 1)
    inside = (r >= -3) & (r <= 130)
    own = inside & (m >= r - R) & (m <= r + R)
    halo = inside & (((m < 64) & (m >= r)) | ((m >= 64) & (m <= r)))
    return weights(own), weights(halo)


def row_sums(band, *planes):
    columns = [jnp.concatenate(split2(p), axis=0) for p in planes]
    out = dot(jnp.concatenate([band, band], axis=1), jnp.concatenate(columns, axis=1))
    return [out[:, k * N : k * N + N] for k in range(len(planes))]


def halo_rows(from_up, from_down, z):
    first = pl.multiple_of(z * 72, 8)
    return jnp.concatenate([from_up[pl.ds(first + 8, 64), :], from_down[pl.ds(first, 64), :]], axis=0)


def finish_sums(from_up, from_down, z, sums, out, lanes=None):
    row8 = iota((8, N), 0)
    row144 = iota((144, N), 0)
    first = pl.multiple_of(z * 72, 8)
    above = jnp.where(row8 >= 5, from_up[pl.ds(first, 8), :], 0.0)
    below = jnp.where(row8 <= 2, from_down[pl.ds(first + 64, 8), :], 0.0)
    above = jnp.where(row8 >= 5, above + roll(above, 7, 0) + roll(above, 6, 0), 0.0)
    below = jnp.where(row8 <= 2, below + roll(below, 1, 0) + roll(below, 2, 0), 0.0)
    total = jnp.concatenate([sums[:8] + above, sums[8:136], sums[136:] + below], axis=0) * (1.0 / WIDTH)
    out[...] = total
    real = (row144 >= 5) & (row144 <= 138)
    if lanes is not None:
        real = real & lanes
    return jnp.max(jnp.where(real, total, -HUGE).reshape(18, 8, N), axis=0)


def row_sums_own(middle, edge, biofilm, edge_biofilm, partial, factor, edge_factor):
    own, _ = row_weights()
    for z in range(0, G, 2):
        partial[z], partial[z + 1] = row_sums(own, middle[z], middle[z + 1])
    partial[G] = row_sums(own, edge[...])[0]
    for z in range(NZ):
        factor[z] = resistance_factor(biofilm[z].astype(F32))
    edge_factor[...] = resistance_factor(edge_biofilm[...])


def resistance_factor(biofilm):
    open_part = 1.0 - 0.06 * biofilm
    solid = (1.0 - 0.35 * open_part) * (1.0 / (1.0 - 0.35))
    return (0.5 * solid * solid) / (open_part * open_part * open_part)


def resistance(logperm, factor, top):
    return jnp.minimum(jnp.exp(top - logperm) * factor, HUGE)


def reciprocal(x):
    guess = pl.reciprocal(x, approx=True)
    return guess * (2.0 - x * guess)


MAIN = slice(8, 152)
BEFORE = slice(7, 151)
AFTER = slice(9, 153)
OWN_ROWS = tuple((start, C3) for start in range(16, 144, C3))


def largest_of(tile):
    return jnp.maximum(jnp.max(jnp.max(tile, axis=0, keepdims=True), axis=1, keepdims=True), -60.0)


def halo_tiles(part, z):
    from_up, from_down, tail = part
    row8 = iota((8, N), 0)
    first = pl.multiple_of(z * 72, 8)
    above = from_up[pl.ds(first, 8), :]
    below = from_down[pl.ds(first + 64, 8), :]
    third_above = from_up[pl.ds(tail + z, 1), :]
    third_below = from_down[pl.ds(tail + z, 1), :]
    source_above = jnp.where(row8 >= 5, roll(above, 5, 0), 0.0)
    source_below = jnp.where(row8 <= 2, roll(below, 5, 0), 0.0)
    biofilm_above = jnp.where(row8 == 5, third_above, jnp.where(row8 >= 6, roll(above, 3, 0), 0.0))
    biofilm_below = jnp.where(row8 == 2, third_below, jnp.where(row8 <= 1, roll(below, 2, 0), 0.0))
    return source_above, source_below, biofilm_above, biofilm_below


def prepare(part, z, top, logperm, out, field, own_source, own_factor):
    row8 = iota((8, N), 0)
    source_above, source_below, biofilm_above, biofilm_below = halo_tiles(part, z)
    field[8:16, :] = source_above
    field[16:144, :] = own_source
    field[144:152, :] = source_below
    out[8:16, :] = jnp.where(row8 >= 5, resistance(logperm[0:8, :], resistance_factor(biofilm_above), top), HUGE)
    out[144:152, :] = jnp.where(row8 <= 2, resistance(logperm[136:144, :], resistance_factor(biofilm_below), top), HUGE)
    out[16:144, :] = resistance(logperm[8:136, :], own_factor, top)
    empty = jnp.full((8, N), HUGE, F32)
    none = jnp.zeros((8, N), F32)
    out[0:8, :] = empty
    out[152:160, :] = empty
    field[0:8, :] = none
    field[152:160, :] = none


def block_faces(here_ref, last_ref, across_x, across_y, across_z):
    here = here_ref[MAIN, :]
    across_x[MAIN, :] = reciprocal(here + here_ref[BEFORE, :])
    across_x[152:160, :] = jnp.zeros((8, N), F32)
    across_y[MAIN, :] = jnp.where(iota((144, N), 1) == 0, 0.0, reciprocal(here + roll(here, 1, 1)))
    if last_ref is None:
        across_z[MAIN, :] = jnp.zeros((144, N), F32)
    else:
        across_z[MAIN, :] = reciprocal(here + last_ref[MAIN, :])


def pack_inner(p, layers):
    group = iota((ROWS, N), 1) // 16
    packed = jnp.zeros((ROWS, N), F32)
    for z, ref in layers:
        if z // 8 == p:
            packed = jnp.where(group == z % 8, roll(ref[...], 16 * (z % 8) + 3, 1), packed)
    return packed


def rows_first(
    middle, factor, source, outer, inner,
    largest, field0, across_x, across_y, across_z, image, last_resist, packed_resist, packed_field,
    logperm, resist, flow,
):
    even = on_even()
    from_up, from_down = Chosen(even, outer, inner), Chosen(even, inner, outer)
    part = (from_up, from_down, X_TAIL[0])
    own, halo = row_weights()
    most = jnp.full((8, N), -HUGE, F32)
    for z in range(0, H, 2):
        near = row_sums(own, middle[z], middle[z + 1])
        far = row_sums(halo, *[halo_rows(from_up, from_down, z + i) for i in (0, 1)])
        for i in (0, 1):
            most = jnp.maximum(most, finish_sums(from_up, from_down, z + i, near[i] + far[i], logperm.at[z + i]))
    top = largest_of(most)
    largest[...] = jnp.broadcast_to(top, (8, N))
    for z in range(H):
        prepare(part, z, top, logperm.at[z], resist.at[z], field0.at[z], source[z], factor[z])
    for z in range(H):
        block_faces(
            resist.at[z], resist.at[z - 1] if z else None, across_x.at[z], across_y.at[z], across_z.at[z]
        )
    last_resist[...] = resist[H - 1]
    for packed, ref in ((packed_resist, resist), (packed_field, field0)):
        for p in range(2):
            packed[p] = pack_inner(p, [(z, ref.at[z]) for z in range(H)])
    for z in range(H):
        here = field0[z, MAIN, :]
        flow[z, MAIN, :] = across_y[z, MAIN, :] * (here - roll(here, 1, 1))
    from_last = jnp.zeros((144, N), F32)
    for z in range(H):
        here = field0[z, MAIN, :]
        inward = flow[z, MAIN, :]
        value = inward - roll(inward, -1, 1) + from_last
        value = value + across_x[z, MAIN, :] * (here - field0[z, BEFORE, :])
        value = value - across_x[z, AFTER, :] * (field0[z, AFTER, :] - here)
        if z < H - 1:
            from_last = across_z[z + 1, MAIN, :] * (field0[z + 1, MAIN, :] - here)
            value = value - from_last
        image[z] = value


def operate_powers(
    largest1, field0_1, across_x1, across_y1, across_z1, image1, last_resist, packed_resist, packed_field,
    partial, factor, edge_factor, edge_source, source, outer2, inner2,
    power1, power2, power3, table,
    resist, across_x2, across_y2, across_z2, flow, field0_2, field1, field2, field3,
    logperm2, plane_resist, plane_field,
    side_resist, side_x, side_y, side_z, side0, side1, side2, side_flux, done,
):
    lane = iota((8, N), 1)
    even = on_even()
    from_up2, from_down2 = Chosen(even, outer2, inner2), Chosen(even, inner2, outer2)
    part = (from_up2, from_down2, X_TAIL[1])

    _, halo = row_weights()
    edge_lane = (iota((144, N), 1) % 8 <= 2) | (iota((144, N), 1) % 8 >= 5)
    largest = largest1[...]
    top1 = largest[:1, :1]
    for z in range(0, G, 2):
        pair = row_sums(halo, halo_rows(from_up2, from_down2, z), halo_rows(from_up2, from_down2, z + 1))
        for i in (0, 1):
            sums = partial[z + i] + pair[i]
            largest = jnp.maximum(largest, finish_sums(from_up2, from_down2, z + i, sums, logperm2.at[z + i]))
    sums = partial[G] + row_sums(halo, halo_rows(from_up2, from_down2, G))[0]
    largest = jnp.maximum(largest, finish_sums(from_up2, from_down2, G, sums, logperm2.at[G], edge_lane))
    top = largest_of(largest)
    shrink = jnp.exp(top1 - top)
    grow = jnp.exp(top - top1)

    prepare(part, G, top, logperm2.at[G], plane_resist, plane_field, edge_source[...], edge_factor[...])
    for k in range(G):
        prepare(part, k, top, logperm2.at[k], resist.at[1 + k], field0_2.at[k], source[H + k], factor[H + k])
    resist[0] = jnp.minimum(last_resist[...] * grow, HUGE)
    none = jnp.zeros((8, N), F32)
    for ref in (field1, field2):
        for z in range(NZ):
            ref[z, 0:8, :] = none
            ref[z, 152:160, :] = none
    for ref in (side1, side2, side_x):
        for p in range(2):
            ref[p, 0:8, :] = none
            ref[p, 152:160, :] = none

    a = iota((N, 2 * N), 0)
    o = iota((N, 2 * N), 1)
    t = o % 16
    spread = weights(
        (a // 8 == o // 16)
        & (((t >= 3) & (t <= 5) & (a % 8 == t - 3)) | ((t >= 10) & (t <= 12) & (a % 8 == t - 5)))
    )
    slot160 = iota((ROWS, N), 1) % 16
    second_resist = [(H + k, resist.at[1 + k]) for k in range(G)]
    second_field = [(H + k, field0_2.at[k]) for k in range(G)]
    first_group = iota((ROWS, N), 1) // 16
    for plane, packed, second, side, fill in (
        (plane_resist, packed_resist, second_resist, side_resist, HUGE),
        (plane_field, packed_field, second_field, side0, 0.0),
    ):
        high, mid, low = split3(plane[...])
        beyond = dot(high, spread) + dot(mid, spread) + dot(low, spread)
        for p in range(2):
            inside = packed[p]
            if fill:
                inside = jnp.minimum(inside * grow, HUGE)
            inside = jnp.where(first_group + 8 * p < H, inside, pack_inner(p, second))
            value = jnp.where(
                slot160 <= 2, inside, jnp.where(slot160 >= 13, roll(inside, 10, 1), beyond[:, p * N : p * N + N])
            )
            side[p] = jnp.where((slot160 <= 5) | (slot160 >= 10), value, fill)

    def next_layer(first, second):
        lanes = iota(first.shape, 1)
        return jnp.where(lanes < 112, roll(first, -16, 1), roll(second, -16, 1)), roll(second, -16, 1)

    def last_layer(first, second):
        lanes = iota(first.shape, 1)
        return (
            jnp.where(lanes >= 16, roll(first, 16, 1), 0.0),
            jnp.where(lanes >= 16, roll(second, 16, 1), roll(first, 16, 1)),
        )

    here = [side_resist[p, MAIN, :] for p in range(2)]
    after = next_layer(*here)
    for p in range(2):
        side_x[p, MAIN, :] = reciprocal(here[p] + side_resist[p, BEFORE, :])
        side_y[p, MAIN, :] = reciprocal(here[p] + roll(here[p], 1, 1))
        value = reciprocal(here[p] + after[p])
        side_z[p, MAIN, :] = value if p == 0 else jnp.where(iota((144, N), 1) < 112, value, 0.0)
    for k in range(G):
        block_faces(resist.at[1 + k], resist.at[k], across_x2.at[k], across_y2.at[k], across_z2.at[k])

    def layer_of(first, second, z):
        return first.at[z] if z < H else second.at[z - H]

    field0 = [layer_of(field0_1, field0_2, z) for z in range(NZ)]
    across_x = [layer_of(across_x1, across_x2, z) for z in range(NZ)]
    across_y = [layer_of(across_y1, across_y2, z) for z in range(NZ)]
    across_z = [layer_of(across_z1, across_z2, z) for z in range(NZ)]

    def apply_sides(field, image):
        slot = iota((144, N), 1) % 16
        here = [field[p, MAIN, :] for p in range(2)]
        inward = [side_y[p, MAIN, :] * (here[p] - roll(here[p], 1, 1)) for p in range(2)]
        for p in range(2):
            side_flux[p, MAIN, :] = jnp.where(slot == 13, inward[p], -roll(inward[p], 9, 1))
        if image is None:
            return
        after = next_layer(*here)
        through = [side_z[p, MAIN, :] * (after[p] - here[p]) for p in range(2)]
        back = last_layer(*through)
        for p in range(2):
            value = inward[p] - roll(inward[p], -1, 1) - through[p] + back[p]
            value = value + side_x[p, MAIN, :] * (here[p] - field[p, BEFORE, :])
            value = value - side_x[p, AFTER, :] * (field[p, AFTER, :] - here[p])
            image[p, MAIN, :] = value

    def flow_along_y(field, layers):
        for z in layers:
            here = field[z][MAIN, :]
            flow[z, MAIN, :] = across_y[z][MAIN, :] * (here - roll(here, 1, 1))

    def from_beside(z, rows, size):
        lanes = iota((size, N), 1)
        beside = roll(side_flux[z // 8, rows, :], 115 - 16 * (z % 8), 1)
        return jnp.where((lanes == 0) | (lanes == 127), beside, 0.0)

    def apply_layers(field, layers, start, size):
        rows = slice(start, start + size)
        before = slice(start - 1, start - 1 + size)
        after = slice(start + 1, start + 1 + size)
        first = layers[0]
        here = field[first][rows, :]
        from_last = 0.0 if first == 0 else across_z[first][rows, :] * (here - field[first - 1][rows, :])
        for z in layers:
            inward = flow[z, rows, :]
            value = inward - roll(inward, -1, 1)
            value = value + across_x[z][rows, :] * (here - field[z][before, :])
            value = value - across_x[z][after, :] * (field[z][after, :] - here)
            nearby = from_beside(z, rows, size)
            if z < NZ - 1:
                following = field[z + 1][rows, :]
                to_next = across_z[z + 1][rows, :] * (following - here)
            else:
                following, to_next = here, 0.0
            if z < H - 1:
                value = shrink * (value + from_last - to_next) + nearby
            elif z == H - 1:
                value = shrink * (value + from_last) + nearby - to_next
            else:
                value = value + nearby + from_last - to_next
            yield z, here, value
            here, from_last = following, to_next

    def hand_out(field, power, k):
        return pltpu.make_async_copy(field.at[:, 16:144, :], power, done.at[k])

    def layers_of(ref):
        return [ref.at[z] for z in range(NZ)]

    apply_sides(side0, side1)
    flow_along_y(field0, range(H, NZ))
    for z in range(H):
        value = shrink * image1[z] + from_beside(z, MAIN, 144)
        if z == H - 1:
            value = value - across_z[H][MAIN, :] * (field0[H][MAIN, :] - field0[z][MAIN, :])
        field1[z, MAIN, :] = value
    for z, _, value in apply_layers(field0, range(H, NZ), 8, 144):
        field1[z, MAIN, :] = value
    hand_out(field1, power1, 0).start()
    apply_sides(side1, side2)
    flow_along_y(layers_of(field1), range(NZ))
    for z, _, value in apply_layers(layers_of(field1), range(NZ), 8, 144):
        field2[z, MAIN, :] = value
    hand_out(field2, power2, 1).start()
    apply_sides(side2, None)
    flow_along_y(layers_of(field2), range(NZ))

    sums = tuple(jnp.zeros((8, N), F32) for _ in range(6))
    for group in range(0, NZ, 4):
        for start, size in OWN_ROWS:
            rows = slice(start, start + size)
            for z, f2, f3 in apply_layers(layers_of(field2), range(group, group + 4), start, size):
                field3[z, start - 16 : start - 16 + size, :] = f3
                f0 = field0[z][rows, :]
                f1 = field1[z, rows, :]
                terms = (f0 * f0, f0 * f1, f1 * f1, f1 * f2, f2 * f2, f2 * f3)
                sums = tuple(s + jnp.sum(t.reshape(size // 8, 8, N), axis=0) for s, t in zip(sums, terms))
        part = pl.ds(group, 4)
        pltpu.make_async_copy(field3.at[part], power3.at[part], done.at[2]).start()

    line = jnp.where((lane[:1] >= 8) & (lane[:1] < 16), top, 0.0)
    for k, s in enumerate(sums):
        amount = jnp.sum(jnp.sum(s, axis=0, keepdims=True), axis=1, keepdims=True)
        line = jnp.where(lane[:1] == k, amount, line)
    table[...] = jnp.broadcast_to(line, table.shape)
    hand_out(field1, power1, 0).wait()
    hand_out(field2, power2, 1).wait()
    pltpu.make_async_copy(field3, power3, done.at[2]).wait()


def coefficients(everyone, own):
    n = everyone.shape[0]
    rows = everyone[...]
    lane = iota((n, N), 1)
    tops = jnp.where(lane < 8, roll(rows, -8, 1), 0.0)
    top = jnp.max(tops, axis=0, keepdims=True)
    top = jnp.max(jnp.where(lane[:1] == 0, top, -HUGE), axis=1, keepdims=True)
    factor = jnp.exp((tops - top) * lane.astype(F32))
    moments = jnp.sum(jnp.where(lane < 6, rows * factor, 0.0), axis=0, keepdims=True)
    u0, u1, u2, u3, u4, u5 = [
        jnp.sum(jnp.where(lane[:1] == k, moments, 0.0), axis=1, keepdims=True) for k in range(6)
    ]
    own_top = jnp.sum(jnp.where(lane[:1] == 8, own[0:1, :], 0.0), axis=1, keepdims=True)
    ratio = jnp.exp(own_top - top)

    def over(a, b):
        return jnp.where(b > 0.0, a / jnp.where(b > 0.0, b, 1.0), 0.0)

    l10 = over(u1, u0)
    l20 = over(u2, u0)
    d1 = u2 - l10 * u1
    s12 = u3 - l10 * u2
    l21 = over(s12, d1)
    d2 = (u4 - l20 * u2) - l21 * s12
    y1 = u4 - l10 * u3
    y2 = u5 - l20 * u3 - l21 * y1
    e2 = -over(y2, d2)
    e1 = -over(y1, d1) - l21 * e2
    e0 = -over(u3, u0) - l10 * e1 - l20 * e2

    sigma = jnp.exp(top)
    tau = jnp.minimum(1.0, 2.0 * sigma)
    kappa = jnp.minimum(1.0, 0.5 / sigma)
    at_zero = ((e0 * tau - e1 * kappa) * tau + e2 * kappa * kappa) * tau - kappa * kappa * kappa
    r_scale = tau * tau * tau / at_zero
    p_scale = -jnp.minimum(1.0 / sigma, 2.0) / at_zero
    q1 = tau * e2 - kappa
    r0 = r_scale * e0
    r1 = r_scale * e1 * ratio
    r2 = r_scale * e2 * ratio * ratio
    r3 = r_scale * ratio * ratio * ratio
    p0 = p_scale * (tau * tau * e1 - kappa * q1)
    p1 = p_scale * (tau * q1) * ratio
    p2 = p_scale * (tau * tau) * ratio * ratio
    return p0, p1, p2, r0, r1, r2, r3


def combine(
    everyone, own, source_in, power1_in, power2_in, power3_in, pressure_out, residual_out,
    source, power1, power2, power3, pressure, residual, arrived, left,
):
    def arrivals(g):
        part = slice(4 * g, 4 * g + 4)
        pairs = ((source_in, source), (power1_in, power1), (power2_in, power2), (power3_in, power3))
        return [
            pltpu.make_async_copy(far.at[part], near.at[part], arrived.at[k, g]) for k, (far, near) in enumerate(pairs)
        ]

    def departures(g):
        part = slice(4 * g, 4 * g + 4)
        return [
            pltpu.make_async_copy(near.at[part], far.at[part], left.at[k, g])
            for k, (near, far) in enumerate(((pressure, pressure_out), (residual, residual_out)))
        ]

    for g in range(4):
        for copy in arrivals(g):
            copy.start()
    p0, p1, p2, r0, r1, r2, r3 = coefficients(everyone, own)
    for g in range(4):
        for copy in arrivals(g):
            copy.wait()
        for z in range(4 * g, 4 * g + 4):
            f0 = source[z]
            f1 = power1[z]
            f2 = power2[z]
            pressure[z] = p0 * f0 + p1 * f1 + p2 * f2
            residual[z] = (r0 * f0 + r1 * f1) + (r2 * f2 + r3 * power3[z])
        for copy in departures(g):
            copy.start()
    for g in range(4):
        for copy in departures(g):
            copy.wait()


def vmem(count):
    return [pl.BlockSpec(memory_space=pltpu.VMEM)] * count


def shape(*dims):
    return jax.ShapeDtypeStruct(dims, F32)


def hbm(count):
    return [pl.BlockSpec(memory_space=pltpu.HBM)] * count


def in_hbm(x):
    return pltpu.with_memory_space_constraint(x, pltpu.HBM)


def call(body, inputs, out, out_specs, scratch=(), name=None, cost=1e6):
    return pl.pallas_call(
        body,
        out_shape=out,
        in_specs=inputs,
        out_specs=out_specs,
        scratch_shapes=list(scratch),
        compiler_params=pltpu.CompilerParams(vmem_limit_bytes=40 * 1024 * 1024),
        cost_estimate=pl.CostEstimate(flops=int(cost), bytes_accessed=int(cost), transcendentals=0),
        name=name,
    )


def exchange(to_next, to_previous, axis):
    count = lax.axis_size(axis)
    forward = [(i, (i + 1) % count) for i in range(count)]
    backward = [(target, source) for source, target in forward]
    return lax.ppermute(to_next, axis, forward), lax.ppermute(to_previous, axis, backward)


def exchange_pairs(outer, inner, axis):
    count = lax.axis_size(axis)
    across = [(i, (i + 1 if i % 2 else i - 1) % count) for i in range(count)]
    from_partner = lax.ppermute(inner, axis, [(i, i ^ 1) for i in range(count)])
    return lax.ppermute(outer, axis, across), from_partner


def local(noise, biofilm, source):
    block = pltpu.VMEM((NZ, N, N), F32)
    to_right, to_left = call(
        pack_first,
        hbm(1),
        [shape(Y_ROWS[0], N)] * 2,
        vmem(2),
        [pltpu.VMEM((H, N, N), F32), pltpu.SemaphoreType.DMA((H // 2,))],
        name="pack_first",
    )(in_hbm(noise))
    beside1 = exchange(to_right, to_left, "gy")
    to_right, to_left = call(
        pack_second,
        vmem(2) + hbm(2),
        [shape(Y_ROWS[1], N)] * 2,
        vmem(2),
        [block, pltpu.VMEM((NZ, N, N), jnp.int32), pltpu.SemaphoreType.DMA((2, 8))],
        name="pack_second",
        cost=2e10,
    )(to_left, noise, in_hbm(source), in_hbm(biofilm))
    beside2 = exchange(to_right, to_left, "gy")
    own_middle, own_edge = call(
        column_sums_own,
        vmem(1),
        [shape(NZ, N, N), shape(N, N)],
        vmem(2),
        name="columns_own",
        cost=2e10,
    )(noise)
    middle1, first_edge, outer, inner = call(
        columns_first,
        vmem(5),
        [shape(H, N, N), shape(N, N)] + [shape(X_ROWS[0], N)] * 2,
        vmem(4),
        name="columns_first",
    )(own_middle, source, biofilm, *beside1)
    above_below1 = exchange_pairs(outer, inner, "gx")
    middle2, edge, edge_source, edge_biofilm, outer, inner = call(
        columns_second,
        vmem(7),
        [shape(G, N, N), shape(N, N), shape(N, N), shape(N, N)] + [shape(X_ROWS[1], N)] * 2,
        vmem(6),
        name="columns_second",
        cost=2e10,
    )(own_middle, own_edge, first_edge, source, biofilm, *beside2)
    above_below2 = exchange_pairs(outer, inner, "gx")
    partial, factor, edge_factor = call(
        row_sums_own,
        vmem(4),
        [shape(G + 1, 144, N), shape(NZ, N, N), shape(N, N)],
        vmem(3),
        name="rows_own",
        cost=1,
    )(middle2, edge, biofilm, edge_biofilm)
    first_layers = shape(H, ROWS, N)
    sides = pltpu.VMEM((2, ROWS, N), F32)
    layers = pltpu.VMEM((NZ, ROWS, N), F32)
    second_layers = pltpu.VMEM((G, ROWS, N), F32)
    plane = pltpu.VMEM((ROWS, N), F32)
    first_results = call(
        rows_first,
        vmem(5),
        [shape(8, N)]
        + [first_layers] * 4
        + [shape(H, 144, N), shape(ROWS, N), shape(2, ROWS, N), shape(2, ROWS, N)],
        vmem(9),
        [pltpu.VMEM((H, 144, N), F32), pltpu.VMEM((H, ROWS, N), F32), pltpu.VMEM((H, ROWS, N), F32)],
        name="rows_first",
        cost=2e10,
    )(middle1, factor, source, *above_below1)
    devices = lax.axis_size("gx") * lax.axis_size("gy")
    power1, power2, power3, table = call(
        operate_powers,
        vmem(16),
        [pltpu.HBM((NZ, N, N), F32)] * 3 + [shape(devices, N)],
        hbm(3) + vmem(1),
        [pltpu.VMEM((G + 1, ROWS, N), F32)]
        + [second_layers] * 3
        + [layers, second_layers, layers, layers, block]
        + [pltpu.VMEM((G + 1, 144, N), F32), plane, plane]
        + [sides] * 8
        + [pltpu.SemaphoreType.DMA((3,))],
        name="powers",
    )(*first_results, partial, factor, edge_factor, edge_source, source, *above_below2)
    everyone = lax.all_to_all(table, ("gx", "gy"), 0, 0, tiled=True)
    return tuple(
        call(
            combine,
            vmem(2) + hbm(4),
            [pltpu.HBM((NZ, N, N), F32)] * 2,
            hbm(2),
            [block] * 6 + [pltpu.SemaphoreType.DMA((4, 4)), pltpu.SemaphoreType.DMA((2, 4))],
            name="combine",
        )(everyone, table, *[in_hbm(x) for x in (source, power1, power2, power3)])
    )


def solution(mesh):
    in_specs = (P(None, "gx", "gy"), P(None, "gx", "gy"), P(None, "gx", "gy"))
    out_specs = (P(None, "gx", "gy"), P(None, "gx", "gy"))
    return jax.shard_map(local, mesh=mesh, in_specs=in_specs, out_specs=out_specs, check_vma=False)
```
